32 devices in a mesh: space: 8 (over y, x, core), inst: 4 (over z).
Axes of the slice: x: 2, y: 2, z: 4, core: 2. Of those that a mesh axis runs over, the one named last changes fastest.
Arguments:
- state: float32 [4, 4, 16, 2048], P('inst', None, None, 'space'), may hold values from -1.3 to 5, as said below
- face_cell: int32 [6144], P('space'), may hold values from 0 to 4095
- face_node: int32 [6144], P('space'), may hold values from 0 to 4095
- face_area: float32 [3, 6144], P(None, 'space'), may hold values from -6 to 6
Outputs:
- increment: float32 [4, 4, 16, 2048], P('inst', None, None, 'space')
- blade_forces: float32 [4, 3, 4096], P('inst', None, 'space')
The draws below stay inside these ranges and needn't reach their ends.
Inputs may be any that keep to these rules, and one draw needn't show every extreme that they name: state: density within 0.7 to 1.4, each velocity component within -0.9 to 0.9, pressure within 0.5 to 1.5. `face_node`: a shell node index.
All inputs are finite; a program needn't handle non-finite values.
Results may differ from the reference program's by a relative error of at most 0.0002.
Values sent between devices are 32-bit elements; how exact they have to be, the bound alone decides.
No kernel may reach another device: no remote copies, remote signals or barrier semaphores. Data moves between devices by JAX's collectives and lax.ppermute only.
A program may use at most 128 MiB of HBM per device.

```python
import math
import jax
import jax.numpy as jnp
import numpy as np
from jax import lax

NR = 16
CC = 256
FACES_DEV = 768
INST = 4
NC = 2048
NODES = 4096
FACES = 6144


def draw_state(key, part):
    subkeys = jax.random.split(jax.random.fold_in(key, 17), 4)
    shape = (INST, NR, NC)
    density = jax.random.uniform(subkeys[0], shape, jnp.float32, 0.7, 1.4)
    radial_velocity = jax.random.uniform(subkeys[1], shape, jnp.float32, -0.9, 0.9)
    around_velocity = jax.random.uniform(subkeys[2], shape, jnp.float32, -0.9, 0.9)
    pressure = jax.random.uniform(subkeys[3], shape, jnp.float32, 0.5, 1.5)
    energy = pressure / 0.4 + 0.5 * density * (radial_velocity * radial_velocity + around_velocity * around_velocity)
    return jnp.stack([density, density * radial_velocity, density * around_velocity, energy], axis=1)


def set_ends(values, own_key, smallest, largest):
    dims = values.shape
    spot = [jax.random.randint(jax.random.fold_in(own_key, axis), (), 0, dims[axis]) for axis in range(len(dims))]
    values = values.at[tuple(spot)].set(smallest)
    longest = dims.index(max(dims))
    spot[longest] = (spot[longest] + 1) % dims[longest]
    return values.at[tuple(spot)].set(largest)


def block_scale(own_key, shape, cuts, low, top_value):
    gain, own = 1.0, jax.random.fold_in(own_key, 6)
    for dim, shards_of in cuts:
        steps = jnp.exp(jax.random.uniform(jax.random.fold_in(own, dim), (shards_of,), jnp.float32, low / len(cuts), top_value / len(cuts)))
        gain = gain * jnp.repeat(steps, shape[dim] // shards_of).reshape([-1 if axis == dim else 1 for axis in range(len(shape))])
    return gain


def bell_draw(key, dims, deviation, limit, cuts=(), held_as=jnp.bfloat16):
    loudness = block_scale(key, dims, cuts, -0.22, 0.18) if cuts else 1.0
    array = jax.random.normal(key, dims, jnp.float32) * deviation * loudness
    return jnp.minimum(jnp.maximum(array, -limit), limit).astype(held_as)


def setup_inputs(seed: int = 0) -> dict:
    key_of = jax.random.split(jax.random.key(seed), 5)
    return {
        "state": draw_state(jax.random.fold_in(key_of[4], 71), 0),
        "face_cell": set_ends(jax.random.randint(key_of[1], (FACES,), 0, NR * CC), jax.random.fold_in(key_of[1], 1), 0, (NR * CC) - 1).astype(jnp.int32),
        "face_node": set_ends(jax.random.randint(key_of[2], (FACES,), 0, NODES), jax.random.fold_in(key_of[2], 1), 0, NODES - 1).astype(jnp.int32),
        "face_area": bell_draw(key_of[3], (3, FACES), 1.0, 6.0, ((1, 8),), jnp.float32),
    }


gamma_ratio = 1.4
omega_rate = 0.5
cfl_number = 0.8

def spectral_table(count):
    values = np.zeros((count, count), np.float32)
    for row_index in range(count):
        for col_index in range(count):
            offset = row_index - col_index
            values[row_index, col_index] = (-1.0) ** offset / count
            if offset != 0:
                values[row_index, col_index] += 0.5 * (-1.0) ** offset / math.tan(math.pi * offset / count)
    return values

def primitives(extended):
    density = extended[..., 0, :, :]
    radial_velocity = extended[..., 1, :, :] / density
    around_velocity = extended[..., 2, :, :] / density
    pressure = (gamma_ratio - 1.0) * (extended[..., 3, :, :] - 0.5 * density * (radial_velocity * radial_velocity + around_velocity * around_velocity))
    sound_speed = jnp.sqrt(gamma_ratio * pressure / density)
    return (radial_velocity, around_velocity, pressure, sound_speed)

def around_faces(cells, around_velocity, pressure, sound_speed):
    face_flux = jnp.stack([cells[..., 2, :, :], cells[..., 1, :, :] * around_velocity, cells[..., 2, :, :] * around_velocity + pressure, (cells[..., 3, :, :] + pressure) * around_velocity], axis=-3)
    speed = jnp.abs(around_velocity) + sound_speed
    dissipation = jnp.expand_dims(jnp.maximum(speed[..., :-1], speed[..., 1:]), -3)
    return 0.5 * (face_flux[..., :-1] + face_flux[..., 1:]) - 0.5 * dissipation * (cells[..., 1:] - cells[..., :-1])

def radial_faces(cells, radial_velocity, pressure, sound_speed):
    face_flux = jnp.stack([cells[..., 1, :, :], cells[..., 1, :, :] * radial_velocity + pressure, cells[..., 2, :, :] * radial_velocity, (cells[..., 3, :, :] + pressure) * radial_velocity], axis=-3)
    speed = jnp.abs(radial_velocity) + sound_speed
    dissipation = jnp.expand_dims(jnp.maximum(speed[..., :-1, :], speed[..., 1:, :]), -3)
    interior = 0.5 * (face_flux[..., :-1, :] + face_flux[..., 1:, :]) - 0.5 * dissipation * (cells[..., 1:, :] - cells[..., :-1, :])
    lower_wall = pressure[..., :1, :]
    upper_wall = pressure[..., -1:, :]
    nothing = jnp.zeros_like(lower_wall)
    lower = jnp.stack([nothing, lower_wall, nothing, nothing], axis=-3)
    upper = jnp.stack([nothing, upper_wall, nothing, nothing], axis=-3)
    return jnp.concatenate([lower, interior, upper], axis=-2)

def spatial_residual(extended):
    radial_velocity, around_velocity, pressure, sound_speed = primitives(extended)
    beside_all = around_faces(extended, around_velocity, pressure, sound_speed)
    div_around = beside_all[..., 1:] - beside_all[..., :-1]
    cells = extended[..., 1:-1]
    radial_velocity = radial_velocity[..., 1:-1]
    around_velocity = around_velocity[..., 1:-1]
    pressure = pressure[..., 1:-1]
    sound_speed = sound_speed[..., 1:-1]
    radial = radial_faces(cells, radial_velocity, pressure, sound_speed)
    div_radial = radial[..., 1:, :] - radial[..., :-1, :]
    return (div_around + div_radial, radial_velocity, around_velocity, pressure, sound_speed)

def one_instance(single):
    extended = jnp.concatenate([single[..., -1:], single, single[..., :1]], axis=-1)
    divergence, radial_velocity, around_velocity, pressure, sound_speed = spatial_residual(extended)
    step = cfl_number / (jnp.abs(radial_velocity) + jnp.abs(around_velocity) + 2.0 * sound_speed + omega_rate * INST / 2.0)
    return (divergence, step, pressure)

def reference(state, face_cell, face_node, face_area):
    divergence, step, pressure = lax.map(one_instance, state)
    spectral = jnp.asarray(spectral_table(INST), jnp.float32)
    time_term = omega_rate * jnp.einsum('nm,mcrx->ncrx', spectral, state, precision=lax.Precision.HIGHEST)
    residual = divergence + time_term
    increment = -step[:, None] * residual
    block = jnp.arange(FACES, dtype=jnp.int32) // FACES_DEV
    radial_index = face_cell // CC
    around_index = block * CC + face_cell % CC
    face_pressure = pressure[:, radial_index, around_index]
    contribution = face_pressure[:, None, :] * face_area[None]
    blade_forces = jnp.zeros((INST, 3, NODES), jnp.float32).at[:, :, face_node].add(contribution)
    return (increment, blade_forces)
```

```python
import functools
import math

import jax
import jax.numpy as jnp
import numpy as np
from jax import lax
from jax.experimental import pallas as pl
from jax.experimental.pallas import tpu as pltpu
from jax.sharding import PartitionSpec as P

gamma_ratio = 1.4
omega_rate = 0.5
cfl_number = 0.8

LANES = 128
ROWS = 16
DIRECT = 16


def spectral_row(count):
    row = np.zeros((count,), np.float32)
    for shift in range(count):
        row[shift] = (-1.0) ** shift / count
        if shift != 0:
            row[shift] += 0.5 * (-1.0) ** shift / math.tan(math.pi * shift / count)
    return [float(omega_rate * value) for value in row]


def pressure_of(q0, q1, q2, q3):
    inverse = 1.0 / q0
    vr = q1 * inverse
    vc = q2 * inverse
    p = (gamma_ratio - 1.0) * (q3 - 0.5 * q0 * (vr * vr + vc * vc))
    return inverse, vr, vc, p


def forces_kernel(blocks, relative, node_block, state, cell, node, area, *outs):
    radial, around = state.shape[2:]
    faces = cell.shape[0] * LANES
    chunks = faces // LANES
    _, _, _, p = pressure_of(state[0, 0], state[0, 1], state[0, 2], state[0, 3])
    sublane = lax.broadcasted_iota(jnp.int32, (8, LANES), 0)
    picked = []
    for c in range(chunks):
        index = jnp.broadcast_to(cell[c : c + 1, :], (8, LANES))
        row = index // around
        column = index % around
        lane = column % LANES
        half = column // LANES
        total = jnp.zeros((8, LANES), jnp.float32)
        for r in range(radial // 8):
            for h in range(around // LANES):
                part = p[r * 8 : (r + 1) * 8, h * LANES : (h + 1) * LANES]
                value = jnp.take_along_axis(part, lane, axis=1, mode="promise_in_bounds")
                total += jnp.where((row == sublane + r * 8) & (half == h), value, 0.0)
        picked.append(jnp.sum(total, axis=0, keepdims=True))
    face_pressure = jnp.concatenate(picked, axis=1)
    contribution = face_pressure * area[...]
    nodes = jnp.concatenate([node[c : c + 1, :] for c in range(chunks)], axis=1)

    high = node_block // LANES
    owner = nodes // node_block
    if relative:
        owner = (owner - lax.axis_index("space") + blocks) % blocks
    place = owner * high + (nodes % node_block) // LANES
    low = nodes % LANES
    pick_low = (
        lax.broadcasted_iota(jnp.int32, (LANES, faces), 0) == jnp.broadcast_to(low, (LANES, faces))
    ).astype(jnp.float32).astype(jnp.bfloat16)
    pattern = jnp.concatenate(
        [jnp.broadcast_to(contribution[k : k + 1], (high, faces)) for k in range(3)]
        + [jnp.zeros((ROWS - 3 * high, faces), jnp.float32)],
        axis=0,
    )
    first = pattern.astype(jnp.bfloat16).astype(jnp.float32)
    second = pattern - first
    place = jnp.broadcast_to(place, (ROWS, faces))
    row_high = lax.broadcasted_iota(jnp.int32, (ROWS, faces), 0) % high

    def dense(start, count):
        masks = [place == row_high + (start + b) * high for b in range(count)]
        result = None
        for part in (first, second):
            left = jnp.concatenate([jnp.where(m, part, 0.0) for m in masks], axis=0)
            product = lax.dot_general(
                left.astype(jnp.bfloat16),
                pick_low,
                (((1,), (1,)), ((), ())),
                preferred_element_type=jnp.float32,
            )
            result = product if result is None else result + product
        return result

    if relative:
        result = dense(0, blocks)
        for b in range(blocks):
            block = result[b * ROWS : (b + 1) * ROWS]
            outs[b][0:ROWS, :] = block
        edge = state[0].reshape(4 * radial, around)
        outs[1][ROWS:, :] = edge[:, around - LANES :]
        outs[blocks - 1][ROWS:, :] = edge[:, :LANES]
    else:
        group = 8

        @pl.loop(0, blocks // group)
        def _(g):
            result = dense(g * group, group)
            outs[0][pl.ds(g * group, group)] = result.reshape(group, ROWS, LANES)


def update_kernel(weights, instances, relative, state, before, after, *refs):
    others = refs[: instances - 1]
    forces = refs[instances - 1 : -2]
    increment, blade = refs[-2:]
    radial, around = state.shape[2:]
    base = ROWS if relative else 0
    lane = lax.broadcasted_iota(jnp.int32, (radial, LANES), 1)
    q = []
    for c in range(4):
        rows = pl.ds(base + c * radial, radial)
        edge = jnp.where(lane == LANES - 1, before[rows, :], after[rows, :])
        q.append(jnp.concatenate([state[0, c], edge], axis=1))
    inverse, vr, vc, p = pressure_of(*q)
    a = jnp.sqrt(gamma_ratio * p * inverse)
    width = around + LANES
    step = cfl_number / (
        jnp.abs(vr) + jnp.abs(vc) + 2.0 * a + omega_rate * instances / 2.0
    )

    def next_lane(x):
        return pltpu.roll(x, width - 1, 1)

    def last_lane(x):
        return pltpu.roll(x, 1, 1)

    speed = jnp.abs(vc) + a
    reach = 0.5 * jnp.maximum(speed, next_lane(speed))
    flux = (q[2], q[1] * vc, q[2] * vc + p, (q[3] + p) * vc)
    divergence = []
    for c in range(4):
        face = 0.5 * (flux[c] + next_lane(flux[c])) - reach * (next_lane(q[c]) - q[c])
        divergence.append((face - last_lane(face))[:, :around])

    own = slice(0, around)
    q = [x[:, own] for x in q]
    vr, p, a, step = vr[:, own], p[:, own], a[:, own], step[:, own]

    def above(x):
        return pltpu.roll(x, radial - 1, 0)

    def below(x):
        return pltpu.roll(x, 1, 0)

    row = lax.broadcasted_iota(jnp.int32, (radial, around), 0)
    hub, tip = row == 0, row == radial - 1
    speed = jnp.abs(vr) + a
    reach = 0.5 * jnp.maximum(speed, above(speed))
    flux = (q[1], q[1] * vr + p, q[2] * vr, (q[3] + p) * vr)
    for c in range(4):
        wall = p if c == 1 else 0.0
        face = 0.5 * (flux[c] + above(flux[c])) - reach * (above(q[c]) - q[c])
        upper = jnp.where(tip, wall, face)
        lower = jnp.where(hub, wall, below(face))
        residual = divergence[c] + (upper - lower) + weights[0] * q[c]
        for shift, other in enumerate(others, 1):
            residual += weights[shift] * other[0, c]
        increment[0, c] = -step * residual

    total = None
    for ref in forces:
        if relative:
            part = ref[0:ROWS, :]
        else:
            part = jnp.sum(ref[...], axis=0)
        total = part if total is None else total + part
    high = blade.shape[2] // LANES
    for k in range(3):
        for h in range(high):
            blade[k, :, pl.ds(h * LANES, LANES)] = total[k * high + h : k * high + h + 1, :]


def per_device(node_block, state, face_cell, face_node, face_area):
    blocks = lax.axis_size("space")
    instances = lax.axis_size("inst")
    radial, around = state.shape[2:]
    relative = 3 <= blocks <= DIRECT
    chunks = face_cell.shape[0] // LANES
    vmem = pl.BlockSpec(memory_space=pltpu.VMEM)
    params = pltpu.CompilerParams(vmem_limit_bytes=(4 if relative else 32) * 2**20)

    others = [
        lax.ppermute(state, "inst", [(i, (i + s) % instances) for i in range(instances)])
        for s in range(1, instances)
    ]

    rows = 4 * radial
    if relative:
        shapes = [
            jax.ShapeDtypeStruct((ROWS + (rows if b in (1, blocks - 1) else 0), LANES), jnp.float32)
            for b in range(blocks)
        ]
    else:
        shapes = [jax.ShapeDtypeStruct((blocks, ROWS, LANES), jnp.float32)]
    parts = pl.pallas_call(
        functools.partial(forces_kernel, blocks, relative, node_block),
        out_shape=shapes,
        in_specs=[vmem] * 4,
        out_specs=[vmem] * len(shapes),
        compiler_params=params,
        name="face_forces",
    )(
        state,
        face_cell.reshape(chunks, LANES),
        face_node.reshape(chunks, LANES),
        face_area,
    )

    def shifted(value, s):
        return lax.ppermute(value, "space", [(i, (i + s) % blocks) for i in range(blocks)])

    if relative:
        forces = [parts[0]] + [shifted(parts[s], s) for s in range(1, blocks)]
        before, after = forces[1], forces[blocks - 1]
    else:
        forces = [lax.all_to_all(parts[0], "space", 0, 0, tiled=True)]
        flat = state.reshape(rows, around)
        before = shifted(flat[:, around - LANES :], 1)
        after = shifted(flat[:, :LANES], blocks - 1)

    increment, blade = pl.pallas_call(
        functools.partial(update_kernel, spectral_row(instances), instances, relative),
        out_shape=[
            jax.ShapeDtypeStruct(state.shape, jnp.float32),
            jax.ShapeDtypeStruct((3, 1, node_block), jnp.float32),
        ],
        in_specs=[vmem] * (3 + len(others) + len(forces)),
        out_specs=[vmem] * 2,
        compiler_params=params,
        name="update",
    )(state, before, after, *others, *forces)
    return increment, jnp.transpose(blade, (1, 0, 2))


def solution(mesh):
    in_specs = (P("inst", None, None, "space"), P("space"), P("space"), P(None, "space"))
    out_specs = (P("inst", None, None, "space"), P("inst", None, "space"))
    return jax.shard_map(
        functools.partial(per_device, 512),
        mesh=mesh,
        in_specs=in_specs,
        out_specs=out_specs,
        check_vma=False,
    )
```

```python
import functools
import math

import jax
import jax.numpy as jnp
import numpy as np
from jax import lax
from jax.experimental import pallas as pl
from jax.experimental.pallas import tpu as pltpu
from jax.sharding import PartitionSpec as P

gamma_ratio = 1.4
omega_rate = 0.5
cfl_number = 0.8

LANES = 128
ROWS = 16


def spectral_row(count):
    row = np.zeros((count,), np.float32)
    for shift in range(count):
        row[shift] = (-1.0) ** shift / count
        if shift != 0:
            row[shift] += 0.5 * (-1.0) ** shift / math.tan(math.pi * shift / count)
    return [float(omega_rate * value) for value in row]


def pressure_of(q0, q1, q2, q3):
    inverse = 1.0 / q0
    vr = q1 * inverse
    vc = q2 * inverse
    p = (gamma_ratio - 1.0) * (q3 - 0.5 * q0 * (vr * vr + vc * vc))
    return inverse, vr, vc, p


def forces_kernel(blocks, node_block, state_hbm, cell_hbm, node_hbm, area_hbm, out, state, cell, node, area, sems):
    loads = [
        pltpu.make_async_copy(source, target, sems.at[i])
        for i, (source, target) in enumerate(
            ((state_hbm, state), (cell_hbm, cell), (node_hbm, node), (area_hbm, area))
        )
    ]
    for load in loads:
        load.start()
    for load in loads:
        load.wait()
    radial, around = state.shape[2:]
    faces = cell.shape[0] * LANES
    chunks = faces // LANES
    _, _, _, p = pressure_of(state[0, 0], state[0, 1], state[0, 2], state[0, 3])
    sublane = lax.broadcasted_iota(jnp.int32, (8, LANES), 0)
    picked = []
    for c in range(chunks):
        index = jnp.broadcast_to(cell[c : c + 1, :], (8, LANES))
        row = index // around
        column = index % around
        lane = column % LANES
        half = column // LANES
        total = jnp.zeros((8, LANES), jnp.float32)
        for r in range(radial // 8):
            for h in range(around // LANES):
                part = p[r * 8 : (r + 1) * 8, h * LANES : (h + 1) * LANES]
                value = jnp.take_along_axis(part, lane, axis=1, mode="promise_in_bounds")
                total += jnp.where((row == sublane + r * 8) & (half == h), value, 0.0)
        picked.append(jnp.sum(total, axis=0, keepdims=True))
    face_pressure = jnp.concatenate(picked, axis=1)
    contribution = face_pressure * area[...]
    nodes = jnp.concatenate([node[c : c + 1, :] for c in range(chunks)], axis=1)

    high = node_block // LANES
    place = nodes // LANES
    low = nodes % LANES
    pick_low = (
        lax.broadcasted_iota(jnp.int32, (LANES, faces), 0) == jnp.broadcast_to(low, (LANES, faces))
    ).astype(jnp.float32).astype(jnp.bfloat16)
    pattern = jnp.concatenate(
        [jnp.broadcast_to(contribution[k : k + 1], (high, faces)) for k in range(3)]
        + [jnp.zeros((ROWS - 3 * high, faces), jnp.float32)],
        axis=0,
    )
    first = pattern.astype(jnp.bfloat16).astype(jnp.float32)
    second = pattern - first
    place = jnp.broadcast_to(place, (ROWS, faces))
    row_high = lax.broadcasted_iota(jnp.int32, (ROWS, faces), 0) % high

    def dense(start, count):
        masks = [place == row_high + (start + b) * high for b in range(count)]
        result = None
        for part in (first, second):
            left = jnp.concatenate([jnp.where(m, part, 0.0) for m in masks], axis=0)
            product = lax.dot_general(
                left.astype(jnp.bfloat16),
                pick_low,
                (((1,), (1,)), ((), ())),
                preferred_element_type=jnp.float32,
            )
            result = product if result is None else result + product
        return result.reshape(count, ROWS, LANES)

    group = math.gcd(blocks, 8)
    if group == blocks:
        out[:, 0:ROWS, :] = dense(0, blocks)
    else:

        @pl.loop(0, blocks // group)
        def _(g):
            out[pl.ds(g * group, group), 0:ROWS, :] = dense(g * group, group)

    lane = lax.broadcasted_iota(jnp.int32, (radial, LANES), 1)
    edge = jnp.zeros((radial, LANES), jnp.float32)
    for c in range(4):
        last = pltpu.roll(state[0, c, :, around - LANES :], (c + 1) % LANES, 1)
        initial = pltpu.roll(state[0, c, :, :LANES], 4 + c, 1)
        edge = jnp.where(lane == c, last, jnp.where(lane == 4 + c, initial, edge))
    out[:, ROWS:, :] = jnp.broadcast_to(edge[None], (blocks, radial, LANES))


def update_kernel(weights, blocks, instances, state, parts, *refs):
    others = refs[: instances - 1]
    increment, blade = refs[-2:]
    radial, around = state.shape[2:]
    me = lax.axis_index("space")
    before = parts[(me + blocks - 1) % blocks, ROWS:, :]
    after = parts[(me + 1) % blocks, ROWS:, :]
    lane = lax.broadcasted_iota(jnp.int32, (radial, LANES), 1)
    q = []
    for c in range(4):
        last = pltpu.roll(before, LANES - 1 - c, 1)
        initial = pltpu.roll(after, LANES - 4 - c, 1)
        edge = jnp.where(lane == LANES - 1, last, initial)
        edge = jnp.where((lane == LANES - 1) | (lane == 0), edge, state[0, c, :, :LANES])
        q.append(jnp.concatenate([state[0, c], edge], axis=1))
    inverse, vr, vc, p = pressure_of(*q)
    a = jnp.sqrt(gamma_ratio * p * inverse)
    width = around + LANES
    step = cfl_number / (
        jnp.abs(vr) + jnp.abs(vc) + 2.0 * a + omega_rate * instances / 2.0
    )

    def next_lane(x):
        return pltpu.roll(x, width - 1, 1)

    def last_lane(x):
        return pltpu.roll(x, 1, 1)

    speed = jnp.abs(vc) + a
    reach = 0.5 * jnp.maximum(speed, next_lane(speed))
    flux = (q[2], q[1] * vc, q[2] * vc + p, (q[3] + p) * vc)
    divergence = []
    for c in range(4):
        face = 0.5 * (flux[c] + next_lane(flux[c])) - reach * (next_lane(q[c]) - q[c])
        divergence.append((face - last_lane(face))[:, :around])

    own = slice(0, around)
    q = [x[:, own] for x in q]
    vr, p, a, step = vr[:, own], p[:, own], a[:, own], step[:, own]

    def above(x):
        return pltpu.roll(x, radial - 1, 0)

    def below(x):
        return pltpu.roll(x, 1, 0)

    row = lax.broadcasted_iota(jnp.int32, (radial, around), 0)
    hub, tip = row == 0, row == radial - 1
    speed = jnp.abs(vr) + a
    reach = 0.5 * jnp.maximum(speed, above(speed))
    flux = (q[1], q[1] * vr + p, q[2] * vr, (q[3] + p) * vr)
    for c in range(4):
        wall = p if c == 1 else 0.0
        face = 0.5 * (flux[c] + above(flux[c])) - reach * (above(q[c]) - q[c])
        upper = jnp.where(tip, wall, face)
        lower = jnp.where(hub, wall, below(face))
        residual = divergence[c] + (upper - lower) + weights[0] * q[c]
        for shift, other in enumerate(others, 1):
            residual += weights[shift] * other[0, c]
        increment[0, c] = -step * residual

    total = jnp.sum(parts[:, 0:ROWS, :], axis=0)
    high = blade.shape[2] // LANES
    for k in range(3):
        for h in range(high):
            blade[k, :, pl.ds(h * LANES, LANES)] = total[k * high + h : k * high + h + 1, :]


def per_device(node_block, state, face_cell, face_node, face_area):
    blocks = lax.axis_size("space")
    instances = lax.axis_size("inst")
    radial, around = state.shape[2:]
    chunks = face_cell.shape[0] // LANES
    vmem = pl.BlockSpec(memory_space=pltpu.VMEM)
    params = pltpu.CompilerParams(vmem_limit_bytes=(4 if blocks <= 16 else 16) * 2**20)

    others = [
        lax.ppermute(state, "inst", [(i, (i + s) % instances) for i in range(instances)])
        for s in range(1, instances)
    ]

    faces = (
        state,
        face_cell.reshape(chunks, LANES),
        face_node.reshape(chunks, LANES),
        face_area,
    )
    parts, near_state = pl.pallas_call(
        functools.partial(forces_kernel, blocks, node_block),
        out_shape=[
            jax.ShapeDtypeStruct((blocks, ROWS + radial, LANES), jnp.float32),
            jax.ShapeDtypeStruct(state.shape, jnp.float32),
        ],
        in_specs=[pl.BlockSpec(memory_space=pltpu.HBM)] * 4,
        out_specs=[vmem] * 2,
        scratch_shapes=[pltpu.VMEM(x.shape, x.dtype) for x in faces[1:]]
        + [pltpu.SemaphoreType.DMA((4,))],
        compiler_params=params,
        cost_estimate=pl.CostEstimate(flops=10**9, bytes_accessed=10**7, transcendentals=0),
        name="face_forces",
    )(*(pltpu.with_memory_space_constraint(x, pltpu.HBM) for x in faces))
    parts = lax.all_to_all(parts, "space", 0, 0, tiled=True)

    increment, blade = pl.pallas_call(
        functools.partial(update_kernel, spectral_row(instances), blocks, instances),
        out_shape=[
            jax.ShapeDtypeStruct(state.shape, jnp.float32),
            jax.ShapeDtypeStruct((3, 1, node_block), jnp.float32),
        ],
        in_specs=[vmem] * (2 + len(others)),
        out_specs=[vmem] * 2,
        compiler_params=params,
        name="update",
    )(near_state, parts, *others)
    return increment, jnp.transpose(blade, (1, 0, 2))


def solution(mesh):
    in_specs = (P("inst", None, None, "space"), P("space"), P("space"), P(None, "space"))
    out_specs = (P("inst", None, None, "space"), P("inst", None, "space"))
    return jax.shard_map(
        functools.partial(per_device, 512),
        mesh=mesh,
        in_specs=in_specs,
        out_specs=out_specs,
        check_vma=False,
    )
```

```python
import functools
import math

import jax
import jax.numpy as jnp
import numpy as np
from jax import lax
from jax.experimental import pallas as pl
from jax.experimental.pallas import tpu as pltpu
from jax.sharding import PartitionSpec as P

gamma_ratio = 1.4
omega_rate = 0.5
cfl_number = 0.8

LANES = 128
ROWS = 16


def spectral_row(count):
    row = np.zeros((count,), np.float32)
    for shift in range(count):
        row[shift] = (-1.0) ** shift / count
        if shift != 0:
            row[shift] += 0.5 * (-1.0) ** shift / math.tan(math.pi * shift / count)
    return [float(omega_rate * value) for value in row]


def pressure_of(q0, q1, q2, q3):
    inverse = 1.0 / q0
    vr = q1 * inverse
    vc = q2 * inverse
    p = (gamma_ratio - 1.0) * (q3 - 0.5 * q0 * (vr * vr + vc * vc))
    return inverse, vr, vc, p


def forces_kernel(blocks, node_block, state_hbm, cell_hbm, node_hbm, area_hbm, out, state, cell, node, area, sems):
    loads = [
        pltpu.make_async_copy(source, target, sems.at[i])
        for i, (source, target) in enumerate(
            ((state_hbm, state), (cell_hbm, cell), (node_hbm, node), (area_hbm, area))
        )
    ]
    for load in loads:
        load.start()
    for load in loads:
        load.wait()
    radial, around = state.shape[2:]
    faces = cell.shape[0] * LANES
    chunks = faces // LANES
    _, _, _, p = pressure_of(state[0, 0], state[0, 1], state[0, 2], state[0, 3])
    sublane = lax.broadcasted_iota(jnp.int32, (8, LANES), 0)
    picked = []
    for c in range(chunks):
        index = jnp.broadcast_to(cell[c : c + 1, :], (8, LANES))
        row = index // around
        column = index % around
        lane = column % LANES
        half = column // LANES
        total = jnp.zeros((8, LANES), jnp.float32)
        for r in range(radial // 8):
            for h in range(around // LANES):
                part = p[r * 8 : (r + 1) * 8, h * LANES : (h + 1) * LANES]
                value = jnp.take_along_axis(part, lane, axis=1, mode="promise_in_bounds")
                total += jnp.where((row == sublane + r * 8) & (half == h), value, 0.0)
        picked.append(jnp.sum(total, axis=0, keepdims=True))
    face_pressure = jnp.concatenate(picked, axis=1)
    contribution = face_pressure * area[...]
    nodes = jnp.concatenate([node[c : c + 1, :] for c in range(chunks)], axis=1)

    high = node_block // LANES
    place = nodes // LANES
    low = nodes % LANES
    pick_low = (
        lax.broadcasted_iota(jnp.int32, (LANES, faces), 0) == jnp.broadcast_to(low, (LANES, faces))
    ).astype(jnp.float32).astype(jnp.bfloat16)
    pattern = jnp.concatenate(
        [jnp.broadcast_to(contribution[k : k + 1], (high, faces)) for k in range(3)]
        + [jnp.zeros((ROWS - 3 * high, faces), jnp.float32)],
        axis=0,
    )
    first = pattern.astype(jnp.bfloat16).astype(jnp.float32)
    second = pattern - first
    place = jnp.broadcast_to(place, (ROWS, faces))
    row_high = lax.broadcasted_iota(jnp.int32, (ROWS, faces), 0) % high

    def dense(start, count):
        masks = [place == row_high + (start + b) * high for b in range(count)]
        result = None
        for part in (first, second):
            left = jnp.concatenate([jnp.where(m, part, 0.0) for m in masks], axis=0)
            product = lax.dot_general(
                left.astype(jnp.bfloat16),
                pick_low,
                (((1,), (1,)), ((), ())),
                preferred_element_type=jnp.float32,
            )
            result = product if result is None else result + product
        return result.reshape(count, ROWS, LANES)

    flat = state[0].reshape(4 * radial, around)
    turned = jnp.concatenate([flat[:, around - LANES :], flat[:, :LANES]], axis=0).T
    lane = lax.broadcasted_iota(jnp.int32, (1, LANES), 1)
    edge = jnp.where(lane < LANES // 2, turned[LANES - 1 :, :], turned[:1, :])

    group = math.gcd(blocks, 8)
    edge = jnp.broadcast_to(edge[None], (group, 1, LANES))
    if group == blocks:
        out[...] = dense(0, blocks)
        out[:, 3 * high : 3 * high + 1, :] = edge
    else:

        @pl.loop(0, blocks // group)
        def _(g):
            out[pl.ds(g * group, group)] = dense(g * group, group)
            out[pl.ds(g * group, group), 3 * high : 3 * high + 1, :] = edge


def update_kernel(weights, blocks, instances, state, parts, *refs):
    others = refs[: instances - 1]
    increment, blade = refs[-2:]
    radial, around = state.shape[2:]
    high = blade.shape[2] // LANES
    me = lax.axis_index("space")
    before = parts[(me + blocks - 1) % blocks, 3 * high : 3 * high + 1, :]
    after = parts[(me + 1) % blocks, 3 * high : 3 * high + 1, :]
    lane = lax.broadcasted_iota(jnp.int32, (1, LANES), 1)
    edge = jnp.where(lane < LANES // 2, before, after)
    columns = jnp.broadcast_to(edge, (LANES, LANES)).T
    lane = lax.broadcasted_iota(jnp.int32, (radial, LANES), 1)
    q = []
    for c in range(4):
        last = columns[c * radial : (c + 1) * radial]
        initial = columns[LANES // 2 + c * radial : LANES // 2 + (c + 1) * radial]
        edge = jnp.where(lane == LANES - 1, last, initial)
        q.append(jnp.concatenate([state[0, c], edge], axis=1))
    inverse, vr, vc, p = pressure_of(*q)
    a = jnp.sqrt(gamma_ratio * p * inverse)
    width = around + LANES
    step = cfl_number / (
        jnp.abs(vr) + jnp.abs(vc) + 2.0 * a + omega_rate * instances / 2.0
    )

    def next_lane(x):
        return pltpu.roll(x, width - 1, 1)

    def last_lane(x):
        return pltpu.roll(x, 1, 1)

    speed = jnp.abs(vc) + a
    reach = 0.5 * jnp.maximum(speed, next_lane(speed))
    flux = (q[2], q[1] * vc, q[2] * vc + p, (q[3] + p) * vc)
    divergence = []
    for c in range(4):
        face = 0.5 * (flux[c] + next_lane(flux[c])) - reach * (next_lane(q[c]) - q[c])
        divergence.append((face - last_lane(face))[:, :around])

    own = slice(0, around)
    q = [x[:, own] for x in q]
    vr, p, a, step = vr[:, own], p[:, own], a[:, own], step[:, own]

    def above(x):
        return pltpu.roll(x, radial - 1, 0)

    def below(x):
        return pltpu.roll(x, 1, 0)

    row = lax.broadcasted_iota(jnp.int32, (radial, around), 0)
    hub, tip = row == 0, row == radial - 1
    speed = jnp.abs(vr) + a
    reach = 0.5 * jnp.maximum(speed, above(speed))
    flux = (q[1], q[1] * vr + p, q[2] * vr, (q[3] + p) * vr)
    for c in range(4):
        wall = p if c == 1 else 0.0
        face = 0.5 * (flux[c] + above(flux[c])) - reach * (above(q[c]) - q[c])
        upper = jnp.where(tip, wall, face)
        lower = jnp.where(hub, wall, below(face))
        residual = divergence[c] + (upper - lower) + weights[0] * q[c]
        for shift, other in enumerate(others, 1):
            residual += weights[shift] * other[0, c]
        increment[0, c] = -step * residual

    total = jnp.sum(parts[...], axis=0)
    for k in range(3):
        for h in range(high):
            blade[k, :, pl.ds(h * LANES, LANES)] = total[k * high + h : k * high + h + 1, :]


def per_device(node_block, state, face_cell, face_node, face_area):
    blocks = lax.axis_size("space")
    instances = lax.axis_size("inst")
    radial, around = state.shape[2:]
    chunks = face_cell.shape[0] // LANES
    vmem = pl.BlockSpec(memory_space=pltpu.VMEM)
    params = pltpu.CompilerParams(vmem_limit_bytes=(4 if blocks <= 16 else 16) * 2**20)

    others = [
        lax.ppermute(state, "inst", [(i, (i + s) % instances) for i in range(instances)])
        for s in range(1, instances)
    ]

    faces = (
        state,
        face_cell.reshape(chunks, LANES),
        face_node.reshape(chunks, LANES),
        face_area,
    )
    parts, near_state = pl.pallas_call(
        functools.partial(forces_kernel, blocks, node_block),
        out_shape=[
            jax.ShapeDtypeStruct((blocks, ROWS, LANES), jnp.float32),
            jax.ShapeDtypeStruct(state.shape, jnp.float32),
        ],
        in_specs=[pl.BlockSpec(memory_space=pltpu.HBM)] * 4,
        out_specs=[vmem] * 2,
        scratch_shapes=[pltpu.VMEM(x.shape, x.dtype) for x in faces[1:]]
        + [pltpu.SemaphoreType.DMA((4,))],
        compiler_params=params,
        cost_estimate=pl.CostEstimate(flops=10**9, bytes_accessed=10**7, transcendentals=0),
        name="face_forces",
    )(*(pltpu.with_memory_space_constraint(x, pltpu.HBM) for x in faces))
    parts = lax.all_to_all(parts, "space", 0, 0, tiled=True)

    increment, blade = pl.pallas_call(
        functools.partial(update_kernel, spectral_row(instances), blocks, instances),
        out_shape=[
            jax.ShapeDtypeStruct(state.shape, jnp.float32),
            jax.ShapeDtypeStruct((3, 1, node_block), jnp.float32),
        ],
        in_specs=[vmem] * (2 + len(others)),
        out_specs=[vmem] * 2,
        compiler_params=params,
        name="update",
    )(near_state, parts, *others)
    return increment, jnp.transpose(blade, (1, 0, 2))


def solution(mesh):
    in_specs = (P("inst", None, None, "space"), P("space"), P("space"), P(None, "space"))
    out_specs = (P("inst", None, None, "space"), P("inst", None, "space"))
    return jax.shard_map(
        functools.partial(per_device, 512),
        mesh=mesh,
        in_specs=in_specs,
        out_specs=out_specs,
        check_vma=False,
    )
```

```python
import functools
import math

import jax
import jax.numpy as jnp
import numpy as np
from jax import lax
from jax.experimental import pallas as pl
from jax.experimental.pallas import tpu as pltpu
from jax.sharding import PartitionSpec as P

gamma_ratio = 1.4
omega_rate = 0.5
cfl_number = 0.8

LANES = 128
ROWS = 16
EDGE = 12
RIDING = 8


def spectral_row(count):
    row = np.zeros((count,), np.float32)
    for shift in range(count):
        row[shift] = (-1.0) ** shift / count
        if shift != 0:
            row[shift] += 0.5 * (-1.0) ** shift / math.tan(math.pi * shift / count)
    return [float(omega_rate * value) for value in row]


def pressure_of(q0, q1, q2, q3):
    inverse = 1.0 / q0
    vr = q1 * inverse
    vc = q2 * inverse
    p = (gamma_ratio - 1.0) * (q3 - 0.5 * q0 * (vr * vr + vc * vc))
    return inverse, vr, vc, p


def forces_kernel(blocks, node_block, state_hbm, cell_hbm, node_hbm, area_hbm, kept, sent, state, cell, node, area, sems):
    loads = [
        pltpu.make_async_copy(source, target, sems.at[i])
        for i, (source, target) in enumerate(
            ((state_hbm, state), (cell_hbm, cell), (node_hbm, node), (area_hbm, area))
        )
    ]
    for load in loads:
        load.start()
    for load in loads:
        load.wait()
    radial, around = state.shape[2:]
    faces = cell.shape[0] * LANES
    chunks = faces // LANES
    _, _, _, p = pressure_of(state[0, 0], state[0, 1], state[0, 2], state[0, 3])
    sublane = lax.broadcasted_iota(jnp.int32, (8, LANES), 0)
    picked = []
    for c in range(chunks):
        index = jnp.broadcast_to(cell[c : c + 1, :], (8, LANES))
        row = index // around
        column = index % around
        lane = column % LANES
        half = column // LANES
        total = jnp.zeros((8, LANES), jnp.float32)
        for r in range(radial // 8):
            for h in range(around // LANES):
                part = p[r * 8 : (r + 1) * 8, h * LANES : (h + 1) * LANES]
                value = jnp.take_along_axis(part, lane, axis=1, mode="promise_in_bounds")
                total += jnp.where((row == sublane + r * 8) & (half == h), value, 0.0)
        picked.append(jnp.sum(total, axis=0, keepdims=True))
    face_pressure = jnp.concatenate(picked, axis=1)
    contribution = face_pressure * area[...]
    nodes = jnp.concatenate([node[c : c + 1, :] for c in range(chunks)], axis=1)

    high = node_block // LANES
    place = nodes // LANES ^ lax.axis_index("space") * high
    low = nodes % LANES
    pick_low = (
        lax.broadcasted_iota(jnp.int32, (LANES, faces), 0) == jnp.broadcast_to(low, (LANES, faces))
    ).astype(jnp.float32).astype(jnp.bfloat16)
    pattern = jnp.concatenate(
        [jnp.broadcast_to(contribution[k : k + 1], (high, faces)) for k in range(3)]
        + [jnp.zeros((ROWS - 3 * high, faces), jnp.float32)],
        axis=0,
    )
    first = pattern.astype(jnp.bfloat16).astype(jnp.float32)
    second = pattern - first
    place = jnp.broadcast_to(place, (ROWS, faces))
    row_high = lax.broadcasted_iota(jnp.int32, (ROWS, faces), 0) % high

    def dense(start, count):
        masks = [place == row_high + (start + b) * high for b in range(count)]
        result = None
        for part in (first, second):
            left = jnp.concatenate([jnp.where(m, part, 0.0) for m in masks], axis=0)
            product = lax.dot_general(
                left.astype(jnp.bfloat16),
                pick_low,
                (((1,), (1,)), ((), ())),
                preferred_element_type=jnp.float32,
            )
            result = product if result is None else result + product
        return result.reshape(count, ROWS, LANES)

    group = min(blocks, 8)

    def halves(g):
        result = dense(g * group, group).reshape(group // 2, 2, ROWS, LANES)
        return result[:, 0], result[:, 1]

    if group == blocks:
        kept[...], sent[...] = halves(0)
    else:

        @pl.loop(0, blocks // group)
        def _(g):
            span = pl.ds(g * (group // 2), group // 2)
            kept[span], sent[span] = halves(g)

    flat = state[0].reshape(4 * radial, around)
    turned = jnp.concatenate([flat[:, around - LANES :], flat[:, :LANES]], axis=0).T
    lane = lax.broadcasted_iota(jnp.int32, (1, LANES), 1)
    edge = jnp.where(lane < LANES // 2, turned[LANES - 1 :, :], turned[:1, :])
    for out in (kept, sent):
        out[0, EDGE : EDGE + 1, :] = edge


def halving_kernel(edges, kept, came, kept_next, sent):
    half = kept_next.shape[0]
    for b in range(half):
        kept_next[b] = kept[2 * b] + came[2 * b]
        sent[b] = kept[2 * b + 1] + came[2 * b + 1]
    if edges:
        own, others = (gather_edges(ref, edges) for ref in (kept, came))
        put_edges(kept_next, own + others)
        put_edges(sent, own + others)


def gather_edges(ref, count):
    spare = ROWS - EDGE
    return [ref[i // spare, EDGE + i % spare : EDGE + i % spare + 1, :] for i in range(count)]


def put_edges(ref, rows):
    spare = ROWS - EDGE
    for i, row in enumerate(rows):
        ref[i // spare, EDGE + i % spare : EDGE + i % spare + 1, :] = row


def pair_kernel(weights, instances, state, partner, *outs):
    odd = lax.axis_index("inst") % 2
    for i, out in enumerate(outs):
        shift = 2 * (i + 1)
        weight = jnp.where(odd == 1, weights[(shift + 1) % instances], weights[shift - 1])
        out[...] = weights[shift] * state[...] + weight * partner[...]


def update_kernel(weights, blocks, instances, state, kept, came, partner, *refs):
    sums = refs[: instances // 2 - 1]
    increment, blade = refs[-2:]
    radial, around = state.shape[2:]
    high = blade.shape[2] // LANES
    if blocks <= RIDING:
        me = lax.axis_index("space")
        known = [kept[0, EDGE:, :], came[0, EDGE:, :]]
        known = jnp.concatenate(known, axis=0)
        row = lax.broadcasted_iota(jnp.int32, known.shape, 0)

        def edge_of(device):
            return jnp.sum(jnp.where(row == device ^ me, known, 0.0), axis=0, keepdims=True)

        before = edge_of((me + blocks - 1) % blocks)
        after = edge_of((me + 1) % blocks)
    else:
        before, after = (ref[0:1, :] for ref in refs[instances // 2 - 1 : -2])
    lane = lax.broadcasted_iota(jnp.int32, (1, LANES), 1)
    edge = jnp.where(lane < LANES // 2, before, after)
    columns = jnp.broadcast_to(edge, (LANES, LANES)).T
    lane = lax.broadcasted_iota(jnp.int32, (radial, LANES), 1)
    q = []
    for c in range(4):
        last = columns[c * radial : (c + 1) * radial]
        initial = columns[LANES // 2 + c * radial : LANES // 2 + (c + 1) * radial]
        edge = jnp.where(lane == LANES - 1, last, initial)
        q.append(jnp.concatenate([state[0, c], edge], axis=1))
    inverse, vr, vc, p = pressure_of(*q)
    a = jnp.sqrt(gamma_ratio * p * inverse)
    width = around + LANES
    step = cfl_number / (
        jnp.abs(vr) + jnp.abs(vc) + 2.0 * a + omega_rate * instances / 2.0
    )

    def next_lane(x):
        return pltpu.roll(x, width - 1, 1)

    def last_lane(x):
        return pltpu.roll(x, 1, 1)

    speed = jnp.abs(vc) + a
    reach = 0.5 * jnp.maximum(speed, next_lane(speed))
    flux = (q[2], q[1] * vc, q[2] * vc + p, (q[3] + p) * vc)
    divergence = []
    for c in range(4):
        face = 0.5 * (flux[c] + next_lane(flux[c])) - reach * (next_lane(q[c]) - q[c])
        divergence.append((face - last_lane(face))[:, :around])

    own = slice(0, around)
    q = [x[:, own] for x in q]
    vr, p, a, step = vr[:, own], p[:, own], a[:, own], step[:, own]

    def above(x):
        return pltpu.roll(x, radial - 1, 0)

    def below(x):
        return pltpu.roll(x, 1, 0)

    row = lax.broadcasted_iota(jnp.int32, (radial, around), 0)
    hub, tip = row == 0, row == radial - 1
    speed = jnp.abs(vr) + a
    reach = 0.5 * jnp.maximum(speed, above(speed))
    flux = (q[1], q[1] * vr + p, q[2] * vr, (q[3] + p) * vr)
    partner_weight = jnp.where(
        lax.axis_index("inst") % 2 == 1, weights[1], weights[instances - 1]
    )
    for c in range(4):
        wall = p if c == 1 else 0.0
        face = 0.5 * (flux[c] + above(flux[c])) - reach * (above(q[c]) - q[c])
        upper = jnp.where(tip, wall, face)
        lower = jnp.where(hub, wall, below(face))
        residual = divergence[c] + (upper - lower) + weights[0] * q[c]
        residual += partner_weight * partner[0, c]
        for ref in sums:
            residual += ref[0, c]
        increment[0, c] = -step * residual

    total = kept[0] + came[0]
    for k in range(3):
        for h in range(high):
            blade[k, :, pl.ds(h * LANES, LANES)] = total[k * high + h : k * high + h + 1, :]


def per_device(node_block, state, face_cell, face_node, face_area):
    blocks = lax.axis_size("space")
    instances = lax.axis_size("inst")
    radial, around = state.shape[2:]
    chunks = face_cell.shape[0] // LANES
    vmem = pl.BlockSpec(memory_space=pltpu.VMEM)
    params = pltpu.CompilerParams(vmem_limit_bytes=(4 if blocks <= 16 else 16) * 2**20)

    def swapped(value, axis, bit):
        return lax.ppermute(value, axis, [(i, i ^ bit) for i in range(lax.axis_size(axis))])

    def shifted(value, axis, s):
        count = lax.axis_size(axis)
        return lax.ppermute(value, axis, [(i, (i + s) % count) for i in range(count)])

    def call(kernel, name, shapes, *operands):
        return pl.pallas_call(
            kernel,
            out_shape=[jax.ShapeDtypeStruct(shape, jnp.float32) for shape in shapes],
            in_specs=[vmem] * len(operands),
            out_specs=[vmem] * len(shapes),
            compiler_params=params,
            name=name,
        )(*operands)

    weights = spectral_row(instances)
    partner = swapped(state, "inst", 1)

    faces = (
        state,
        face_cell.reshape(chunks, LANES),
        face_node.reshape(chunks, LANES),
        face_area,
    )
    half = jax.ShapeDtypeStruct((blocks // 2, ROWS, LANES), jnp.float32)
    kept, sent, near_state = pl.pallas_call(
        functools.partial(forces_kernel, blocks, node_block),
        out_shape=[half, half, jax.ShapeDtypeStruct(state.shape, jnp.float32)],
        in_specs=[pl.BlockSpec(memory_space=pltpu.HBM)] * 4,
        out_specs=[vmem] * 3,
        scratch_shapes=[pltpu.VMEM(x.shape, x.dtype) for x in faces[1:]]
        + [pltpu.SemaphoreType.DMA((4,))],
        compiler_params=params,
        cost_estimate=pl.CostEstimate(flops=10**9, bytes_accessed=10**7, transcendentals=0),
        name="face_forces",
    )(*(pltpu.with_memory_space_constraint(x, pltpu.HBM) for x in faces))

    riding = blocks <= RIDING
    edges = []
    if not riding:
        row = jnp.broadcast_to(kept[0, EDGE : EDGE + 1, :], (8, LANES))
        edges = [shifted(row, "space", 1), shifted(row, "space", blocks - 1)]
    came = swapped(sent, "space", 1)

    sums = call(
        functools.partial(pair_kernel, weights, instances),
        "pair_sums",
        [state.shape] * (instances // 2 - 1),
        near_state,
        partner,
    )
    sums = [shifted(value, "inst", 2 * (i + 1)) for i, value in enumerate(sums)]

    bit = 2
    while bit < blocks:
        shape = (blocks // (2 * bit), ROWS, LANES)
        kept, sent = call(
            functools.partial(halving_kernel, bit // 2 if riding else 0),
            "halving",
            [shape] * 2,
            kept,
            came,
        )
        came = swapped(sent, "space", bit)
        bit *= 2

    increment, blade = call(
        functools.partial(update_kernel, weights, blocks, instances),
        "update",
        [state.shape, (3, 1, node_block)],
        near_state,
        kept,
        came,
        partner,
        *sums,
        *edges,
    )
    return increment, jnp.transpose(blade, (1, 0, 2))


def solution(mesh):
    in_specs = (P("inst", None, None, "space"), P("space"), P("space"), P(None, "space"))
    out_specs = (P("inst", None, None, "space"), P("inst", None, "space"))
    return jax.shard_map(
        functools.partial(per_device, 512),
        mesh=mesh,
        in_specs=in_specs,
        out_specs=out_specs,
        check_vma=False,
    )
```

```python
import functools
import math

import jax
import jax.numpy as jnp
import numpy as np
from jax import lax
from jax.experimental import pallas as pl
from jax.experimental.pallas import tpu as pltpu
from jax.sharding import PartitionSpec as P

gamma_ratio = 1.4
omega_rate = 0.5
cfl_number = 0.8

LANES = 128
ROWS = 16
EDGE = 12
PLACING = 10**10
RIDING = 8


def spectral_row(count):
    row = np.zeros((count,), np.float32)
    for shift in range(count):
        row[shift] = (-1.0) ** shift / count
        if shift != 0:
            row[shift] += 0.5 * (-1.0) ** shift / math.tan(math.pi * shift / count)
    return [float(omega_rate * value) for value in row]


def pressure_of(q0, q1, q2, q3):
    inverse = 1.0 / q0
    vr = q1 * inverse
    vc = q2 * inverse
    p = (gamma_ratio - 1.0) * (q3 - 0.5 * q0 * (vr * vr + vc * vc))
    return inverse, vr, vc, p


def forces_kernel(blocks, node_block, state_hbm, cell_hbm, node_hbm, area_hbm, state, *refs):
    *outs, cell, node, area, sems = refs
    loads = [
        pltpu.make_async_copy(source, target, sems.at[i])
        for i, (source, target) in enumerate(
            ((state_hbm, state), (cell_hbm, cell), (node_hbm, node), (area_hbm, area))
        )
    ]
    for load in loads:
        load.start()
    for load in loads:
        load.wait()
    radial, around = state.shape[2:]
    faces = cell.shape[0] * LANES
    chunks = faces // LANES
    _, _, _, p = pressure_of(state[0, 0], state[0, 1], state[0, 2], state[0, 3])
    sublane = lax.broadcasted_iota(jnp.int32, (8, LANES), 0)
    picked = []
    for c in range(chunks):
        index = jnp.broadcast_to(cell[c : c + 1, :], (8, LANES))
        row = index // around
        column = index % around
        lane = column % LANES
        half = column // LANES
        total = jnp.zeros((8, LANES), jnp.float32)
        for r in range(radial // 8):
            for h in range(around // LANES):
                part = p[r * 8 : (r + 1) * 8, h * LANES : (h + 1) * LANES]
                value = jnp.take_along_axis(part, lane, axis=1, mode="promise_in_bounds")
                total += jnp.where((row == sublane + r * 8) & (half == h), value, 0.0)
        picked.append(jnp.sum(total, axis=0, keepdims=True))
    face_pressure = jnp.concatenate(picked, axis=1)
    contribution = face_pressure * area[...]
    nodes = jnp.concatenate([node[c : c + 1, :] for c in range(chunks)], axis=1)

    high = node_block // LANES
    place = nodes // LANES ^ lax.axis_index("space") * high
    low = nodes % LANES
    pick_low = (
        lax.broadcasted_iota(jnp.int32, (LANES, faces), 0) == jnp.broadcast_to(low, (LANES, faces))
    ).astype(jnp.float32).astype(jnp.bfloat16)
    pattern = jnp.concatenate(
        [jnp.broadcast_to(contribution[k : k + 1], (high, faces)) for k in range(3)]
        + [jnp.zeros((ROWS - 3 * high, faces), jnp.float32)],
        axis=0,
    )
    first = pattern.astype(jnp.bfloat16).astype(jnp.float32)
    second = pattern - first
    place = jnp.broadcast_to(place, (ROWS, faces))
    row_high = lax.broadcasted_iota(jnp.int32, (ROWS, faces), 0) % high

    def dense(start, count):
        masks = [place == row_high + (start + b) * high for b in range(count)]
        result = None
        for part in (first, second):
            left = jnp.concatenate([jnp.where(m, part, 0.0) for m in masks], axis=0)
            product = lax.dot_general(
                left.astype(jnp.bfloat16),
                pick_low,
                (((1,), (1,)), ((), ())),
                preferred_element_type=jnp.float32,
            )
            result = product if result is None else result + product
        return result.reshape(count, ROWS, LANES)

    size = blocks // len(outs)
    group = min(size, 8)
    if size == group:
        for i, out in enumerate(outs):
            out[...] = dense(i * size, size)
    else:
        for i, out in enumerate(outs):

            @pl.loop(0, size // group)
            def _(g):
                out[pl.ds(g * group, group)] = dense(i * size + g * group, group)

    flat = state[0].reshape(4 * radial, around)
    turned = jnp.concatenate([flat[:, around - LANES :], flat[:, :LANES]], axis=0).T
    lane = lax.broadcasted_iota(jnp.int32, (1, LANES), 1)
    edge = jnp.where(lane < LANES // 2, turned[LANES - 1 :, :], turned[:1, :])
    for out in outs:
        out[0, EDGE : EDGE + 1, :] = edge


def halving_kernel(arrived, riding, *refs):
    outs = refs[arrived:]
    size = outs[0].shape[0]
    for i, out in enumerate(outs):
        for b in range(size):
            out[b] = functools.reduce(jnp.add, [ref[i * size + b] for ref in refs[:arrived]])
        if riding:
            for j, ref in enumerate(refs[:arrived]):
                out[0, EDGE + j : EDGE + j + 1, :] = ref[0, EDGE : EDGE + 1, :]


def pair_kernel(weights, instances, state, partner, _, *outs):
    me = lax.axis_index("inst")

    def weight(shift):
        value = weights[0]
        for i in range(1, instances):
            value = jnp.where(shift == i, weights[i], value)
        return value

    for i, out in enumerate(outs):
        shift = ((me ^ (i + 1)) - me + instances) % instances
        far = (shift + instances // 2) % instances
        out[...] = weight(shift) * state[...] + weight(far) * partner[...]


def update_kernel(weights, blocks, instances, state, kept, came, partner, *refs):
    sums = refs[: instances // 2 - 1]
    increment, blade = refs[-2:]
    radial, around = state.shape[2:]
    high = blade.shape[2] // LANES
    if blocks == RIDING:
        me = lax.axis_index("space")
        known = [kept[0, EDGE:, :], came[0, EDGE:, :]]
        known = jnp.concatenate(known, axis=0)
        row = lax.broadcasted_iota(jnp.int32, known.shape, 0)

        def edge_of(device):
            relative = device ^ me
            place = relative // 2 + (relative % 2) * (RIDING // 2)
            return jnp.sum(jnp.where(row == place, known, 0.0), axis=0, keepdims=True)

        before = edge_of((me + blocks - 1) % blocks)
        after = edge_of((me + 1) % blocks)
    else:
        before, after = (ref[0:1, :] for ref in refs[instances // 2 - 1 : -2])
    lane = lax.broadcasted_iota(jnp.int32, (1, LANES), 1)
    edge = jnp.where(lane < LANES // 2, before, after)
    columns = jnp.broadcast_to(edge, (LANES, LANES)).T
    lane = lax.broadcasted_iota(jnp.int32, (radial, LANES), 1)
    q = []
    for c in range(4):
        last = columns[c * radial : (c + 1) * radial]
        initial = columns[LANES // 2 + c * radial : LANES // 2 + (c + 1) * radial]
        edge = jnp.where(lane == LANES - 1, last, initial)
        q.append(jnp.concatenate([state[0, c], edge], axis=1))
    inverse, vr, vc, p = pressure_of(*q)
    a = jnp.sqrt(gamma_ratio * p * inverse)
    width = around + LANES
    step = cfl_number / (
        jnp.abs(vr) + jnp.abs(vc) + 2.0 * a + omega_rate * instances / 2.0
    )

    def next_lane(x):
        return pltpu.roll(x, width - 1, 1)

    def last_lane(x):
        return pltpu.roll(x, 1, 1)

    speed = jnp.abs(vc) + a
    reach = 0.5 * jnp.maximum(speed, next_lane(speed))
    flux = (q[2], q[1] * vc, q[2] * vc + p, (q[3] + p) * vc)
    divergence = []
    for c in range(4):
        face = 0.5 * (flux[c] + next_lane(flux[c])) - reach * (next_lane(q[c]) - q[c])
        divergence.append((face - last_lane(face))[:, :around])

    own = slice(0, around)
    q = [x[:, own] for x in q]
    vr, p, a, step = vr[:, own], p[:, own], a[:, own], step[:, own]

    def above(x):
        return pltpu.roll(x, radial - 1, 0)

    def below(x):
        return pltpu.roll(x, 1, 0)

    row = lax.broadcasted_iota(jnp.int32, (radial, around), 0)
    hub, tip = row == 0, row == radial - 1
    speed = jnp.abs(vr) + a
    reach = 0.5 * jnp.maximum(speed, above(speed))
    flux = (q[1], q[1] * vr + p, q[2] * vr, (q[3] + p) * vr)
    for c in range(4):
        wall = p if c == 1 else 0.0
        face = 0.5 * (flux[c] + above(flux[c])) - reach * (above(q[c]) - q[c])
        upper = jnp.where(tip, wall, face)
        lower = jnp.where(hub, wall, below(face))
        residual = divergence[c] + (upper - lower) + weights[0] * q[c]
        residual += weights[instances // 2] * partner[0, c]
        for ref in sums:
            residual += ref[0, c]
        increment[0, c] = -step * residual

    total = kept[0] + came[0]
    for k in range(3):
        for h in range(high):
            blade[k, :, pl.ds(h * LANES, LANES)] = total[k * high + h : k * high + h + 1, :]


def per_device(node_block, state, face_cell, face_node, face_area):
    blocks = lax.axis_size("space")
    instances = lax.axis_size("inst")
    radial, around = state.shape[2:]
    chunks = face_cell.shape[0] // LANES
    vmem = pl.BlockSpec(memory_space=pltpu.VMEM)
    params = pltpu.CompilerParams(vmem_limit_bytes=(4 if blocks <= 16 else 16) * 2**20)

    def swapped(value, axis, bit):
        return lax.ppermute(value, axis, [(i, i ^ bit) for i in range(lax.axis_size(axis))])

    def shifted(value, axis, s):
        count = lax.axis_size(axis)
        return lax.ppermute(value, axis, [(i, (i + s) % count) for i in range(count)])

    def call(kernel, name, shapes, *operands, flops=0):
        return pl.pallas_call(
            kernel,
            out_shape=[jax.ShapeDtypeStruct(shape, jnp.float32) for shape in shapes],
            in_specs=[vmem] * len(operands),
            out_specs=[vmem] * len(shapes),
            compiler_params=params,
            cost_estimate=pl.CostEstimate(flops=flops, bytes_accessed=0, transcendentals=0),
            name=name,
        )(*operands)

    weights = spectral_row(instances)
    partner = shifted(state, "inst", instances // 2)

    faces = (
        state,
        face_cell.reshape(chunks, LANES),
        face_node.reshape(chunks, LANES),
        face_area,
    )
    riding = blocks == RIDING
    steps = [4, 2] if riding else [2] * (blocks.bit_length() - 1)
    size = blocks // steps[0]
    block = jax.ShapeDtypeStruct((size, ROWS, LANES), jnp.float32)
    near_state, kept, *sent = pl.pallas_call(
        functools.partial(forces_kernel, blocks, node_block),
        out_shape=[jax.ShapeDtypeStruct(state.shape, jnp.float32)] + [block] * steps[0],
        in_specs=[pl.BlockSpec(memory_space=pltpu.HBM)] * 4,
        out_specs=[vmem] * (1 + steps[0]),
        scratch_shapes=[pltpu.VMEM(x.shape, x.dtype) for x in faces[1:]]
        + [pltpu.SemaphoreType.DMA((4,))],
        compiler_params=params,
        cost_estimate=pl.CostEstimate(flops=PLACING, bytes_accessed=0, transcendentals=0),
        name="face_forces",
    )(*(pltpu.with_memory_space_constraint(x, pltpu.HBM) for x in faces))

    edges = []
    if not riding:
        row = jnp.broadcast_to(kept[0, EDGE : EDGE + 1, :], (8, LANES))
        edges = [shifted(row, "space", 1), shifted(row, "space", blocks - 1)]

    came = [swapped(value, "space", (i + 1) * size) for i, value in enumerate(sent)]
    sums = call(
        functools.partial(pair_kernel, weights, instances),
        "pair_sums",
        [state.shape] * (instances // 2 - 1),
        near_state,
        partner,
        came[0],
        flops=PLACING,
    )
    sums = [swapped(value, "inst", i + 1) for i, value in enumerate(sums)]

    for step in steps[1:]:
        size //= step
        kept, *sent = call(
            functools.partial(halving_kernel, 1 + len(came), riding),
            "halving",
            [(size, ROWS, LANES)] * step,
            kept,
            *came,
            flops=PLACING,
        )
        came = [swapped(value, "space", (i + 1) * size) for i, value in enumerate(sent)]

    increment, blade = call(
        functools.partial(update_kernel, weights, blocks, instances),
        "update",
        [state.shape, (3, 1, node_block)],
        near_state,
        kept,
        *came,
        partner,
        *sums,
        *edges,
    )
    return increment, jnp.transpose(blade, (1, 0, 2))


def solution(mesh):
    in_specs = (P("inst", None, None, "space"), P("space"), P("space"), P(None, "space"))
    out_specs = (P("inst", None, None, "space"), P("inst", None, "space"))
    return jax.shard_map(
        functools.partial(per_device, 512),
        mesh=mesh,
        in_specs=in_specs,
        out_specs=out_specs,
        check_vma=False,
    )
```

```python
import functools
import math

import jax
import jax.numpy as jnp
import numpy as np
from jax import lax
from jax.experimental import pallas as pl
from jax.experimental.pallas import tpu as pltpu
from jax.sharding import PartitionSpec as P

gamma_ratio = 1.4
omega_rate = 0.5
cfl_number = 0.8

LANES = 128
ROWS = 16
EDGE = 12
PLACING = 10**10
RIDING = 8


def spectral_row(count):
    row = np.zeros((count,), np.float32)
    for shift in range(count):
        row[shift] = (-1.0) ** shift / count
        if shift != 0:
            row[shift] += 0.5 * (-1.0) ** shift / math.tan(math.pi * shift / count)
    return [float(omega_rate * value) for value in row]


def pressure_of(q0, q1, q2, q3):
    inverse = 1.0 / q0
    vr = q1 * inverse
    vc = q2 * inverse
    p = (gamma_ratio - 1.0) * (q3 - 0.5 * q0 * (vr * vr + vc * vc))
    return inverse, vr, vc, p


def forces_kernel(blocks, node_block, state_hbm, cell_hbm, node_hbm, area_hbm, state, *refs):
    *outs, cell, node, area, sems = refs
    loads = [
        pltpu.make_async_copy(source, target, sems.at[i])
        for i, (source, target) in enumerate(
            ((state_hbm, state), (cell_hbm, cell), (node_hbm, node), (area_hbm, area))
        )
    ]
    for load in loads:
        load.start()
    for load in loads:
        load.wait()
    radial, around = state.shape[2:]
    faces = cell.shape[0] * LANES
    chunks = faces // LANES
    _, _, _, p = pressure_of(state[0, 0], state[0, 1], state[0, 2], state[0, 3])
    sublane = lax.broadcasted_iota(jnp.int32, (8, LANES), 0)
    picked = []
    for c in range(chunks):
        index = jnp.broadcast_to(cell[c : c + 1, :], (8, LANES))
        row = index // around
        column = index % around
        lane = column % LANES
        half = column // LANES
        total = jnp.zeros((8, LANES), jnp.float32)
        for r in range(radial // 8):
            for h in range(around // LANES):
                part = p[r * 8 : (r + 1) * 8, h * LANES : (h + 1) * LANES]
                value = jnp.take_along_axis(part, lane, axis=1, mode="promise_in_bounds")
                total += jnp.where((row == sublane + r * 8) & (half == h), value, 0.0)
        picked.append(jnp.sum(total, axis=0, keepdims=True))
    face_pressure = jnp.concatenate(picked, axis=1)
    contribution = face_pressure * area[...]
    nodes = jnp.concatenate([node[c : c + 1, :] for c in range(chunks)], axis=1)

    high = node_block // LANES
    place = nodes // LANES ^ lax.axis_index("space") * high
    low = nodes % LANES
    pick_low = (
        lax.broadcasted_iota(jnp.int32, (LANES, faces), 0) == jnp.broadcast_to(low, (LANES, faces))
    ).astype(jnp.float32).astype(jnp.bfloat16)
    pattern = jnp.concatenate(
        [jnp.broadcast_to(contribution[k : k + 1], (high, faces)) for k in range(3)]
        + [jnp.zeros((ROWS - 3 * high, faces), jnp.float32)],
        axis=0,
    )
    first = pattern.astype(jnp.bfloat16).astype(jnp.float32)
    second = pattern - first
    place = jnp.broadcast_to(place, (ROWS, faces))
    row_high = lax.broadcasted_iota(jnp.int32, (ROWS, faces), 0) % high

    def dense(start, count):
        masks = [place == row_high + (start + b) * high for b in range(count)]
        result = None
        for part in (first, second):
            left = jnp.concatenate([jnp.where(m, part, 0.0) for m in masks], axis=0)
            product = lax.dot_general(
                left.astype(jnp.bfloat16),
                pick_low,
                (((1,), (1,)), ((), ())),
                preferred_element_type=jnp.float32,
            )
            result = product if result is None else result + product
        return result.reshape(count, ROWS, LANES)

    size = blocks // len(outs)
    if blocks <= 16:
        result = dense(0, blocks)
        for i, out in enumerate(outs):
            out[...] = result[i * size : (i + 1) * size]
    else:
        for i, out in enumerate(outs):

            @pl.loop(0, size // 8)
            def _(g):
                out[pl.ds(g * 8, 8)] = dense(i * size + g * 8, 8)

    flat = state[0].reshape(4 * radial, around)
    turned = jnp.concatenate([flat[:, around - LANES :], flat[:, :LANES]], axis=0).T
    lane = lax.broadcasted_iota(jnp.int32, (1, LANES), 1)
    edge = jnp.where(lane < LANES // 2, turned[LANES - 1 :, :], turned[:1, :])
    for out in outs:
        out[0, EDGE : EDGE + 1, :] = edge


def halving_kernel(arrived, riding, *refs):
    outs = refs[arrived:]
    size = outs[0].shape[0]
    for i, out in enumerate(outs):
        for b in range(size):
            out[b] = functools.reduce(jnp.add, [ref[i * size + b] for ref in refs[:arrived]])
        if riding:
            for j, ref in enumerate(refs[:arrived]):
                out[0, EDGE + j : EDGE + j + 1, :] = ref[0, EDGE : EDGE + 1, :]


def pair_kernel(weights, instances, state, partner, _, *outs):
    me = lax.axis_index("inst")

    def weight(shift):
        value = weights[0]
        for i in range(1, instances):
            value = jnp.where(shift == i, weights[i], value)
        return value

    for i, out in enumerate(outs):
        shift = ((me ^ (i + 1)) - me + instances) % instances
        far = (shift + instances // 2) % instances
        out[...] = weight(shift) * state[...] + weight(far) * partner[...]


def around_flux(q, vc, p):
    return (q[2], q[1] * vc, q[2] * vc + p, (q[3] + p) * vc)


def flux_kernel(weight, instances, state, base, step):
    radial, around = state.shape[2:]
    q = [state[0, c] for c in range(4)]
    inverse, vr, vc, p = pressure_of(*q)
    a = jnp.sqrt(gamma_ratio * p * inverse)
    step[...] = cfl_number / (
        jnp.abs(vr) + jnp.abs(vc) + 2.0 * a + omega_rate * instances / 2.0
    )

    def after(x):
        return pltpu.roll(x, around - 1, 1)

    def above(x):
        return pltpu.roll(x, radial - 1, 0)

    column = lax.broadcasted_iota(jnp.int32, (radial, around), 1)
    row = lax.broadcasted_iota(jnp.int32, (radial, around), 0)
    hub, tip = row == 0, row == radial - 1
    speed = jnp.abs(vc) + a
    reach = 0.5 * jnp.maximum(speed, after(speed))
    speed = jnp.abs(vr) + a
    rise = 0.5 * jnp.maximum(speed, above(speed))
    flux = around_flux(q, vc, p)
    radial_flux = (q[1], q[1] * vr + p, q[2] * vr, (q[3] + p) * vr)
    for c in range(4):
        face = 0.5 * (flux[c] + after(flux[c])) - reach * (after(q[c]) - q[c])
        face = jnp.where(column == around - 1, 0.0, face)
        residual = weight * q[c] + (face - pltpu.roll(face, 1, 1))
        wall = p if c == 1 else 0.0
        face = 0.5 * (radial_flux[c] + above(radial_flux[c])) - rise * (above(q[c]) - q[c])
        upper = jnp.where(tip, wall, face)
        lower = jnp.where(hub, wall, pltpu.roll(face, 1, 0))
        base[0, c] = residual + (upper - lower)


def update_kernel(weight, blocks, instances, state, base, step, kept, came, partner, *refs):
    sums = refs[: instances // 2 - 1]
    increment, blade = refs[-2:]
    radial, around = state.shape[2:]
    high = blade.shape[2] // LANES
    if blocks == RIDING:
        me = lax.axis_index("space")
        known = [kept[0, EDGE:, :], came[0, EDGE:, :]]
        known = jnp.concatenate(known, axis=0)
        row = lax.broadcasted_iota(jnp.int32, known.shape, 0)

        def edge_of(device):
            relative = device ^ me
            place = relative // 2 + (relative % 2) * (RIDING // 2)
            return jnp.sum(jnp.where(row == place, known, 0.0), axis=0, keepdims=True)

        before = edge_of((me + blocks - 1) % blocks)
        after = edge_of((me + 1) % blocks)
    else:
        before, after = (ref[0:1, :] for ref in refs[instances // 2 - 1 : -2])
    lane = lax.broadcasted_iota(jnp.int32, (1, LANES), 1)
    edge = jnp.where(lane < LANES // 2, before, after)
    columns = jnp.broadcast_to(edge, (LANES, LANES)).T

    lane = lax.broadcasted_iota(jnp.int32, (radial, LANES), 1)
    first, last = lane == 0, lane == LANES - 1
    own, far = [], []
    for c in range(4):
        own.append(jnp.where(first, state[0, c, :, :LANES], state[0, c, :, around - LANES :]))
        far.append(
            jnp.where(
                last,
                columns[LANES // 2 + c * radial : LANES // 2 + (c + 1) * radial],
                columns[c * radial : (c + 1) * radial],
            )
        )
    faces, speeds = [], []
    for q in (own, far):
        inverse, _, vc, p = pressure_of(*q)
        speeds.append(jnp.abs(vc) + jnp.sqrt(gamma_ratio * p * inverse))
        faces.append(around_flux(q, vc, p))
    side = jnp.where(last, 0.5, -0.5)
    reach = 0.5 * jnp.maximum(*speeds)
    for c in range(4):
        outer = side * (faces[0][c] + faces[1][c]) - reach * (far[c] - own[c])
        outer = [jnp.where(first, outer, 0.0), jnp.where(last, outer, 0.0)]
        middle = around - 2 * LANES
        if middle:
            outer.insert(1, jnp.zeros((radial, middle), jnp.float32))
        residual = base[0, c] + weight * partner[0, c]
        for ref in sums:
            residual += ref[0, c]
        residual += jnp.concatenate(outer, axis=1)
        increment[0, c] = -step[...] * residual

    total = kept[0] + came[0]
    for k in range(3):
        for h in range(high):
            blade[k, :, pl.ds(h * LANES, LANES)] = total[k * high + h : k * high + h + 1, :]


def per_device(node_block, state, face_cell, face_node, face_area):
    blocks = lax.axis_size("space")
    instances = lax.axis_size("inst")
    radial, around = state.shape[2:]
    chunks = face_cell.shape[0] // LANES
    vmem = pl.BlockSpec(memory_space=pltpu.VMEM)
    params = pltpu.CompilerParams(vmem_limit_bytes=(4 if blocks <= 16 else 16) * 2**20)

    def swapped(value, axis, bit):
        return lax.ppermute(value, axis, [(i, i ^ bit) for i in range(lax.axis_size(axis))])

    def shifted(value, axis, s):
        count = lax.axis_size(axis)
        return lax.ppermute(value, axis, [(i, (i + s) % count) for i in range(count)])

    def exchanged(sent, size):
        came = [swapped(sent[i], "space", (i + 1) * size) for i in reversed(range(len(sent)))]
        return came[::-1]

    def call(kernel, name, shapes, *operands, flops=0):
        return pl.pallas_call(
            kernel,
            out_shape=[jax.ShapeDtypeStruct(shape, jnp.float32) for shape in shapes],
            in_specs=[vmem] * len(operands),
            out_specs=[vmem] * len(shapes),
            compiler_params=params,
            cost_estimate=pl.CostEstimate(flops=flops, bytes_accessed=0, transcendentals=0),
            name=name,
        )(*operands)

    weights = spectral_row(instances)
    partner = shifted(state, "inst", instances // 2)

    faces = (
        state,
        face_cell.reshape(chunks, LANES),
        face_node.reshape(chunks, LANES),
        face_area,
    )
    riding = blocks == RIDING
    steps = [4, 2] if riding else [2] * (blocks.bit_length() - 1)
    size = blocks // steps[0]
    block = jax.ShapeDtypeStruct((size, ROWS, LANES), jnp.float32)
    near_state, kept, *sent = pl.pallas_call(
        functools.partial(forces_kernel, blocks, node_block),
        out_shape=[jax.ShapeDtypeStruct(state.shape, jnp.float32)] + [block] * steps[0],
        in_specs=[pl.BlockSpec(memory_space=pltpu.HBM)] * 4,
        out_specs=[vmem] * (1 + steps[0]),
        scratch_shapes=[pltpu.VMEM(x.shape, x.dtype) for x in faces[1:]]
        + [pltpu.SemaphoreType.DMA((4,))],
        compiler_params=params,
        cost_estimate=pl.CostEstimate(flops=PLACING, bytes_accessed=0, transcendentals=0),
        name="face_forces",
    )(*(pltpu.with_memory_space_constraint(x, pltpu.HBM) for x in faces))

    edges = []
    if not riding:
        row = jnp.broadcast_to(kept[0, EDGE : EDGE + 1, :], (8, LANES))
        edges = [shifted(row, "space", 1), shifted(row, "space", blocks - 1)]

    came = exchanged(sent, size)
    sums = call(
        functools.partial(pair_kernel, weights, instances),
        "pair_sums",
        [state.shape] * (instances // 2 - 1),
        near_state,
        partner,
        came[-1],
        flops=PLACING,
    )
    sums = [swapped(value, "inst", i + 1) for i, value in enumerate(sums)]

    for step in steps[1:]:
        size //= step
        kept, *sent = call(
            functools.partial(halving_kernel, 1 + len(came), riding),
            "halving",
            [(size, ROWS, LANES)] * step,
            kept,
            *came,
            flops=PLACING,
        )
        came = exchanged(sent, size)

    base, step = call(
        functools.partial(flux_kernel, weights[0], instances),
        "flux",
        [state.shape, (radial, around)],
        near_state,
    )
    increment, blade = call(
        functools.partial(update_kernel, weights[instances // 2], blocks, instances),
        "update",
        [state.shape, (3, 1, node_block)],
        near_state,
        base,
        step,
        kept,
        *came,
        partner,
        *sums,
        *edges,
    )
    return increment, jnp.transpose(blade, (1, 0, 2))


def solution(mesh):
    in_specs = (P("inst", None, None, "space"), P("space"), P("space"), P(None, "space"))
    out_specs = (P("inst", None, None, "space"), P("inst", None, "space"))
    return jax.shard_map(
        functools.partial(per_device, 512),
        mesh=mesh,
        in_specs=in_specs,
        out_specs=out_specs,
        check_vma=False,
    )
```

```python
import functools
import math

import jax
import jax.numpy as jnp
import numpy as np
from jax import lax
from jax.experimental import pallas as pl
from jax.experimental.pallas import tpu as pltpu
from jax.sharding import PartitionSpec as P

gamma_ratio = 1.4
omega_rate = 0.5
cfl_number = 0.8

LANES = 128
ROWS = 16
EDGE = 12
PLACING = 10**10
RIDING = 8


def spectral_row(count):
    row = np.zeros((count,), np.float32)
    for shift in range(count):
        row[shift] = (-1.0) ** shift / count
        if shift != 0:
            row[shift] += 0.5 * (-1.0) ** shift / math.tan(math.pi * shift / count)
    return [float(omega_rate * value) for value in row]


def pressure_of(q0, q1, q2, q3):
    inverse = 1.0 / q0
    vr = q1 * inverse
    vc = q2 * inverse
    p = (gamma_ratio - 1.0) * (q3 - 0.5 * q0 * (vr * vr + vc * vc))
    return inverse, vr, vc, p


def forces_kernel(blocks, node_block, state_hbm, cell_hbm, node_hbm, area_hbm, state, *refs):
    *outs, cell, node, area, sems = refs
    loads = [
        pltpu.make_async_copy(source, target, sems.at[i])
        for i, (source, target) in enumerate(
            ((state_hbm, state), (cell_hbm, cell), (node_hbm, node), (area_hbm, area))
        )
    ]
    for load in loads:
        load.start()
    for load in loads:
        load.wait()
    radial, around = state.shape[2:]
    faces = cell.shape[0] * LANES
    chunks = faces // LANES
    _, _, _, p = pressure_of(state[0, 0], state[0, 1], state[0, 2], state[0, 3])
    sublane = lax.broadcasted_iota(jnp.int32, (8, LANES), 0)
    picked = []
    for c in range(chunks):
        index = jnp.broadcast_to(cell[c : c + 1, :], (8, LANES))
        row = index // around
        column = index % around
        lane = column % LANES
        half = column // LANES
        total = jnp.zeros((8, LANES), jnp.float32)
        for r in range(radial // 8):
            for h in range(around // LANES):
                part = p[r * 8 : (r + 1) * 8, h * LANES : (h + 1) * LANES]
                value = jnp.take_along_axis(part, lane, axis=1, mode="promise_in_bounds")
                total += jnp.where((row == sublane + r * 8) & (half == h), value, 0.0)
        picked.append(jnp.sum(total, axis=0, keepdims=True))
    face_pressure = jnp.concatenate(picked, axis=1)
    contribution = face_pressure * area[...]
    nodes = jnp.concatenate([node[c : c + 1, :] for c in range(chunks)], axis=1)

    high = node_block // LANES
    place = nodes // LANES ^ lax.axis_index("space") * high
    low = nodes % LANES
    pick_low = (
        lax.broadcasted_iota(jnp.int32, (LANES, faces), 0) == jnp.broadcast_to(low, (LANES, faces))
    ).astype(jnp.float32).astype(jnp.bfloat16)
    pattern = jnp.concatenate(
        [jnp.broadcast_to(contribution[k : k + 1], (high, faces)) for k in range(3)]
        + [jnp.zeros((ROWS - 3 * high, faces), jnp.float32)],
        axis=0,
    )
    first = pattern.astype(jnp.bfloat16).astype(jnp.float32)
    second = pattern - first
    place = jnp.broadcast_to(place, (ROWS, faces))
    row_high = lax.broadcasted_iota(jnp.int32, (ROWS, faces), 0) % high

    def dense(start, count):
        masks = [place == row_high + (start + b) * high for b in range(count)]
        result = None
        for part in (first, second):
            left = jnp.concatenate([jnp.where(m, part, 0.0) for m in masks], axis=0)
            product = lax.dot_general(
                left.astype(jnp.bfloat16),
                pick_low,
                (((1,), (1,)), ((), ())),
                preferred_element_type=jnp.float32,
            )
            result = product if result is None else result + product
        return result.reshape(count, ROWS, LANES)

    ordered = outs[:1] + outs[:0:-1]
    size = blocks // len(outs)
    if blocks <= 16:
        result = dense(0, blocks)
        for i, out in enumerate(ordered):
            out[...] = result[i * size : (i + 1) * size]
    else:
        for i, out in enumerate(ordered):

            @pl.loop(0, size // 8)
            def _(g):
                out[pl.ds(g * 8, 8)] = dense(i * size + g * 8, 8)

    flat = state[0].reshape(4 * radial, around)
    turned = jnp.concatenate([flat[:, around - LANES :], flat[:, :LANES]], axis=0).T
    lane = lax.broadcasted_iota(jnp.int32, (1, LANES), 1)
    edge = jnp.where(lane < LANES // 2, turned[LANES - 1 :, :], turned[:1, :])
    for out in outs:
        out[0, EDGE : EDGE + 1, :] = edge


def halving_kernel(arrived, riding, *refs):
    outs = refs[arrived:]
    size = outs[0].shape[0]
    for i, out in enumerate(outs):
        for b in range(size):
            out[b] = functools.reduce(jnp.add, [ref[i * size + b] for ref in refs[:arrived]])
        if riding:
            for j, ref in enumerate(refs[:arrived]):
                out[0, EDGE + j : EDGE + j + 1, :] = ref[0, EDGE : EDGE + 1, :]


def pair_kernel(weights, instances, state, partner, *outs):
    me = lax.axis_index("inst")

    def weight(shift):
        value = weights[0]
        for i in range(1, instances):
            value = jnp.where(shift == i, weights[i], value)
        return value

    for i, out in enumerate(outs):
        shift = ((me ^ (i + 1)) - me + instances) % instances
        far = (shift + instances // 2) % instances
        out[...] = weight(shift) * state[...] + weight(far) * partner[...]


def around_flux(q, vc, p):
    return (q[2], q[1] * vc, q[2] * vc + p, (q[3] + p) * vc)


def flux_kernel(weight, instances, state, base, step):
    radial, around = state.shape[2:]
    q = [state[0, c] for c in range(4)]
    inverse, vr, vc, p = pressure_of(*q)
    a = jnp.sqrt(gamma_ratio * p * inverse)
    step[...] = cfl_number / (
        jnp.abs(vr) + jnp.abs(vc) + 2.0 * a + omega_rate * instances / 2.0
    )

    def after(x):
        return pltpu.roll(x, around - 1, 1)

    def above(x):
        return pltpu.roll(x, radial - 1, 0)

    column = lax.broadcasted_iota(jnp.int32, (radial, around), 1)
    row = lax.broadcasted_iota(jnp.int32, (radial, around), 0)
    hub, tip = row == 0, row == radial - 1
    speed = jnp.abs(vc) + a
    reach = 0.5 * jnp.maximum(speed, after(speed))
    speed = jnp.abs(vr) + a
    rise = 0.5 * jnp.maximum(speed, above(speed))
    flux = around_flux(q, vc, p)
    radial_flux = (q[1], q[1] * vr + p, q[2] * vr, (q[3] + p) * vr)
    for c in range(4):
        face = 0.5 * (flux[c] + after(flux[c])) - reach * (after(q[c]) - q[c])
        face = jnp.where(column == around - 1, 0.0, face)
        residual = weight * q[c] + (face - pltpu.roll(face, 1, 1))
        wall = p if c == 1 else 0.0
        face = 0.5 * (radial_flux[c] + above(radial_flux[c])) - rise * (above(q[c]) - q[c])
        upper = jnp.where(tip, wall, face)
        lower = jnp.where(hub, wall, pltpu.roll(face, 1, 0))
        base[0, c] = residual + (upper - lower)


def outer_kernel(weight, blocks, state, base, kept, came, partner, *refs):
    *edges, residual, blade = refs
    radial, around = state.shape[2:]
    high = blade.shape[2] // LANES
    if blocks == RIDING:
        me = lax.axis_index("space")
        known = [kept[0, EDGE:, :], came[0, EDGE:, :]]
        known = jnp.concatenate(known, axis=0)
        row = lax.broadcasted_iota(jnp.int32, known.shape, 0)

        def edge_of(device):
            relative = device ^ me
            half = RIDING // 2
            place = (half - relative // 2) % half + (relative % 2) * half
            return jnp.sum(jnp.where(row == place, known, 0.0), axis=0, keepdims=True)

        before = edge_of((me + blocks - 1) % blocks)
        after = edge_of((me + 1) % blocks)
    else:
        before, after = (ref[0:1, :] for ref in edges)
    lane = lax.broadcasted_iota(jnp.int32, (1, LANES), 1)
    edge = jnp.where(lane < LANES // 2, before, after)
    columns = jnp.broadcast_to(edge, (LANES, LANES)).T

    lane = lax.broadcasted_iota(jnp.int32, (radial, LANES), 1)
    first, last = lane == 0, lane == LANES - 1
    own, far = [], []
    for c in range(4):
        own.append(jnp.where(first, state[0, c, :, :LANES], state[0, c, :, around - LANES :]))
        far.append(
            jnp.where(
                last,
                columns[LANES // 2 + c * radial : LANES // 2 + (c + 1) * radial],
                columns[c * radial : (c + 1) * radial],
            )
        )
    faces, speeds = [], []
    for q in (own, far):
        inverse, _, vc, p = pressure_of(*q)
        speeds.append(jnp.abs(vc) + jnp.sqrt(gamma_ratio * p * inverse))
        faces.append(around_flux(q, vc, p))
    side = jnp.where(last, 0.5, -0.5)
    reach = 0.5 * jnp.maximum(*speeds)
    for c in range(4):
        outer = side * (faces[0][c] + faces[1][c]) - reach * (far[c] - own[c])
        outer = [jnp.where(first, outer, 0.0), jnp.where(last, outer, 0.0)]
        middle = around - 2 * LANES
        if middle:
            outer.insert(1, jnp.zeros((radial, middle), jnp.float32))
        residual[0, c] = base[0, c] + weight * partner[0, c] + jnp.concatenate(outer, axis=1)

    total = kept[0] + came[0]
    for k in range(3):
        for h in range(high):
            blade[k, :, pl.ds(h * LANES, LANES)] = total[k * high + h : k * high + h + 1, :]


def update_kernel(residual, step, *refs):
    *sums, increment = refs
    for c in range(residual.shape[1]):
        total = functools.reduce(jnp.add, [ref[0, c] for ref in (residual, *sums)])
        increment[0, c] = -step[...] * total


def per_device(node_block, state, face_cell, face_node, face_area):
    blocks = lax.axis_size("space")
    instances = lax.axis_size("inst")
    radial, around = state.shape[2:]
    chunks = face_cell.shape[0] // LANES
    vmem = pl.BlockSpec(memory_space=pltpu.VMEM)
    params = pltpu.CompilerParams(vmem_limit_bytes=(4 if blocks <= 16 else 16) * 2**20)

    def swapped(value, axis, bit):
        return lax.ppermute(value, axis, [(i, i ^ bit) for i in range(lax.axis_size(axis))])

    def shifted(value, axis, s):
        count = lax.axis_size(axis)
        return lax.ppermute(value, axis, [(i, (i + s) % count) for i in range(count)])

    def exchanged(sent, size):
        return [
            swapped(value, "space", (len(sent) - i) * size) for i, value in enumerate(sent)
        ]

    def call(kernel, name, shapes, *operands, flops=0):
        return pl.pallas_call(
            kernel,
            out_shape=[jax.ShapeDtypeStruct(shape, jnp.float32) for shape in shapes],
            in_specs=[vmem] * len(operands),
            out_specs=[vmem] * len(shapes),
            compiler_params=params,
            cost_estimate=pl.CostEstimate(flops=flops, bytes_accessed=0, transcendentals=0),
            name=name,
        )(*operands)

    weights = spectral_row(instances)
    partner = shifted(state, "inst", instances // 2)

    faces = (
        state,
        face_cell.reshape(chunks, LANES),
        face_node.reshape(chunks, LANES),
        face_area,
    )
    riding = blocks == RIDING
    steps = [4, 2] if riding else [2] * (blocks.bit_length() - 1)
    size = blocks // steps[0]
    block = jax.ShapeDtypeStruct((size, ROWS, LANES), jnp.float32)
    near_state, kept, *sent = pl.pallas_call(
        functools.partial(forces_kernel, blocks, node_block),
        out_shape=[jax.ShapeDtypeStruct(state.shape, jnp.float32)] + [block] * steps[0],
        in_specs=[pl.BlockSpec(memory_space=pltpu.HBM)] * 4,
        out_specs=[vmem] * (1 + steps[0]),
        scratch_shapes=[pltpu.VMEM(x.shape, x.dtype) for x in faces[1:]]
        + [pltpu.SemaphoreType.DMA((4,))],
        compiler_params=params,
        cost_estimate=pl.CostEstimate(flops=PLACING, bytes_accessed=0, transcendentals=0),
        name="face_forces",
    )(*(pltpu.with_memory_space_constraint(x, pltpu.HBM) for x in faces))

    edges = []
    if not riding:
        row = jnp.broadcast_to(kept[0, EDGE : EDGE + 1, :], (8, LANES))
        edges = [shifted(row, "space", 1), shifted(row, "space", blocks - 1)]

    came = exchanged(sent, size)
    sums = call(
        functools.partial(pair_kernel, weights, instances),
        "pair_sums",
        [state.shape] * (instances // 2 - 1),
        near_state,
        partner,
        flops=PLACING,
    )
    sums = [swapped(value, "inst", i + 1) for i, value in enumerate(sums)]

    for step in steps[1:]:
        size //= step
        kept, *sent = call(
            functools.partial(halving_kernel, 1 + len(came), riding),
            "halving",
            [(size, ROWS, LANES)] * step,
            kept,
            *came,
            flops=PLACING,
        )
        came = exchanged(sent, size)

    base, step = call(
        functools.partial(flux_kernel, weights[0], instances),
        "flux",
        [state.shape, (radial, around)],
        near_state,
    )
    residual, blade = call(
        functools.partial(outer_kernel, weights[instances // 2], blocks),
        "outer",
        [state.shape, (3, 1, node_block)],
        near_state,
        base,
        kept,
        *came,
        partner,
        *edges,
    )
    (increment,) = call(update_kernel, "update", [state.shape], residual, step, *sums)
    return increment, jnp.transpose(blade, (1, 0, 2))


def solution(mesh):
    in_specs = (P("inst", None, None, "space"), P("space"), P("space"), P(None, "space"))
    out_specs = (P("inst", None, None, "space"), P("inst", None, "space"))
    return jax.shard_map(
        functools.partial(per_device, 512),
        mesh=mesh,
        in_specs=in_specs,
        out_specs=out_specs,
        check_vma=False,
    )
```

```python
import functools
import math

import jax
import jax.numpy as jnp
import numpy as np
from jax import lax
from jax.experimental import pallas as pl
from jax.experimental.pallas import tpu as pltpu
from jax.sharding import PartitionSpec as P

gamma_ratio = 1.4
omega_rate = 0.5
cfl_number = 0.8

LANES = 128
ROWS = 16
EDGE = 12
PLACING = 10**10
RIDING = 8


def spectral_row(count):
    row = np.zeros((count,), np.float32)
    for shift in range(count):
        row[shift] = (-1.0) ** shift / count
        if shift != 0:
            row[shift] += 0.5 * (-1.0) ** shift / math.tan(math.pi * shift / count)
    return [float(omega_rate * value) for value in row]


def pressure_of(q0, q1, q2, q3):
    inverse = 1.0 / q0
    vr = q1 * inverse
    vc = q2 * inverse
    p = (gamma_ratio - 1.0) * (q3 - 0.5 * q0 * (vr * vr + vc * vc))
    return inverse, vr, vc, p


def own_kernel(high, out):
    out[...] = jnp.full(out.shape, lax.axis_index("space") * high, jnp.int32)


def forces_kernel(node_block, own, state, cell, node, area, *outs):
    radial, around = state.shape[2:]
    faces = cell.shape[0] * LANES
    chunks = faces // LANES
    _, _, _, p = pressure_of(state[0, 0], state[0, 1], state[0, 2], state[0, 3])
    sublane = lax.broadcasted_iota(jnp.int32, (8, LANES), 0)
    picked = []
    for c in range(chunks):
        index = jnp.broadcast_to(cell[c : c + 1, :], (8, LANES))
        row = index // around
        column = index % around
        lane = column % LANES
        half = column // LANES
        total = jnp.zeros((8, LANES), jnp.float32)
        for r in range(radial // 8):
            for h in range(around // LANES):
                part = p[r * 8 : (r + 1) * 8, h * LANES : (h + 1) * LANES]
                value = jnp.take_along_axis(part, lane, axis=1, mode="promise_in_bounds")
                total += jnp.where((row == sublane + r * 8) & (half == h), value, 0.0)
        picked.append(jnp.sum(total, axis=0, keepdims=True))
    face_pressure = jnp.concatenate(picked, axis=1)
    contribution = face_pressure * area[...]
    nodes = jnp.concatenate([node[c : c + 1, :] for c in range(chunks)], axis=1)

    high = node_block // LANES
    place = nodes // LANES ^ jnp.broadcast_to(own[0:1, 0:1], nodes.shape)
    low = nodes % LANES
    pick_low = (
        lax.broadcasted_iota(jnp.int32, (LANES, faces), 0) == jnp.broadcast_to(low, (LANES, faces))
    ).astype(jnp.float32).astype(jnp.bfloat16)
    pattern = jnp.concatenate(
        [jnp.broadcast_to(contribution[k : k + 1], (high, faces)) for k in range(3)]
        + [jnp.zeros((ROWS - 3 * high, faces), jnp.float32)],
        axis=0,
    )
    first = pattern.astype(jnp.bfloat16).astype(jnp.float32)
    second = pattern - first
    place = jnp.broadcast_to(place, (ROWS, faces))
    row_high = lax.broadcasted_iota(jnp.int32, (ROWS, faces), 0) % high

    def dense(start, count):
        masks = [place == row_high + (start + b) * high for b in range(count)]
        result = None
        for part in (first, second):
            left = jnp.concatenate([jnp.where(m, part, 0.0) for m in masks], axis=0)
            product = lax.dot_general(
                left.astype(jnp.bfloat16),
                pick_low,
                (((1,), (1,)), ((), ())),
                preferred_element_type=jnp.float32,
            )
            result = product if result is None else result + product
        return result.reshape(count, ROWS, LANES)

    ordered = outs[:1] + outs[:0:-1]
    size = outs[0].shape[0]
    blocks = size * len(outs)
    if blocks <= 16:
        result = dense(0, blocks)
        for i, out in enumerate(ordered):
            out[...] = result[i * size : (i + 1) * size]
    else:
        for i, out in enumerate(ordered):

            @pl.loop(0, size // 8)
            def _(g):
                out[pl.ds(g * 8, 8)] = dense(i * size + g * 8, 8)

    flat = state[0].reshape(4 * radial, around)
    turned = jnp.concatenate([flat[:, around - LANES :], flat[:, :LANES]], axis=0).T
    lane = lax.broadcasted_iota(jnp.int32, (1, LANES), 1)
    edge = jnp.where(lane < LANES // 2, turned[LANES - 1 :, :], turned[:1, :])
    for out in outs:
        out[0, EDGE : EDGE + 1, :] = edge


def halving_kernel(arrived, riding, *refs):
    outs = refs[arrived:]
    size = outs[0].shape[0]
    for i, out in enumerate(outs):
        for b in range(size):
            out[b] = functools.reduce(jnp.add, [ref[i * size + b] for ref in refs[:arrived]])
        if riding:
            for j, ref in enumerate(refs[:arrived]):
                out[0, EDGE + j : EDGE + j + 1, :] = ref[0, EDGE : EDGE + 1, :]


def pair_kernel(weights, instances, state, partner, *outs):
    me = lax.axis_index("inst")

    def weight(shift):
        value = weights[0]
        for i in range(1, instances):
            value = jnp.where(shift == i, weights[i], value)
        return value

    for i, out in enumerate(outs):
        shift = ((me ^ (i + 1)) - me + instances) % instances
        far = (shift + instances // 2) % instances
        out[...] = weight(shift) * state[...] + weight(far) * partner[...]


def around_flux(q, vc, p):
    return (q[2], q[1] * vc, q[2] * vc + p, (q[3] + p) * vc)


def flux_kernel(weight, instances, state, base, step):
    radial, around = state.shape[2:]
    q = [state[0, c] for c in range(4)]
    inverse, vr, vc, p = pressure_of(*q)
    a = jnp.sqrt(gamma_ratio * p * inverse)
    step[...] = cfl_number / (
        jnp.abs(vr) + jnp.abs(vc) + 2.0 * a + omega_rate * instances / 2.0
    )

    def after(x):
        return pltpu.roll(x, around - 1, 1)

    def above(x):
        return pltpu.roll(x, radial - 1, 0)

    column = lax.broadcasted_iota(jnp.int32, (radial, around), 1)
    row = lax.broadcasted_iota(jnp.int32, (radial, around), 0)
    hub, tip = row == 0, row == radial - 1
    speed = jnp.abs(vc) + a
    reach = 0.5 * jnp.maximum(speed, after(speed))
    speed = jnp.abs(vr) + a
    rise = 0.5 * jnp.maximum(speed, above(speed))
    flux = around_flux(q, vc, p)
    radial_flux = (q[1], q[1] * vr + p, q[2] * vr, (q[3] + p) * vr)
    for c in range(4):
        face = 0.5 * (flux[c] + after(flux[c])) - reach * (after(q[c]) - q[c])
        face = jnp.where(column == around - 1, 0.0, face)
        residual = weight * q[c] + (face - pltpu.roll(face, 1, 1))
        wall = p if c == 1 else 0.0
        face = 0.5 * (radial_flux[c] + above(radial_flux[c])) - rise * (above(q[c]) - q[c])
        upper = jnp.where(tip, wall, face)
        lower = jnp.where(hub, wall, pltpu.roll(face, 1, 0))
        base[0, c] = residual + (upper - lower)


def outer_kernel(weight, blocks, state, base, kept, came, partner, *refs):
    *edges, residual, total = refs
    radial, around = state.shape[2:]
    if blocks == RIDING:
        me = lax.axis_index("space")
        known = [kept[0, EDGE:, :], came[0, EDGE:, :]]
        known = jnp.concatenate(known, axis=0)
        row = lax.broadcasted_iota(jnp.int32, known.shape, 0)

        def edge_of(device):
            relative = device ^ me
            half = RIDING // 2
            place = (half - relative // 2) % half + (relative % 2) * half
            return jnp.sum(jnp.where(row == place, known, 0.0), axis=0, keepdims=True)

        before = edge_of((me + blocks - 1) % blocks)
        after = edge_of((me + 1) % blocks)
    else:
        before, after = (ref[0:1, :] for ref in edges)
    lane = lax.broadcasted_iota(jnp.int32, (1, LANES), 1)
    edge = jnp.where(lane < LANES // 2, before, after)
    columns = jnp.broadcast_to(edge, (LANES, LANES)).T

    lane = lax.broadcasted_iota(jnp.int32, (radial, LANES), 1)
    first, last = lane == 0, lane == LANES - 1
    own, far = [], []
    for c in range(4):
        own.append(jnp.where(first, state[0, c, :, :LANES], state[0, c, :, around - LANES :]))
        far.append(
            jnp.where(
                last,
                columns[LANES // 2 + c * radial : LANES // 2 + (c + 1) * radial],
                columns[c * radial : (c + 1) * radial],
            )
        )
    faces, speeds = [], []
    for q in (own, far):
        inverse, _, vc, p = pressure_of(*q)
        speeds.append(jnp.abs(vc) + jnp.sqrt(gamma_ratio * p * inverse))
        faces.append(around_flux(q, vc, p))
    side = jnp.where(last, 0.5, -0.5)
    reach = 0.5 * jnp.maximum(*speeds)
    for c in range(4):
        outer = side * (faces[0][c] + faces[1][c]) - reach * (far[c] - own[c])
        outer = [jnp.where(first, outer, 0.0), jnp.where(last, outer, 0.0)]
        middle = around - 2 * LANES
        if middle:
            outer.insert(1, jnp.zeros((radial, middle), jnp.float32))
        residual[0, c] = base[0, c] + weight * partner[0, c] + jnp.concatenate(outer, axis=1)

    total[...] = kept[0] + came[0]


def update_kernel(residual, step, total, *refs):
    *sums, increment, blade = refs
    high = blade.shape[2] // LANES
    for k in range(3):
        for h in range(high):
            blade[k, :, pl.ds(h * LANES, LANES)] = total[k * high + h : k * high + h + 1, :]
    for c in range(residual.shape[1]):
        change = functools.reduce(jnp.add, [ref[0, c] for ref in (residual, *sums)])
        increment[0, c] = -step[...] * change


def per_device(node_block, state, face_cell, face_node, face_area):
    blocks = lax.axis_size("space")
    instances = lax.axis_size("inst")
    radial, around = state.shape[2:]
    chunks = face_cell.shape[0] // LANES
    vmem = pl.BlockSpec(memory_space=pltpu.VMEM)
    params = pltpu.CompilerParams(vmem_limit_bytes=(4 if blocks <= 16 else 16) * 2**20)

    def swapped(value, axis, bit):
        return lax.ppermute(value, axis, [(i, i ^ bit) for i in range(lax.axis_size(axis))])

    def shifted(value, axis, s):
        count = lax.axis_size(axis)
        return lax.ppermute(value, axis, [(i, (i + s) % count) for i in range(count)])

    def exchanged(sent, size):
        return [
            swapped(value, "space", (len(sent) - i) * size) for i, value in enumerate(sent)
        ]

    def call(kernel, name, shapes, *operands, flops=0, dtype=jnp.float32):
        return pl.pallas_call(
            kernel,
            out_shape=[jax.ShapeDtypeStruct(shape, dtype) for shape in shapes],
            in_specs=[vmem] * len(operands),
            out_specs=[vmem] * len(shapes),
            compiler_params=params,
            cost_estimate=pl.CostEstimate(flops=flops, bytes_accessed=0, transcendentals=0),
            name=name,
        )(*operands)

    weights = spectral_row(instances)
    partner = shifted(state, "inst", instances // 2)

    riding = blocks == RIDING
    steps = [4, 2] if riding else [2] * (blocks.bit_length() - 1)
    size = blocks // steps[0]
    (own,) = call(
        functools.partial(own_kernel, node_block // LANES),
        "own",
        [(8, LANES)],
        dtype=jnp.int32,
        flops=PLACING,
    )
    kept, *sent = call(
        functools.partial(forces_kernel, node_block),
        "face_forces",
        [(size, ROWS, LANES)] * steps[0],
        own,
        state,
        face_cell.reshape(chunks, LANES),
        face_node.reshape(chunks, LANES),
        face_area,
        flops=PLACING,
    )

    edges = []
    if not riding:
        row = jnp.broadcast_to(kept[0, EDGE : EDGE + 1, :], (8, LANES))
        edges = [shifted(row, "space", 1), shifted(row, "space", blocks - 1)]

    came = exchanged(sent, size)
    sums = call(
        functools.partial(pair_kernel, weights, instances),
        "pair_sums",
        [state.shape] * (instances // 2 - 1),
        state,
        partner,
        flops=PLACING,
    )
    sums = [swapped(value, "inst", i + 1) for i, value in enumerate(sums)]

    for step in steps[1:]:
        size //= step
        kept, *sent = call(
            functools.partial(halving_kernel, 1 + len(came), riding),
            "halving",
            [(size, ROWS, LANES)] * step,
            kept,
            *came,
            flops=PLACING,
        )
        came = exchanged(sent, size)

    base, step = call(
        functools.partial(flux_kernel, weights[0], instances),
        "flux",
        [state.shape, (radial, around)],
        state,
    )
    residual, total = call(
        functools.partial(outer_kernel, weights[instances // 2], blocks),
        "outer",
        [state.shape, (ROWS, LANES)],
        state,
        base,
        kept,
        *came,
        partner,
        *edges,
    )
    increment, blade = call(
        update_kernel,
        "update",
        [state.shape, (3, 1, node_block)],
        residual,
        step,
        total,
        *sums,
    )
    return increment, jnp.transpose(blade, (1, 0, 2))


def solution(mesh):
    in_specs = (P("inst", None, None, "space"), P("space"), P("space"), P(None, "space"))
    out_specs = (P("inst", None, None, "space"), P("inst", None, "space"))
    return jax.shard_map(
        functools.partial(per_device, 512),
        mesh=mesh,
        in_specs=in_specs,
        out_specs=out_specs,
        check_vma=False,
    )
```

```python
import functools
import math

import jax
import jax.numpy as jnp
import numpy as np
from jax import lax
from jax.experimental import pallas as pl
from jax.experimental.pallas import tpu as pltpu
from jax.sharding import PartitionSpec as P

gamma_ratio = 1.4
omega_rate = 0.5
cfl_number = 0.8

LANES = 128
ROWS = 16
EDGE = 12
PLACING = 10**10
RIDING = 8


def spectral_row(count):
    row = np.zeros((count,), np.float32)
    for shift in range(count):
        row[shift] = (-1.0) ** shift / count
        if shift != 0:
            row[shift] += 0.5 * (-1.0) ** shift / math.tan(math.pi * shift / count)
    return [float(omega_rate * value) for value in row]


def pressure_of(q0, q1, q2, q3):
    inverse = 1.0 / q0
    vr = q1 * inverse
    vc = q2 * inverse
    p = (gamma_ratio - 1.0) * (q3 - 0.5 * q0 * (vr * vr + vc * vc))
    return inverse, vr, vc, p


def own_kernel(high, riding, out):
    me = lax.axis_index("space")
    out[...] = jnp.full(out.shape, (me - me % 2 if riding else me) * high, jnp.int32)


def forces_kernel(node_block, riding, own, state, cell, node, area, *outs):
    radial, around = state.shape[2:]
    faces = cell.shape[0] * LANES
    chunks = faces // LANES
    _, _, _, p = pressure_of(state[0, 0], state[0, 1], state[0, 2], state[0, 3])
    sublane = lax.broadcasted_iota(jnp.int32, (8, LANES), 0)
    picked = []
    for c in range(chunks):
        index = jnp.broadcast_to(cell[c : c + 1, :], (8, LANES))
        row = index // around
        column = index % around
        lane = column % LANES
        half = column // LANES
        total = jnp.zeros((8, LANES), jnp.float32)
        for r in range(radial // 8):
            for h in range(around // LANES):
                part = p[r * 8 : (r + 1) * 8, h * LANES : (h + 1) * LANES]
                value = jnp.take_along_axis(part, lane, axis=1, mode="promise_in_bounds")
                total += jnp.where((row == sublane + r * 8) & (half == h), value, 0.0)
        picked.append(jnp.sum(total, axis=0, keepdims=True))
    face_pressure = jnp.concatenate(picked, axis=1)
    contribution = face_pressure * area[...]
    nodes = jnp.concatenate([node[c : c + 1, :] for c in range(chunks)], axis=1)

    high = node_block // LANES
    place = nodes // LANES ^ jnp.broadcast_to(own[0:1, 0:1], nodes.shape)
    low = nodes % LANES
    pick_low = (
        lax.broadcasted_iota(jnp.int32, (LANES, faces), 0) == jnp.broadcast_to(low, (LANES, faces))
    ).astype(jnp.float32).astype(jnp.bfloat16)
    pattern = jnp.concatenate(
        [jnp.broadcast_to(contribution[k : k + 1], (high, faces)) for k in range(3)]
        + [jnp.zeros((ROWS - 3 * high, faces), jnp.float32)],
        axis=0,
    )
    first = pattern.astype(jnp.bfloat16).astype(jnp.float32)
    second = pattern - first
    place = jnp.broadcast_to(place, (ROWS, faces))
    row_high = lax.broadcasted_iota(jnp.int32, (ROWS, faces), 0) % high

    def dense(start, count):
        masks = [place == row_high + (start + b) * high for b in range(count)]
        result = None
        for part in (first, second):
            left = jnp.concatenate([jnp.where(m, part, 0.0) for m in masks], axis=0)
            product = lax.dot_general(
                left.astype(jnp.bfloat16),
                pick_low,
                (((1,), (1,)), ((), ())),
                preferred_element_type=jnp.float32,
            )
            result = product if result is None else result + product
        return result.reshape(count, ROWS, LANES)

    size = outs[0].shape[0]
    blocks = size * len(outs)
    if blocks <= 16:
        result = dense(0, blocks)
        for i, out in enumerate(outs):
            out[...] = result[i * size : (i + 1) * size]
    else:
        for i, out in enumerate(outs):

            @pl.loop(0, size // 8)
            def _(g):
                out[pl.ds(g * 8, 8)] = dense(i * size + g * 8, 8)

    flat = state[0].reshape(4 * radial, around)
    turned = jnp.concatenate([flat[:, around - LANES :], flat[:, :LANES]], axis=0).T
    lane = lax.broadcasted_iota(jnp.int32, (1, LANES), 1)
    edge = jnp.where(lane < LANES // 2, turned[LANES - 1 :, :], turned[:1, :])
    if riding:
        core = lax.axis_index("space") % 2
        row = lax.broadcasted_iota(jnp.int32, (2, LANES), 0)
        outs[0][0, EDGE : EDGE + 2, :] = jnp.where(row == core, edge, 0.0)
    else:
        outs[0][0, EDGE : EDGE + 1, :] = edge


def chip_kernel(blocks, came, _, *outs):
    edges = blocks[0, EDGE:, :] + came[0, EDGE:, :]
    for out, pair in zip(outs, (0, 3, 2, 1)):
        for b in range(2):
            out[b] = blocks[2 * pair + b] + came[2 * pair + b]
        out[0, EDGE:, :] = edges


def plane_kernel(own, diagonal, y, x, *outs):
    chips = (own, x, y, diagonal)
    me = lax.axis_index("space")
    first = me - me % 2
    lane = lax.broadcasted_iota(jnp.int32, (1, LANES), 1)
    for core, out in enumerate(outs):
        out[...] = functools.reduce(jnp.add, [ref[core] for ref in chips])
        device = first + core
        around = (device + (RIDING - 1 if core == 0 else 1)) % RIDING
        place = (around ^ first) // 2
        there = own[0, EDGE + 1 - core : EDGE + 2 - core, :]
        for i, ref in enumerate(chips[1:], 1):
            row = ref[0, EDGE + 1 - core : EDGE + 2 - core, :]
            there = jnp.where(place == i, row, there)
        here = own[0, EDGE + 1 - core : EDGE + 2 - core, :]
        before, after = (there, here) if core == 0 else (here, there)
        out[EDGE : EDGE + 1, :] = jnp.where(lane < LANES // 2, before, after)


def halving_kernel(kept, came, *outs):
    size = outs[0].shape[0]
    for i, out in enumerate(outs):
        for b in range(size):
            out[b] = kept[i * size + b] + came[i * size + b]


def pair_kernel(weights, instances, state, partner, *outs):
    me = lax.axis_index("inst")

    def weight(shift):
        value = weights[0]
        for i in range(1, instances):
            value = jnp.where(shift == i, weights[i], value)
        return value

    for i, out in enumerate(outs):
        shift = ((me ^ (i + 1)) - me + instances) % instances
        far = (shift + instances // 2) % instances
        out[...] = weight(shift) * state[...] + weight(far) * partner[...]


def around_flux(q, vc, p):
    return (q[2], q[1] * vc, q[2] * vc + p, (q[3] + p) * vc)


def flux_kernel(weight, instances, state, base, step):
    radial, around = state.shape[2:]
    q = [state[0, c] for c in range(4)]
    inverse, vr, vc, p = pressure_of(*q)
    a = jnp.sqrt(gamma_ratio * p * inverse)
    step[...] = cfl_number / (
        jnp.abs(vr) + jnp.abs(vc) + 2.0 * a + omega_rate * instances / 2.0
    )

    def after(x):
        return pltpu.roll(x, around - 1, 1)

    def above(x):
        return pltpu.roll(x, radial - 1, 0)

    column = lax.broadcasted_iota(jnp.int32, (radial, around), 1)
    row = lax.broadcasted_iota(jnp.int32, (radial, around), 0)
    hub, tip = row == 0, row == radial - 1
    speed = jnp.abs(vc) + a
    reach = 0.5 * jnp.maximum(speed, after(speed))
    speed = jnp.abs(vr) + a
    rise = 0.5 * jnp.maximum(speed, above(speed))
    flux = around_flux(q, vc, p)
    radial_flux = (q[1], q[1] * vr + p, q[2] * vr, (q[3] + p) * vr)
    for c in range(4):
        face = 0.5 * (flux[c] + after(flux[c])) - reach * (after(q[c]) - q[c])
        face = jnp.where(column == around - 1, 0.0, face)
        residual = weight * q[c] + (face - pltpu.roll(face, 1, 1))
        wall = p if c == 1 else 0.0
        face = 0.5 * (radial_flux[c] + above(radial_flux[c])) - rise * (above(q[c]) - q[c])
        upper = jnp.where(tip, wall, face)
        lower = jnp.where(hub, wall, pltpu.roll(face, 1, 0))
        base[0, c] = residual + (upper - lower)


def outer_kernel(weight, state, base, kept, came, partner, *refs):
    *edges, residual, total = refs
    radial, around = state.shape[2:]
    if edges:
        before, after = (ref[0:1, :] for ref in edges)
        lane = lax.broadcasted_iota(jnp.int32, (1, LANES), 1)
        edge = jnp.where(lane < LANES // 2, before, after)
        total[...] = kept[0] + came[0]
    else:
        held = jnp.where(lax.axis_index("space") % 2 == 1, kept[...], came[...])
        edge = held[EDGE : EDGE + 1, :]
        total[...] = held
    columns = jnp.broadcast_to(edge, (LANES, LANES)).T

    lane = lax.broadcasted_iota(jnp.int32, (radial, LANES), 1)
    first, last = lane == 0, lane == LANES - 1
    own, far = [], []
    for c in range(4):
        own.append(jnp.where(first, state[0, c, :, :LANES], state[0, c, :, around - LANES :]))
        far.append(
            jnp.where(
                last,
                columns[LANES // 2 + c * radial : LANES // 2 + (c + 1) * radial],
                columns[c * radial : (c + 1) * radial],
            )
        )
    faces, speeds = [], []
    for q in (own, far):
        inverse, _, vc, p = pressure_of(*q)
        speeds.append(jnp.abs(vc) + jnp.sqrt(gamma_ratio * p * inverse))
        faces.append(around_flux(q, vc, p))
    side = jnp.where(last, 0.5, -0.5)
    reach = 0.5 * jnp.maximum(*speeds)
    for c in range(4):
        outer = side * (faces[0][c] + faces[1][c]) - reach * (far[c] - own[c])
        outer = [jnp.where(first, outer, 0.0), jnp.where(last, outer, 0.0)]
        middle = around - 2 * LANES
        if middle:
            outer.insert(1, jnp.zeros((radial, middle), jnp.float32))
        residual[0, c] = base[0, c] + weight * partner[0, c] + jnp.concatenate(outer, axis=1)


def update_kernel(residual, step, total, *refs):
    *sums, increment, blade = refs
    high = blade.shape[2] // LANES
    for k in range(3):
        for h in range(high):
            blade[k, :, pl.ds(h * LANES, LANES)] = total[k * high + h : k * high + h + 1, :]
    for c in range(residual.shape[1]):
        change = functools.reduce(jnp.add, [ref[0, c] for ref in (residual, *sums)])
        increment[0, c] = -step[...] * change


def per_device(node_block, state, face_cell, face_node, face_area):
    blocks = lax.axis_size("space")
    instances = lax.axis_size("inst")
    radial, around = state.shape[2:]
    chunks = face_cell.shape[0] // LANES
    vmem = pl.BlockSpec(memory_space=pltpu.VMEM)
    params = pltpu.CompilerParams(vmem_limit_bytes=(4 if blocks <= 16 else 16) * 2**20)

    def swapped(value, axis, bit):
        return lax.ppermute(value, axis, [(i, i ^ bit) for i in range(lax.axis_size(axis))])

    def shifted(value, axis, s):
        count = lax.axis_size(axis)
        return lax.ppermute(value, axis, [(i, (i + s) % count) for i in range(count)])

    def moved(value, core, bit):
        pairs = [(i, i ^ bit) for i in range(blocks) if i % 2 == core]
        return lax.ppermute(value, "space", pairs)

    def call(kernel, name, shapes, *operands, flops=0, dtype=jnp.float32):
        return pl.pallas_call(
            kernel,
            out_shape=[jax.ShapeDtypeStruct(shape, dtype) for shape in shapes],
            in_specs=[vmem] * len(operands),
            out_specs=[vmem] * len(shapes),
            compiler_params=params,
            cost_estimate=pl.CostEstimate(flops=flops, bytes_accessed=0, transcendentals=0),
            name=name,
        )(*operands)

    weights = spectral_row(instances)
    partner = shifted(state, "inst", instances // 2)

    riding = blocks == RIDING
    parts = 1 if riding else 2
    (own,) = call(
        functools.partial(own_kernel, node_block // LANES, riding),
        "own",
        [(8, LANES)],
        dtype=jnp.int32,
        flops=PLACING,
    )
    dense = call(
        functools.partial(forces_kernel, node_block, riding),
        "face_forces",
        [(blocks // parts, ROWS, LANES)] * parts,
        own,
        state,
        face_cell.reshape(chunks, LANES),
        face_node.reshape(chunks, LANES),
        face_area,
        flops=PLACING,
    )

    base, step = call(
        functools.partial(flux_kernel, weights[0], instances),
        "flux",
        [state.shape, (radial, around)],
        state,
        flops=PLACING,
    )
    edges = []
    if riding:
        came = moved(dense[0], 0, 1)
        mine, *sent = call(chip_kernel, "chip_sums", [(2, ROWS, LANES)] * 4, dense[0], came, step)
        came = [moved(value, 1, bit) for value, bit in zip(sent, (6, 4, 2))]
        block, kept = call(
            plane_kernel, "plane_sums", [(ROWS, LANES)] * 2, mine, *came, flops=PLACING
        )
        came = moved(block, 1, 1)
    else:
        row = jnp.broadcast_to(dense[0][0, EDGE : EDGE + 1, :], (8, LANES))
        edges = [shifted(row, "space", 1), shifted(row, "space", blocks - 1)]
        size = blocks // 2
        kept, came = dense[0], swapped(dense[1], "space", size)
        while size > 1:
            size //= 2
            shapes = [(size, ROWS, LANES)] * 2
            kept, sent = call(halving_kernel, "halving", shapes, kept, came)
            came = swapped(sent, "space", size)

    sums = call(
        functools.partial(pair_kernel, weights, instances),
        "pair_sums",
        [state.shape] * (instances // 2 - 1),
        state,
        partner,
        flops=PLACING,
    )
    sums = [swapped(value, "inst", i + 1) for i, value in enumerate(sums)]

    residual, total = call(
        functools.partial(outer_kernel, weights[instances // 2]),
        "outer",
        [state.shape, (ROWS, LANES)],
        state,
        base,
        kept,
        came,
        partner,
        *edges,
    )
    increment, blade = call(
        update_kernel,
        "update",
        [state.shape, (3, 1, node_block)],
        residual,
        step,
        total,
        *sums,
    )
    return increment, jnp.transpose(blade, (1, 0, 2))


def solution(mesh):
    in_specs = (P("inst", None, None, "space"), P("space"), P("space"), P(None, "space"))
    out_specs = (P("inst", None, None, "space"), P("inst", None, "space"))
    return jax.shard_map(
        functools.partial(per_device, 512),
        mesh=mesh,
        in_specs=in_specs,
        out_specs=out_specs,
        check_vma=False,
    )
```

```python
import functools
import math

import jax
import jax.numpy as jnp
import numpy as np
from jax import lax
from jax.experimental import pallas as pl
from jax.experimental.pallas import tpu as pltpu
from jax.sharding import PartitionSpec as P

gamma_ratio = 1.4
omega_rate = 0.5
cfl_number = 0.8

LANES = 128
ROWS = 16
EDGE = 12
PLACING = 10**10
RIDING = 8


def spectral_row(count):
    row = np.zeros((count,), np.float32)
    for shift in range(count):
        row[shift] = (-1.0) ** shift / count
        if shift != 0:
            row[shift] += 0.5 * (-1.0) ** shift / math.tan(math.pi * shift / count)
    return [float(omega_rate * value) for value in row]


def pressure_of(q0, q1, q2, q3):
    inverse = 1.0 / q0
    vr = q1 * inverse
    vc = q2 * inverse
    p = (gamma_ratio - 1.0) * (q3 - 0.5 * q0 * (vr * vr + vc * vc))
    return inverse, vr, vc, p


def own_kernel(high, riding, out):
    me = lax.axis_index("space")
    out[...] = jnp.full(out.shape, (me - me % 2 if riding else me) * high, jnp.int32)


def forces_kernel(node_block, riding, own, state, cell, node, area, *outs):
    radial, around = state.shape[2:]
    faces = cell.shape[0] * LANES
    chunks = faces // LANES
    _, _, _, p = pressure_of(state[0, 0], state[0, 1], state[0, 2], state[0, 3])
    sublane = lax.broadcasted_iota(jnp.int32, (8, LANES), 0)
    picked = []
    for c in range(chunks):
        index = jnp.broadcast_to(cell[c : c + 1, :], (8, LANES))
        row = index // around
        column = index % around
        lane = column % LANES
        half = column // LANES
        total = jnp.zeros((8, LANES), jnp.float32)
        for r in range(radial // 8):
            for h in range(around // LANES):
                part = p[r * 8 : (r + 1) * 8, h * LANES : (h + 1) * LANES]
                value = jnp.take_along_axis(part, lane, axis=1, mode="promise_in_bounds")
                total += jnp.where((row == sublane + r * 8) & (half == h), value, 0.0)
        picked.append(jnp.sum(total, axis=0, keepdims=True))
    face_pressure = jnp.concatenate(picked, axis=1)
    contribution = face_pressure * area[...]
    nodes = jnp.concatenate([node[c : c + 1, :] for c in range(chunks)], axis=1)

    high = node_block // LANES
    place = nodes // LANES ^ jnp.broadcast_to(own[0:1, 0:1], nodes.shape)
    low = nodes % LANES
    pick_low = (
        lax.broadcasted_iota(jnp.int32, (LANES, faces), 0) == jnp.broadcast_to(low, (LANES, faces))
    ).astype(jnp.float32).astype(jnp.bfloat16)
    pattern = jnp.concatenate(
        [jnp.broadcast_to(contribution[k : k + 1], (high, faces)) for k in range(3)]
        + [jnp.zeros((ROWS - 3 * high, faces), jnp.float32)],
        axis=0,
    )
    first = pattern.astype(jnp.bfloat16).astype(jnp.float32)
    second = pattern - first
    place = jnp.broadcast_to(place, (ROWS, faces))
    row_high = lax.broadcasted_iota(jnp.int32, (ROWS, faces), 0) % high

    def dense(start, count):
        masks = [place == row_high + (start + b) * high for b in range(count)]
        result = None
        for part in (first, second):
            left = jnp.concatenate([jnp.where(m, part, 0.0) for m in masks], axis=0)
            product = lax.dot_general(
                left.astype(jnp.bfloat16),
                pick_low,
                (((1,), (1,)), ((), ())),
                preferred_element_type=jnp.float32,
            )
            result = product if result is None else result + product
        return result.reshape(count, ROWS, LANES)

    size = outs[0].shape[0]
    blocks = size * len(outs)
    if blocks <= 16:
        result = dense(0, blocks)
        for i, out in enumerate(outs):
            out[...] = result[i * size : (i + 1) * size]
    else:
        for i, out in enumerate(outs):

            @pl.loop(0, size // 8)
            def _(g):
                out[pl.ds(g * 8, 8)] = dense(i * size + g * 8, 8)

    flat = state[0].reshape(4 * radial, around)
    turned = jnp.concatenate([flat[:, around - LANES :], flat[:, :LANES]], axis=0).T
    lane = lax.broadcasted_iota(jnp.int32, (1, LANES), 1)
    edge = jnp.where(lane < LANES // 2, turned[LANES - 1 :, :], turned[:1, :])
    if riding:
        core = lax.axis_index("space") % 2
        row = lax.broadcasted_iota(jnp.int32, (2, LANES), 0)
        outs[0][0, EDGE : EDGE + 2, :] = jnp.where(row == core, edge, 0.0)
    else:
        outs[0][0, EDGE : EDGE + 1, :] = edge


def chip_kernel(blocks, came, _, *outs):
    edges = blocks[0, EDGE:, :] + came[0, EDGE:, :]
    for out, pair in zip(outs, (0, 3, 2, 1)):
        for b in range(2):
            out[b] = blocks[2 * pair + b] + came[2 * pair + b]
        out[0, EDGE:, :] = edges


def plane_kernel(own, diagonal, y, x, *outs):
    chips = (own, x, y, diagonal)
    me = lax.axis_index("space")
    first = me - me % 2
    lane = lax.broadcasted_iota(jnp.int32, (1, LANES), 1)
    for core, out in enumerate(outs):
        out[...] = functools.reduce(jnp.add, [ref[core] for ref in chips])
        device = first + core
        around = (device + (RIDING - 1 if core == 0 else 1)) % RIDING
        place = (around ^ first) // 2
        there = own[0, EDGE + 1 - core : EDGE + 2 - core, :]
        for i, ref in enumerate(chips[1:], 1):
            row = ref[0, EDGE + 1 - core : EDGE + 2 - core, :]
            there = jnp.where(place == i, row, there)
        here = own[0, EDGE + 1 - core : EDGE + 2 - core, :]
        before, after = (there, here) if core == 0 else (here, there)
        out[EDGE : EDGE + 1, :] = jnp.where(lane < LANES // 2, before, after)


def halving_kernel(kept, came, *outs):
    size = outs[0].shape[0]
    for i, out in enumerate(outs):
        for b in range(size):
            out[b] = kept[i * size + b] + came[i * size + b]


def pair_kernel(weights, instances, state, partner, *outs):
    me = lax.axis_index("inst")

    def weight(shift):
        value = weights[0]
        for i in range(1, instances):
            value = jnp.where(shift == i, weights[i], value)
        return value

    for i, out in enumerate(outs):
        shift = ((me ^ (i + 1)) - me + instances) % instances
        far = (shift + instances // 2) % instances
        out[...] = weight(shift) * state[...] + weight(far) * partner[...]


def around_flux(q, vc, p):
    return (q[2], q[1] * vc, q[2] * vc + p, (q[3] + p) * vc)


def flux_kernel(weight, instances, state, base, step):
    radial, around = state.shape[2:]
    q = [state[0, c] for c in range(4)]
    inverse, vr, vc, p = pressure_of(*q)
    a = jnp.sqrt(gamma_ratio * p * inverse)
    step[...] = cfl_number / (
        jnp.abs(vr) + jnp.abs(vc) + 2.0 * a + omega_rate * instances / 2.0
    )

    def after(x):
        return pltpu.roll(x, around - 1, 1)

    def above(x):
        return pltpu.roll(x, radial - 1, 0)

    column = lax.broadcasted_iota(jnp.int32, (radial, around), 1)
    row = lax.broadcasted_iota(jnp.int32, (radial, around), 0)
    hub, tip = row == 0, row == radial - 1
    speed = jnp.abs(vc) + a
    reach = 0.5 * jnp.maximum(speed, after(speed))
    speed = jnp.abs(vr) + a
    rise = 0.5 * jnp.maximum(speed, above(speed))
    flux = around_flux(q, vc, p)
    radial_flux = (q[1], q[1] * vr + p, q[2] * vr, (q[3] + p) * vr)
    for c in range(4):
        face = 0.5 * (flux[c] + after(flux[c])) - reach * (after(q[c]) - q[c])
        face = jnp.where(column == around - 1, 0.0, face)
        residual = weight * q[c] + (face - pltpu.roll(face, 1, 1))
        wall = p if c == 1 else 0.0
        face = 0.5 * (radial_flux[c] + above(radial_flux[c])) - rise * (above(q[c]) - q[c])
        upper = jnp.where(tip, wall, face)
        lower = jnp.where(hub, wall, pltpu.roll(face, 1, 0))
        base[0, c] = residual + (upper - lower)


def outer_kernel(weight, state, base, kept, came, partner, *refs):
    *edges, residual, total = refs
    radial, around = state.shape[2:]
    if edges:
        before, after = (ref[0:1, :] for ref in edges)
        lane = lax.broadcasted_iota(jnp.int32, (1, LANES), 1)
        edge = jnp.where(lane < LANES // 2, before, after)
        total[...] = kept[0] + came[0]
    else:
        held = jnp.where(lax.axis_index("space") % 2 == 1, kept[...], came[...])
        edge = held[EDGE : EDGE + 1, :]
        total[...] = held
    columns = jnp.broadcast_to(edge, (LANES, LANES)).T

    lane = lax.broadcasted_iota(jnp.int32, (radial, LANES), 1)
    first, last = lane == 0, lane == LANES - 1
    own, far = [], []
    for c in range(4):
        own.append(jnp.where(first, state[0, c, :, :LANES], state[0, c, :, around - LANES :]))
        far.append(
            jnp.where(
                last,
                columns[LANES // 2 + c * radial : LANES // 2 + (c + 1) * radial],
                columns[c * radial : (c + 1) * radial],
            )
        )
    faces, speeds = [], []
    for q in (own, far):
        inverse, _, vc, p = pressure_of(*q)
        speeds.append(jnp.abs(vc) + jnp.sqrt(gamma_ratio * p * inverse))
        faces.append(around_flux(q, vc, p))
    side = jnp.where(last, 0.5, -0.5)
    reach = 0.5 * jnp.maximum(*speeds)
    for c in range(4):
        outer = side * (faces[0][c] + faces[1][c]) - reach * (far[c] - own[c])
        outer = [jnp.where(first, outer, 0.0), jnp.where(last, outer, 0.0)]
        middle = around - 2 * LANES
        if middle:
            outer.insert(1, jnp.zeros((radial, middle), jnp.float32))
        residual[0, c] = base[0, c] + weight * partner[0, c] + jnp.concatenate(outer, axis=1)


def update_kernel(residual, step, total, *refs):
    *sums, increment, blade = refs
    high = blade.shape[2] // LANES
    for k in range(3):
        for h in range(high):
            blade[k, :, pl.ds(h * LANES, LANES)] = total[k * high + h : k * high + h + 1, :]
    for c in range(residual.shape[1]):
        change = functools.reduce(jnp.add, [ref[0, c] for ref in (residual, *sums)])
        increment[0, c] = -step[...] * change


def per_device(node_block, state, face_cell, face_node, face_area):
    blocks = lax.axis_size("space")
    instances = lax.axis_size("inst")
    radial, around = state.shape[2:]
    chunks = face_cell.shape[0] // LANES
    vmem = pl.BlockSpec(memory_space=pltpu.VMEM)
    params = pltpu.CompilerParams(vmem_limit_bytes=(4 if blocks <= 16 else 16) * 2**20)

    def swapped(value, axis, bit):
        return lax.ppermute(value, axis, [(i, i ^ bit) for i in range(lax.axis_size(axis))])

    def shifted(value, axis, s):
        count = lax.axis_size(axis)
        return lax.ppermute(value, axis, [(i, (i + s) % count) for i in range(count)])

    def swapped_by_second(value, bit):
        pairs = [(i, i ^ bit if i % 2 else i) for i in range(blocks)]
        return lax.ppermute(value, "space", pairs)

    def call(kernel, name, shapes, *operands, flops=0, dtype=jnp.float32):
        return pl.pallas_call(
            kernel,
            out_shape=[jax.ShapeDtypeStruct(shape, dtype) for shape in shapes],
            in_specs=[vmem] * len(operands),
            out_specs=[vmem] * len(shapes),
            compiler_params=params,
            cost_estimate=pl.CostEstimate(flops=flops, bytes_accessed=0, transcendentals=0),
            name=name,
        )(*operands)

    weights = spectral_row(instances)
    partner = shifted(state, "inst", instances // 2)

    riding = blocks == RIDING
    parts = 1 if riding else 2
    (own,) = call(
        functools.partial(own_kernel, node_block // LANES, riding),
        "own",
        [(8, LANES)],
        dtype=jnp.int32,
        flops=PLACING,
    )
    dense = call(
        functools.partial(forces_kernel, node_block, riding),
        "face_forces",
        [(blocks // parts, ROWS, LANES)] * parts,
        own,
        state,
        face_cell.reshape(chunks, LANES),
        face_node.reshape(chunks, LANES),
        face_area,
        flops=PLACING,
    )

    base, step = call(
        functools.partial(flux_kernel, weights[0], instances),
        "flux",
        [state.shape, (radial, around)],
        state,
        flops=PLACING,
    )
    edges = []
    if riding:
        came = swapped(dense[0], "space", 1)
        mine, *sent = call(chip_kernel, "chip_sums", [(2, ROWS, LANES)] * 4, dense[0], came, step)
        came = [swapped_by_second(value, bit) for value, bit in zip(sent, (6, 4, 2))]
        block, kept = call(
            plane_kernel, "plane_sums", [(ROWS, LANES)] * 2, mine, *came, flops=PLACING
        )
        came = swapped(block, "space", 1)
    else:
        row = jnp.broadcast_to(dense[0][0, EDGE : EDGE + 1, :], (8, LANES))
        edges = [shifted(row, "space", 1), shifted(row, "space", blocks - 1)]
        size = blocks // 2
        kept, came = dense[0], swapped(dense[1], "space", size)
        while size > 1:
            size //= 2
            shapes = [(size, ROWS, LANES)] * 2
            kept, sent = call(halving_kernel, "halving", shapes, kept, came)
            came = swapped(sent, "space", size)

    sums = call(
        functools.partial(pair_kernel, weights, instances),
        "pair_sums",
        [state.shape] * (instances // 2 - 1),
        state,
        partner,
        flops=PLACING,
    )
    sums = [swapped(value, "inst", i + 1) for i, value in enumerate(sums)]

    residual, total = call(
        functools.partial(outer_kernel, weights[instances // 2]),
        "outer",
        [state.shape, (ROWS, LANES)],
        state,
        base,
        kept,
        came,
        partner,
        *edges,
    )
    increment, blade = call(
        update_kernel,
        "update",
        [state.shape, (3, 1, node_block)],
        residual,
        step,
        total,
        *sums,
    )
    return increment, jnp.transpose(blade, (1, 0, 2))


def solution(mesh):
    in_specs = (P("inst", None, None, "space"), P("space"), P("space"), P(None, "space"))
    out_specs = (P("inst", None, None, "space"), P("inst", None, "space"))
    return jax.shard_map(
        functools.partial(per_device, 512),
        mesh=mesh,
        in_specs=in_specs,
        out_specs=out_specs,
        check_vma=False,
    )
```

```python
import functools
import math

import jax
import jax.numpy as jnp
import numpy as np
from jax import lax
from jax.experimental import pallas as pl
from jax.experimental.pallas import tpu as pltpu
from jax.sharding import PartitionSpec as P

gamma_ratio = 1.4
omega_rate = 0.5
cfl_number = 0.8

LANES = 128
ROWS = 16
EDGE = 12
PLACING = 10**10
PLACES = (2, 3, 1)
RIDING = 8


def spectral_row(count):
    row = np.zeros((count,), np.float32)
    for shift in range(count):
        row[shift] = (-1.0) ** shift / count
        if shift != 0:
            row[shift] += 0.5 * (-1.0) ** shift / math.tan(math.pi * shift / count)
    return [float(omega_rate * value) for value in row]


def pressure_of(q0, q1, q2, q3):
    inverse = 1.0 / q0
    vr = q1 * inverse
    vc = q2 * inverse
    p = (gamma_ratio - 1.0) * (q3 - 0.5 * q0 * (vr * vr + vc * vc))
    return inverse, vr, vc, p


def own_kernel(high, out):
    out[...] = jnp.full(out.shape, lax.axis_index("space") * high, jnp.int32)


def forces_kernel(node_block, own, state, cell, node, area, *outs):
    radial, around = state.shape[2:]
    faces = cell.shape[0] * LANES
    chunks = faces // LANES
    _, _, _, p = pressure_of(state[0, 0], state[0, 1], state[0, 2], state[0, 3])
    sublane = lax.broadcasted_iota(jnp.int32, (8, LANES), 0)
    picked = []
    for c in range(chunks):
        index = jnp.broadcast_to(cell[c : c + 1, :], (8, LANES))
        row = index // around
        column = index % around
        lane = column % LANES
        half = column // LANES
        total = jnp.zeros((8, LANES), jnp.float32)
        for r in range(radial // 8):
            for h in range(around // LANES):
                part = p[r * 8 : (r + 1) * 8, h * LANES : (h + 1) * LANES]
                value = jnp.take_along_axis(part, lane, axis=1, mode="promise_in_bounds")
                total += jnp.where((row == sublane + r * 8) & (half == h), value, 0.0)
        picked.append(jnp.sum(total, axis=0, keepdims=True))
    face_pressure = jnp.concatenate(picked, axis=1)
    contribution = face_pressure * area[...]
    nodes = jnp.concatenate([node[c : c + 1, :] for c in range(chunks)], axis=1)

    high = node_block // LANES
    place = nodes // LANES ^ jnp.broadcast_to(own[0:1, 0:1], nodes.shape)
    low = nodes % LANES
    pick_low = (
        lax.broadcasted_iota(jnp.int32, (LANES, faces), 0) == jnp.broadcast_to(low, (LANES, faces))
    ).astype(jnp.float32).astype(jnp.bfloat16)
    pattern = jnp.concatenate(
        [jnp.broadcast_to(contribution[k : k + 1], (high, faces)) for k in range(3)]
        + [jnp.zeros((ROWS - 3 * high, faces), jnp.float32)],
        axis=0,
    )
    first = pattern.astype(jnp.bfloat16).astype(jnp.float32)
    second = pattern - first
    place = jnp.broadcast_to(place, (ROWS, faces))
    row_high = lax.broadcasted_iota(jnp.int32, (ROWS, faces), 0) % high

    def dense(start, count):
        masks = [place == row_high + (start + b) * high for b in range(count)]
        result = None
        for part in (first, second):
            left = jnp.concatenate([jnp.where(m, part, 0.0) for m in masks], axis=0)
            product = lax.dot_general(
                left.astype(jnp.bfloat16),
                pick_low,
                (((1,), (1,)), ((), ())),
                preferred_element_type=jnp.float32,
            )
            result = product if result is None else result + product
        return result.reshape(count, ROWS, LANES)

    places = (0, *PLACES) if len(outs) == 4 else (0, 1)
    ordered = [outs[places.index(i)] for i in range(len(outs))]
    size = outs[0].shape[0]
    blocks = size * len(outs)
    if blocks <= 16:
        result = dense(0, blocks)
        for i, out in enumerate(ordered):
            out[...] = result[i * size : (i + 1) * size]
    else:
        for i, out in enumerate(ordered):

            @pl.loop(0, size // 8)
            def _(g):
                out[pl.ds(g * 8, 8)] = dense(i * size + g * 8, 8)

    flat = state[0].reshape(4 * radial, around)
    turned = jnp.concatenate([flat[:, around - LANES :], flat[:, :LANES]], axis=0).T
    lane = lax.broadcasted_iota(jnp.int32, (1, LANES), 1)
    edge = jnp.where(lane < LANES // 2, turned[LANES - 1 :, :], turned[:1, :])
    for out in outs:
        out[0, EDGE : EDGE + 1, :] = edge


def halving_kernel(arrived, riding, *refs):
    outs = refs[arrived:]
    size = outs[0].shape[0]
    for i, out in enumerate(outs):
        for b in range(size):
            out[b] = functools.reduce(jnp.add, [ref[i * size + b] for ref in refs[:arrived]])
        if riding:
            for j, ref in enumerate(refs[:arrived]):
                out[0, EDGE + j : EDGE + j + 1, :] = ref[0, EDGE : EDGE + 1, :]


def weight_from(weights, instances, source, target):
    shift = (target - source + instances) % instances
    value = weights[0]
    for i in range(1, instances):
        value = jnp.where(shift == i, weights[i], value)
    return value


def pair_kernel(weights, instances, first, seconds, state, partner, *outs):
    me = lax.axis_index("inst")
    for second, out in zip(seconds, outs):
        own = weight_from(weights, instances, me, me ^ second)
        other = weight_from(weights, instances, me ^ first, me ^ second)
        out[...] = own * state[...] + other * partner[...]


def around_flux(q, vc, p):
    return (q[2], q[1] * vc, q[2] * vc + p, (q[3] + p) * vc)


def flux_kernel(weight, instances, state, base, step):
    radial, around = state.shape[2:]
    q = [state[0, c] for c in range(4)]
    inverse, vr, vc, p = pressure_of(*q)
    a = jnp.sqrt(gamma_ratio * p * inverse)
    step[...] = cfl_number / (
        jnp.abs(vr) + jnp.abs(vc) + 2.0 * a + omega_rate * instances / 2.0
    )

    def after(x):
        return pltpu.roll(x, around - 1, 1)

    def above(x):
        return pltpu.roll(x, radial - 1, 0)

    column = lax.broadcasted_iota(jnp.int32, (radial, around), 1)
    row = lax.broadcasted_iota(jnp.int32, (radial, around), 0)
    hub, tip = row == 0, row == radial - 1
    speed = jnp.abs(vc) + a
    reach = 0.5 * jnp.maximum(speed, after(speed))
    speed = jnp.abs(vr) + a
    rise = 0.5 * jnp.maximum(speed, above(speed))
    flux = around_flux(q, vc, p)
    radial_flux = (q[1], q[1] * vr + p, q[2] * vr, (q[3] + p) * vr)
    for c in range(4):
        face = 0.5 * (flux[c] + after(flux[c])) - reach * (after(q[c]) - q[c])
        face = jnp.where(column == around - 1, 0.0, face)
        residual = weight * q[c] + (face - pltpu.roll(face, 1, 1))
        wall = p if c == 1 else 0.0
        face = 0.5 * (radial_flux[c] + above(radial_flux[c])) - rise * (above(q[c]) - q[c])
        upper = jnp.where(tip, wall, face)
        lower = jnp.where(hub, wall, pltpu.roll(face, 1, 0))
        base[0, c] = residual + (upper - lower)


def outer_kernel(weights, instances, first, blocks, state, base, kept, came, partner, *refs):
    *edges, residual, total = refs
    radial, around = state.shape[2:]
    if blocks == RIDING:
        me = lax.axis_index("space")
        known = [kept[0, EDGE:, :], came[0, EDGE:, :]]
        known = jnp.concatenate(known, axis=0)
        row = lax.broadcasted_iota(jnp.int32, known.shape, 0)

        def edge_of(device):
            relative = device ^ me
            half = RIDING // 2
            place = 0
            for row_place, chip in enumerate(PLACES, 1):
                place = jnp.where(relative // 2 == chip, row_place, place)
            place += (relative % 2) * half
            return jnp.sum(jnp.where(row == place, known, 0.0), axis=0, keepdims=True)

        before = edge_of((me + blocks - 1) % blocks)
        after = edge_of((me + 1) % blocks)
    else:
        before, after = (ref[0:1, :] for ref in edges)
    me = lax.axis_index("inst")
    weight = weight_from(weights, instances, me ^ first, me)
    lane = lax.broadcasted_iota(jnp.int32, (1, LANES), 1)
    edge = jnp.where(lane < LANES // 2, before, after)
    columns = jnp.broadcast_to(edge, (LANES, LANES)).T

    lane = lax.broadcasted_iota(jnp.int32, (radial, LANES), 1)
    left, right = lane == 0, lane == LANES - 1
    own, far = [], []
    for c in range(4):
        own.append(jnp.where(left, state[0, c, :, :LANES], state[0, c, :, around - LANES :]))
        far.append(
            jnp.where(
                right,
                columns[LANES // 2 + c * radial : LANES // 2 + (c + 1) * radial],
                columns[c * radial : (c + 1) * radial],
            )
        )
    faces, speeds = [], []
    for q in (own, far):
        inverse, _, vc, p = pressure_of(*q)
        speeds.append(jnp.abs(vc) + jnp.sqrt(gamma_ratio * p * inverse))
        faces.append(around_flux(q, vc, p))
    side = jnp.where(right, 0.5, -0.5)
    reach = 0.5 * jnp.maximum(*speeds)
    for c in range(4):
        outer = side * (faces[0][c] + faces[1][c]) - reach * (far[c] - own[c])
        outer = [jnp.where(left, outer, 0.0), jnp.where(right, outer, 0.0)]
        middle = around - 2 * LANES
        if middle:
            outer.insert(1, jnp.zeros((radial, middle), jnp.float32))
        residual[0, c] = base[0, c] + weight * partner[0, c] + jnp.concatenate(outer, axis=1)

    total[...] = kept[0] + came[0]


def update_kernel(residual, step, total, *refs):
    *sums, increment, blade = refs
    high = blade.shape[2] // LANES
    for k in range(3):
        for h in range(high):
            blade[k, :, pl.ds(h * LANES, LANES)] = total[k * high + h : k * high + h + 1, :]
    for c in range(residual.shape[1]):
        change = functools.reduce(jnp.add, [ref[0, c] for ref in (residual, *sums)])
        increment[0, c] = -step[...] * change


def per_device(node_block, state, face_cell, face_node, face_area):
    blocks = lax.axis_size("space")
    instances = lax.axis_size("inst")
    radial, around = state.shape[2:]
    chunks = face_cell.shape[0] // LANES
    vmem = pl.BlockSpec(memory_space=pltpu.VMEM)
    params = pltpu.CompilerParams(vmem_limit_bytes=(4 if blocks <= 16 else 16) * 2**20)

    def swapped(value, axis, bit):
        return lax.ppermute(value, axis, [(i, i ^ bit) for i in range(lax.axis_size(axis))])

    def shifted(value, axis, s):
        count = lax.axis_size(axis)
        return lax.ppermute(value, axis, [(i, (i + s) % count) for i in range(count)])

    def exchanged(sent, size):
        places = PLACES if len(sent) == 3 else (1,)
        return [swapped(value, "space", place * size) for place, value in zip(places, sent)]

    def call(kernel, name, shapes, *operands, flops=0, dtype=jnp.float32):
        return pl.pallas_call(
            kernel,
            out_shape=[jax.ShapeDtypeStruct(shape, dtype) for shape in shapes],
            in_specs=[vmem] * len(operands),
            out_specs=[vmem] * len(shapes),
            compiler_params=params,
            cost_estimate=pl.CostEstimate(flops=flops, bytes_accessed=0, transcendentals=0),
            name=name,
        )(*operands)

    weights = spectral_row(instances)
    first, seconds = 1, range(2, instances, 2)
    partner = swapped(state, "inst", first)

    riding = blocks == RIDING
    steps = [4, 2] if riding else [2] * (blocks.bit_length() - 1)
    size = blocks // steps[0]
    (own,) = call(
        functools.partial(own_kernel, node_block // LANES),
        "own",
        [(8, LANES)],
        dtype=jnp.int32,
        flops=PLACING,
    )
    kept, *sent = call(
        functools.partial(forces_kernel, node_block),
        "face_forces",
        [(size, ROWS, LANES)] * steps[0],
        own,
        state,
        face_cell.reshape(chunks, LANES),
        face_node.reshape(chunks, LANES),
        face_area,
        flops=PLACING,
    )

    edges = []
    if not riding:
        row = jnp.broadcast_to(kept[0, EDGE : EDGE + 1, :], (8, LANES))
        edges = [shifted(row, "space", 1), shifted(row, "space", blocks - 1)]

    came = exchanged(sent, size)
    sums = call(
        functools.partial(pair_kernel, weights, instances, first, seconds),
        "pair_sums",
        [state.shape] * len(seconds),
        state,
        partner,
        flops=PLACING,
    )
    sums = [swapped(value, "inst", second) for second, value in zip(seconds, sums)]

    for step in steps[1:]:
        size //= step
        kept, *sent = call(
            functools.partial(halving_kernel, 1 + len(came), riding),
            "halving",
            [(size, ROWS, LANES)] * step,
            kept,
            *came,
            flops=PLACING,
        )
        came = exchanged(sent, size)

    base, step = call(
        functools.partial(flux_kernel, weights[0], instances),
        "flux",
        [state.shape, (radial, around)],
        state,
    )
    residual, total = call(
        functools.partial(outer_kernel, weights, instances, first, blocks),
        "outer",
        [state.shape, (ROWS, LANES)],
        state,
        base,
        kept,
        *came,
        partner,
        *edges,
    )
    increment, blade = call(
        update_kernel,
        "update",
        [state.shape, (3, 1, node_block)],
        residual,
        step,
        total,
        *sums,
    )
    return increment, jnp.transpose(blade, (1, 0, 2))


def solution(mesh):
    in_specs = (P("inst", None, None, "space"), P("space"), P("space"), P(None, "space"))
    out_specs = (P("inst", None, None, "space"), P("inst", None, "space"))
    return jax.shard_map(
        functools.partial(per_device, 512),
        mesh=mesh,
        in_specs=in_specs,
        out_specs=out_specs,
        check_vma=False,
    )
```

```python
import functools
import math

import jax
import jax.numpy as jnp
import numpy as np
from jax import lax
from jax.experimental import pallas as pl
from jax.experimental.pallas import tpu as pltpu
from jax.sharding import PartitionSpec as P

gamma_ratio = 1.4
omega_rate = 0.5
cfl_number = 0.8

LANES = 128
ROWS = 16
EDGE = 12
PLACING = 10**10
PLACES = (2, 3, 1)
ORDERS = ((1, 2), (2, 1))
RIDING = 8


def spectral_row(count):
    row = np.zeros((count,), np.float32)
    for shift in range(count):
        row[shift] = (-1.0) ** shift / count
        if shift != 0:
            row[shift] += 0.5 * (-1.0) ** shift / math.tan(math.pi * shift / count)
    return [float(omega_rate * value) for value in row]


def pressure_of(q0, q1, q2, q3):
    inverse = 1.0 / q0
    vr = q1 * inverse
    vc = q2 * inverse
    p = (gamma_ratio - 1.0) * (q3 - 0.5 * q0 * (vr * vr + vc * vc))
    return inverse, vr, vc, p


def own_kernel(high, out):
    out[...] = jnp.full(out.shape, lax.axis_index("space") * high, jnp.int32)


def forces_kernel(node_block, own, state, cell, node, area, *outs):
    radial, around = state.shape[2:]
    faces = cell.shape[0] * LANES
    chunks = faces // LANES
    _, _, _, p = pressure_of(state[0, 0], state[0, 1], state[0, 2], state[0, 3])
    sublane = lax.broadcasted_iota(jnp.int32, (8, LANES), 0)
    picked = []
    for c in range(chunks):
        index = jnp.broadcast_to(cell[c : c + 1, :], (8, LANES))
        row = index // around
        column = index % around
        lane = column % LANES
        half = column // LANES
        total = jnp.zeros((8, LANES), jnp.float32)
        for r in range(radial // 8):
            for h in range(around // LANES):
                part = p[r * 8 : (r + 1) * 8, h * LANES : (h + 1) * LANES]
                value = jnp.take_along_axis(part, lane, axis=1, mode="promise_in_bounds")
                total += jnp.where((row == sublane + r * 8) & (half == h), value, 0.0)
        picked.append(jnp.sum(total, axis=0, keepdims=True))
    face_pressure = jnp.concatenate(picked, axis=1)
    contribution = face_pressure * area[...]
    nodes = jnp.concatenate([node[c : c + 1, :] for c in range(chunks)], axis=1)

    high = node_block // LANES
    place = nodes // LANES ^ jnp.broadcast_to(own[0:1, 0:1], nodes.shape)
    low = nodes % LANES
    pick_low = (
        lax.broadcasted_iota(jnp.int32, (LANES, faces), 0) == jnp.broadcast_to(low, (LANES, faces))
    ).astype(jnp.float32).astype(jnp.bfloat16)
    pattern = jnp.concatenate(
        [jnp.broadcast_to(contribution[k : k + 1], (high, faces)) for k in range(3)]
        + [jnp.zeros((ROWS - 3 * high, faces), jnp.float32)],
        axis=0,
    )
    first = pattern.astype(jnp.bfloat16).astype(jnp.float32)
    second = pattern - first
    place = jnp.broadcast_to(place, (ROWS, faces))
    row_high = lax.broadcasted_iota(jnp.int32, (ROWS, faces), 0) % high

    def dense(start, count):
        masks = [place == row_high + (start + b) * high for b in range(count)]
        result = None
        for part in (first, second):
            left = jnp.concatenate([jnp.where(m, part, 0.0) for m in masks], axis=0)
            product = lax.dot_general(
                left.astype(jnp.bfloat16),
                pick_low,
                (((1,), (1,)), ((), ())),
                preferred_element_type=jnp.float32,
            )
            result = product if result is None else result + product
        return result.reshape(count, ROWS, LANES)

    places = (0, *PLACES) if len(outs) == 4 else (0, 1)
    ordered = [outs[places.index(i)] for i in range(len(outs))]
    size = outs[0].shape[0]
    blocks = size * len(outs)
    if blocks <= 16:
        result = dense(0, blocks)
        for i, out in enumerate(ordered):
            out[...] = result[i * size : (i + 1) * size]
    else:
        for i, out in enumerate(ordered):

            @pl.loop(0, size // 8)
            def _(g):
                out[pl.ds(g * 8, 8)] = dense(i * size + g * 8, 8)

    flat = state[0].reshape(4 * radial, around)
    turned = jnp.concatenate([flat[:, around - LANES :], flat[:, :LANES]], axis=0).T
    lane = lax.broadcasted_iota(jnp.int32, (1, LANES), 1)
    edge = jnp.where(lane < LANES // 2, turned[LANES - 1 :, :], turned[:1, :])
    for out in outs:
        out[0, EDGE : EDGE + 1, :] = edge


def halving_kernel(arrived, riding, *refs):
    outs = refs[arrived:]
    size = outs[0].shape[0]
    for i, out in enumerate(outs):
        for b in range(size):
            out[b] = functools.reduce(jnp.add, [ref[i * size + b] for ref in refs[:arrived]])
        if riding:
            for j, ref in enumerate(refs[:arrived]):
                out[0, EDGE + j : EDGE + j + 1, :] = ref[0, EDGE : EDGE + 1, :]


def weight_from(weights, instances, source, target):
    shift = (target - source + instances) % instances
    value = weights[0]
    for i in range(1, instances):
        value = jnp.where(shift == i, weights[i], value)
    return value


def of_core(orders):
    odd = lax.axis_index("space") % 2
    return [jnp.where(odd == 1, b, a) for a, b in zip(*orders)]


def pair_kernel(weights, instances, orders, state, partner, *outs):
    me = lax.axis_index("inst")
    first, *seconds = of_core(orders)
    for second, out in zip(seconds, outs):
        own = weight_from(weights, instances, me, me ^ second)
        other = weight_from(weights, instances, me ^ first, me ^ second)
        out[...] = own * state[...] + other * partner[...]


def around_flux(q, vc, p):
    return (q[2], q[1] * vc, q[2] * vc + p, (q[3] + p) * vc)


def flux_kernel(weight, instances, state, base, step):
    radial, around = state.shape[2:]
    q = [state[0, c] for c in range(4)]
    inverse, vr, vc, p = pressure_of(*q)
    a = jnp.sqrt(gamma_ratio * p * inverse)
    step[...] = cfl_number / (
        jnp.abs(vr) + jnp.abs(vc) + 2.0 * a + omega_rate * instances / 2.0
    )

    def after(x):
        return pltpu.roll(x, around - 1, 1)

    def above(x):
        return pltpu.roll(x, radial - 1, 0)

    column = lax.broadcasted_iota(jnp.int32, (radial, around), 1)
    row = lax.broadcasted_iota(jnp.int32, (radial, around), 0)
    hub, tip = row == 0, row == radial - 1
    speed = jnp.abs(vc) + a
    reach = 0.5 * jnp.maximum(speed, after(speed))
    speed = jnp.abs(vr) + a
    rise = 0.5 * jnp.maximum(speed, above(speed))
    flux = around_flux(q, vc, p)
    radial_flux = (q[1], q[1] * vr + p, q[2] * vr, (q[3] + p) * vr)
    for c in range(4):
        face = 0.5 * (flux[c] + after(flux[c])) - reach * (after(q[c]) - q[c])
        face = jnp.where(column == around - 1, 0.0, face)
        residual = weight * q[c] + (face - pltpu.roll(face, 1, 1))
        wall = p if c == 1 else 0.0
        face = 0.5 * (radial_flux[c] + above(radial_flux[c])) - rise * (above(q[c]) - q[c])
        upper = jnp.where(tip, wall, face)
        lower = jnp.where(hub, wall, pltpu.roll(face, 1, 0))
        base[0, c] = residual + (upper - lower)


def outer_kernel(weights, instances, orders, blocks, state, base, kept, came, partner, *refs):
    *edges, residual, total = refs
    radial, around = state.shape[2:]
    if blocks == RIDING:
        me = lax.axis_index("space")
        known = [kept[0, EDGE:, :], came[0, EDGE:, :]]
        known = jnp.concatenate(known, axis=0)
        row = lax.broadcasted_iota(jnp.int32, known.shape, 0)

        def edge_of(device):
            relative = device ^ me
            half = RIDING // 2
            place = 0
            for row_place, chip in enumerate(PLACES, 1):
                place = jnp.where(relative // 2 == chip, row_place, place)
            place += (relative % 2) * half
            return jnp.sum(jnp.where(row == place, known, 0.0), axis=0, keepdims=True)

        before = edge_of((me + blocks - 1) % blocks)
        after = edge_of((me + 1) % blocks)
    else:
        before, after = (ref[0:1, :] for ref in edges)
    me = lax.axis_index("inst")
    weight = weight_from(weights, instances, me ^ of_core(orders)[0], me)
    lane = lax.broadcasted_iota(jnp.int32, (1, LANES), 1)
    edge = jnp.where(lane < LANES // 2, before, after)
    columns = jnp.broadcast_to(edge, (LANES, LANES)).T

    lane = lax.broadcasted_iota(jnp.int32, (radial, LANES), 1)
    left, right = lane == 0, lane == LANES - 1
    own, far = [], []
    for c in range(4):
        own.append(jnp.where(left, state[0, c, :, :LANES], state[0, c, :, around - LANES :]))
        far.append(
            jnp.where(
                right,
                columns[LANES // 2 + c * radial : LANES // 2 + (c + 1) * radial],
                columns[c * radial : (c + 1) * radial],
            )
        )
    faces, speeds = [], []
    for q in (own, far):
        inverse, _, vc, p = pressure_of(*q)
        speeds.append(jnp.abs(vc) + jnp.sqrt(gamma_ratio * p * inverse))
        faces.append(around_flux(q, vc, p))
    side = jnp.where(right, 0.5, -0.5)
    reach = 0.5 * jnp.maximum(*speeds)
    for c in range(4):
        outer = side * (faces[0][c] + faces[1][c]) - reach * (far[c] - own[c])
        outer = [jnp.where(left, outer, 0.0), jnp.where(right, outer, 0.0)]
        middle = around - 2 * LANES
        if middle:
            outer.insert(1, jnp.zeros((radial, middle), jnp.float32))
        residual[0, c] = base[0, c] + weight * partner[0, c] + jnp.concatenate(outer, axis=1)

    total[...] = kept[0] + came[0]


def update_kernel(residual, step, total, *refs):
    *sums, increment, blade = refs
    high = blade.shape[2] // LANES
    for k in range(3):
        for h in range(high):
            blade[k, :, pl.ds(h * LANES, LANES)] = total[k * high + h : k * high + h + 1, :]
    for c in range(residual.shape[1]):
        change = functools.reduce(jnp.add, [ref[0, c] for ref in (residual, *sums)])
        increment[0, c] = -step[...] * change


def per_device(node_block, state, face_cell, face_node, face_area):
    blocks = lax.axis_size("space")
    instances = lax.axis_size("inst")
    radial, around = state.shape[2:]
    chunks = face_cell.shape[0] // LANES
    vmem = pl.BlockSpec(memory_space=pltpu.VMEM)
    params = pltpu.CompilerParams(vmem_limit_bytes=(4 if blocks <= 16 else 16) * 2**20)

    def swapped(value, axis, bit):
        return lax.ppermute(value, axis, [(i, i ^ bit) for i in range(lax.axis_size(axis))])

    def shifted(value, axis, s):
        count = lax.axis_size(axis)
        return lax.ppermute(value, axis, [(i, (i + s) % count) for i in range(count)])

    def exchanged(sent, size):
        places = PLACES if len(sent) == 3 else (1,)
        return [swapped(value, "space", place * size) for place, value in zip(places, sent)]

    def call(kernel, name, shapes, *operands, flops=0, dtype=jnp.float32):
        return pl.pallas_call(
            kernel,
            out_shape=[jax.ShapeDtypeStruct(shape, dtype) for shape in shapes],
            in_specs=[vmem] * len(operands),
            out_specs=[vmem] * len(shapes),
            compiler_params=params,
            cost_estimate=pl.CostEstimate(flops=flops, bytes_accessed=0, transcendentals=0),
            name=name,
        )(*operands)

    weights = spectral_row(instances)
    def partnered(value, place):
        pairs = [
            (i * instances + n, i * instances + (n ^ orders[i % 2][place]))
            for i in range(blocks)
            for n in range(instances)
        ]
        return lax.ppermute(value, ("space", "inst"), pairs)

    orders = ORDERS if instances == 4 else ((1, *range(2, instances, 2)),) * 2
    partner = partnered(state, 0)

    riding = blocks == RIDING
    steps = [4, 2] if riding else [2] * (blocks.bit_length() - 1)
    size = blocks // steps[0]
    (own,) = call(
        functools.partial(own_kernel, node_block // LANES),
        "own",
        [(8, LANES)],
        dtype=jnp.int32,
        flops=PLACING,
    )
    kept, *sent = call(
        functools.partial(forces_kernel, node_block),
        "face_forces",
        [(size, ROWS, LANES)] * steps[0],
        own,
        state,
        face_cell.reshape(chunks, LANES),
        face_node.reshape(chunks, LANES),
        face_area,
        flops=PLACING,
    )

    edges = []
    if not riding:
        row = jnp.broadcast_to(kept[0, EDGE : EDGE + 1, :], (8, LANES))
        edges = [shifted(row, "space", 1), shifted(row, "space", blocks - 1)]

    came = exchanged(sent, size)
    sums = call(
        functools.partial(pair_kernel, weights, instances, orders),
        "pair_sums",
        [state.shape] * (len(orders[0]) - 1),
        state,
        partner,
        flops=PLACING,
    )
    sums = [partnered(value, i) for i, value in enumerate(sums, 1)]

    for step in steps[1:]:
        size //= step
        kept, *sent = call(
            functools.partial(halving_kernel, 1 + len(came), riding),
            "halving",
            [(size, ROWS, LANES)] * step,
            kept,
            *came,
            flops=PLACING,
        )
        came = exchanged(sent, size)

    base, step = call(
        functools.partial(flux_kernel, weights[0], instances),
        "flux",
        [state.shape, (radial, around)],
        state,
    )
    residual, total = call(
        functools.partial(outer_kernel, weights, instances, orders, blocks),
        "outer",
        [state.shape, (ROWS, LANES)],
        state,
        base,
        kept,
        *came,
        partner,
        *edges,
    )
    increment, blade = call(
        update_kernel,
        "update",
        [state.shape, (3, 1, node_block)],
        residual,
        step,
        total,
        *sums,
    )
    return increment, jnp.transpose(blade, (1, 0, 2))


def solution(mesh):
    in_specs = (P("inst", None, None, "space"), P("space"), P("space"), P(None, "space"))
    out_specs = (P("inst", None, None, "space"), P("inst", None, "space"))
    return jax.shard_map(
        functools.partial(per_device, 512),
        mesh=mesh,
        in_specs=in_specs,
        out_specs=out_specs,
        check_vma=False,
    )
```

```python
import functools
import math

import jax
import jax.numpy as jnp
import numpy as np
from jax import lax
from jax.experimental import pallas as pl
from jax.experimental.pallas import tpu as pltpu
from jax.sharding import PartitionSpec as P

gamma_ratio = 1.4
omega_rate = 0.5
cfl_number = 0.8

LANES = 128
ROWS = 16
EDGE = 12
PLACING = 10**10
PLACES = (2, 3, 1)
PARTS = 2
RIDING = 8


def spectral_row(count):
    row = np.zeros((count,), np.float32)
    for shift in range(count):
        row[shift] = (-1.0) ** shift / count
        if shift != 0:
            row[shift] += 0.5 * (-1.0) ** shift / math.tan(math.pi * shift / count)
    return [float(omega_rate * value) for value in row]


def pressure_of(q0, q1, q2, q3):
    inverse = 1.0 / q0
    vr = q1 * inverse
    vc = q2 * inverse
    p = (gamma_ratio - 1.0) * (q3 - 0.5 * q0 * (vr * vr + vc * vc))
    return inverse, vr, vc, p


def own_kernel(high, out):
    out[...] = jnp.full(out.shape, lax.axis_index("space") * high, jnp.int32)


def forces_kernel(node_block, own, state, cell, node, area, *outs):
    radial, around = state.shape[2:]
    faces = cell.shape[0] * LANES
    chunks = faces // LANES
    _, _, _, p = pressure_of(state[0, 0], state[0, 1], state[0, 2], state[0, 3])
    sublane = lax.broadcasted_iota(jnp.int32, (8, LANES), 0)
    picked = []
    for c in range(chunks):
        index = jnp.broadcast_to(cell[c : c + 1, :], (8, LANES))
        row = index // around
        column = index % around
        lane = column % LANES
        half = column // LANES
        total = jnp.zeros((8, LANES), jnp.float32)
        for r in range(radial // 8):
            for h in range(around // LANES):
                part = p[r * 8 : (r + 1) * 8, h * LANES : (h + 1) * LANES]
                value = jnp.take_along_axis(part, lane, axis=1, mode="promise_in_bounds")
                total += jnp.where((row == sublane + r * 8) & (half == h), value, 0.0)
        picked.append(jnp.sum(total, axis=0, keepdims=True))
    face_pressure = jnp.concatenate(picked, axis=1)
    contribution = face_pressure * area[...]
    nodes = jnp.concatenate([node[c : c + 1, :] for c in range(chunks)], axis=1)

    high = node_block // LANES
    place = nodes // LANES ^ jnp.broadcast_to(own[0:1, 0:1], nodes.shape)
    low = nodes % LANES
    pick_low = (
        lax.broadcasted_iota(jnp.int32, (LANES, faces), 0) == jnp.broadcast_to(low, (LANES, faces))
    ).astype(jnp.float32).astype(jnp.bfloat16)
    pattern = jnp.concatenate(
        [jnp.broadcast_to(contribution[k : k + 1], (high, faces)) for k in range(3)]
        + [jnp.zeros((ROWS - 3 * high, faces), jnp.float32)],
        axis=0,
    )
    first = pattern.astype(jnp.bfloat16).astype(jnp.float32)
    second = pattern - first
    place = jnp.broadcast_to(place, (ROWS, faces))
    row_high = lax.broadcasted_iota(jnp.int32, (ROWS, faces), 0) % high

    def dense(start, count):
        masks = [place == row_high + (start + b) * high for b in range(count)]
        result = None
        for part in (first, second):
            left = jnp.concatenate([jnp.where(m, part, 0.0) for m in masks], axis=0)
            product = lax.dot_general(
                left.astype(jnp.bfloat16),
                pick_low,
                (((1,), (1,)), ((), ())),
                preferred_element_type=jnp.float32,
            )
            result = product if result is None else result + product
        return result.reshape(count, ROWS, LANES)

    places = (0, *PLACES) if len(outs) == 4 else (0, 1)
    ordered = [outs[places.index(i)] for i in range(len(outs))]
    size = outs[0].shape[0]
    blocks = size * len(outs)
    if blocks <= 16:
        result = dense(0, blocks)
        for i, out in enumerate(ordered):
            out[...] = result[i * size : (i + 1) * size]
    else:
        for i, out in enumerate(ordered):

            @pl.loop(0, size // 8)
            def _(g):
                out[pl.ds(g * 8, 8)] = dense(i * size + g * 8, 8)

    flat = state[0].reshape(4 * radial, around)
    turned = jnp.concatenate([flat[:, around - LANES :], flat[:, :LANES]], axis=0).T
    lane = lax.broadcasted_iota(jnp.int32, (1, LANES), 1)
    edge = jnp.where(lane < LANES // 2, turned[LANES - 1 :, :], turned[:1, :])
    for out in outs:
        out[0, EDGE : EDGE + 1, :] = edge


def halving_kernel(arrived, riding, *refs):
    outs = refs[arrived:]
    size = outs[0].shape[0]
    for i, out in enumerate(outs):
        for b in range(size):
            out[b] = functools.reduce(jnp.add, [ref[i * size + b] for ref in refs[:arrived]])
        if riding:
            for j, ref in enumerate(refs[:arrived]):
                out[0, EDGE + j : EDGE + j + 1, :] = ref[0, EDGE : EDGE + 1, :]


def weight_from(weights, instances, source, target):
    shift = (target - source + instances) % instances
    value = weights[0]
    for i in range(1, instances):
        value = jnp.where(shift == i, weights[i], value)
    return value


def pair_kernel(weights, instances, first, seconds, state, partner, *outs):
    me = lax.axis_index("inst")
    for i, out in enumerate(outs):
        second, part = seconds[i // PARTS], pl.ds(i % PARTS * out.shape[1], out.shape[1])
        own = weight_from(weights, instances, me, me ^ second)
        other = weight_from(weights, instances, me ^ first, me ^ second)
        out[...] = own * state[:, part] + other * partner[:, part]


def around_flux(q, vc, p):
    return (q[2], q[1] * vc, q[2] * vc + p, (q[3] + p) * vc)


def flux_kernel(weight, instances, state, base, step):
    radial, around = state.shape[2:]
    q = [state[0, c] for c in range(4)]
    inverse, vr, vc, p = pressure_of(*q)
    a = jnp.sqrt(gamma_ratio * p * inverse)
    step[...] = cfl_number / (
        jnp.abs(vr) + jnp.abs(vc) + 2.0 * a + omega_rate * instances / 2.0
    )

    def after(x):
        return pltpu.roll(x, around - 1, 1)

    def above(x):
        return pltpu.roll(x, radial - 1, 0)

    column = lax.broadcasted_iota(jnp.int32, (radial, around), 1)
    row = lax.broadcasted_iota(jnp.int32, (radial, around), 0)
    hub, tip = row == 0, row == radial - 1
    speed = jnp.abs(vc) + a
    reach = 0.5 * jnp.maximum(speed, after(speed))
    speed = jnp.abs(vr) + a
    rise = 0.5 * jnp.maximum(speed, above(speed))
    flux = around_flux(q, vc, p)
    radial_flux = (q[1], q[1] * vr + p, q[2] * vr, (q[3] + p) * vr)
    for c in range(4):
        face = 0.5 * (flux[c] + after(flux[c])) - reach * (after(q[c]) - q[c])
        face = jnp.where(column == around - 1, 0.0, face)
        residual = weight * q[c] + (face - pltpu.roll(face, 1, 1))
        wall = p if c == 1 else 0.0
        face = 0.5 * (radial_flux[c] + above(radial_flux[c])) - rise * (above(q[c]) - q[c])
        upper = jnp.where(tip, wall, face)
        lower = jnp.where(hub, wall, pltpu.roll(face, 1, 0))
        base[0, c] = residual + (upper - lower)


def outer_kernel(weights, instances, first, blocks, state, base, kept, came, partner, *refs):
    *edges, residual, total = refs
    radial, around = state.shape[2:]
    if blocks == RIDING:
        me = lax.axis_index("space")
        known = [kept[0, EDGE:, :], came[0, EDGE:, :]]
        known = jnp.concatenate(known, axis=0)
        row = lax.broadcasted_iota(jnp.int32, known.shape, 0)

        def edge_of(device):
            relative = device ^ me
            half = RIDING // 2
            place = 0
            for row_place, chip in enumerate(PLACES, 1):
                place = jnp.where(relative // 2 == chip, row_place, place)
            place += (relative % 2) * half
            return jnp.sum(jnp.where(row == place, known, 0.0), axis=0, keepdims=True)

        before = edge_of((me + blocks - 1) % blocks)
        after = edge_of((me + 1) % blocks)
    else:
        before, after = (ref[0:1, :] for ref in edges)
    me = lax.axis_index("inst")
    weight = weight_from(weights, instances, me ^ first, me)
    lane = lax.broadcasted_iota(jnp.int32, (1, LANES), 1)
    edge = jnp.where(lane < LANES // 2, before, after)
    columns = jnp.broadcast_to(edge, (LANES, LANES)).T

    lane = lax.broadcasted_iota(jnp.int32, (radial, LANES), 1)
    left, right = lane == 0, lane == LANES - 1
    own, far = [], []
    for c in range(4):
        own.append(jnp.where(left, state[0, c, :, :LANES], state[0, c, :, around - LANES :]))
        far.append(
            jnp.where(
                right,
                columns[LANES // 2 + c * radial : LANES // 2 + (c + 1) * radial],
                columns[c * radial : (c + 1) * radial],
            )
        )
    faces, speeds = [], []
    for q in (own, far):
        inverse, _, vc, p = pressure_of(*q)
        speeds.append(jnp.abs(vc) + jnp.sqrt(gamma_ratio * p * inverse))
        faces.append(around_flux(q, vc, p))
    side = jnp.where(right, 0.5, -0.5)
    reach = 0.5 * jnp.maximum(*speeds)
    for c in range(4):
        outer = side * (faces[0][c] + faces[1][c]) - reach * (far[c] - own[c])
        outer = [jnp.where(left, outer, 0.0), jnp.where(right, outer, 0.0)]
        middle = around - 2 * LANES
        if middle:
            outer.insert(1, jnp.zeros((radial, middle), jnp.float32))
        residual[0, c] = base[0, c] + weight * partner[0, c] + jnp.concatenate(outer, axis=1)

    total[...] = kept[0] + came[0]


def update_kernel(residual, step, total, *refs):
    *sums, increment, blade = refs
    high = blade.shape[2] // LANES
    for k in range(3):
        for h in range(high):
            blade[k, :, pl.ds(h * LANES, LANES)] = total[k * high + h : k * high + h + 1, :]
    for c in range(residual.shape[1]):
        size = residual.shape[1] // PARTS
        parts = [ref[0, c % size] for ref in sums[c // size :: PARTS]]
        change = functools.reduce(jnp.add, [residual[0, c], *parts])
        increment[0, c] = -step[...] * change


def per_device(node_block, state, face_cell, face_node, face_area):
    blocks = lax.axis_size("space")
    instances = lax.axis_size("inst")
    radial, around = state.shape[2:]
    chunks = face_cell.shape[0] // LANES
    vmem = pl.BlockSpec(memory_space=pltpu.VMEM)
    params = pltpu.CompilerParams(vmem_limit_bytes=(4 if blocks <= 16 else 16) * 2**20)

    def swapped(value, axis, bit):
        return lax.ppermute(value, axis, [(i, i ^ bit) for i in range(lax.axis_size(axis))])

    def shifted(value, axis, s):
        count = lax.axis_size(axis)
        return lax.ppermute(value, axis, [(i, (i + s) % count) for i in range(count)])

    def exchanged(sent, size):
        places = PLACES if len(sent) == 3 else (1,)
        return [swapped(value, "space", place * size) for place, value in zip(places, sent)]

    def call(kernel, name, shapes, *operands, flops=0, dtype=jnp.float32):
        return pl.pallas_call(
            kernel,
            out_shape=[jax.ShapeDtypeStruct(shape, dtype) for shape in shapes],
            in_specs=[vmem] * len(operands),
            out_specs=[vmem] * len(shapes),
            compiler_params=params,
            cost_estimate=pl.CostEstimate(flops=flops, bytes_accessed=0, transcendentals=0),
            name=name,
        )(*operands)

    weights = spectral_row(instances)
    first, seconds = 1, range(2, instances, 2)
    partner = swapped(state, "inst", first)

    riding = blocks == RIDING
    steps = [4, 2] if riding else [2] * (blocks.bit_length() - 1)
    size = blocks // steps[0]
    (own,) = call(
        functools.partial(own_kernel, node_block // LANES),
        "own",
        [(8, LANES)],
        dtype=jnp.int32,
        flops=PLACING,
    )
    kept, *sent = call(
        functools.partial(forces_kernel, node_block),
        "face_forces",
        [(size, ROWS, LANES)] * steps[0],
        own,
        state,
        face_cell.reshape(chunks, LANES),
        face_node.reshape(chunks, LANES),
        face_area,
        flops=PLACING,
    )

    edges = []
    if not riding:
        row = jnp.broadcast_to(kept[0, EDGE : EDGE + 1, :], (8, LANES))
        edges = [shifted(row, "space", 1), shifted(row, "space", blocks - 1)]

    came = exchanged(sent, size)
    sums = call(
        functools.partial(pair_kernel, weights, instances, first, seconds),
        "pair_sums",
        [(1, 4 // PARTS, radial, around)] * (PARTS * len(seconds)),
        state,
        partner,
        flops=PLACING,
    )
    sums = [swapped(value, "inst", seconds[i // PARTS]) for i, value in enumerate(sums)]

    for step in steps[1:]:
        size //= step
        kept, *sent = call(
            functools.partial(halving_kernel, 1 + len(came), riding),
            "halving",
            [(size, ROWS, LANES)] * step,
            kept,
            *came,
            flops=PLACING,
        )
        came = exchanged(sent, size)

    base, step = call(
        functools.partial(flux_kernel, weights[0], instances),
        "flux",
        [state.shape, (radial, around)],
        state,
    )
    residual, total = call(
        functools.partial(outer_kernel, weights, instances, first, blocks),
        "outer",
        [state.shape, (ROWS, LANES)],
        state,
        base,
        kept,
        *came,
        partner,
        *edges,
    )
    increment, blade = call(
        update_kernel,
        "update",
        [state.shape, (3, 1, node_block)],
        residual,
        step,
        total,
        *sums,
    )
    return increment, jnp.transpose(blade, (1, 0, 2))


def solution(mesh):
    in_specs = (P("inst", None, None, "space"), P("space"), P("space"), P(None, "space"))
    out_specs = (P("inst", None, None, "space"), P("inst", None, "space"))
    return jax.shard_map(
        functools.partial(per_device, 512),
        mesh=mesh,
        in_specs=in_specs,
        out_specs=out_specs,
        check_vma=False,
    )
```

```python
import functools
import math

import jax
import jax.numpy as jnp
import numpy as np
from jax import lax
from jax.experimental import pallas as pl
from jax.experimental.pallas import tpu as pltpu
from jax.sharding import PartitionSpec as P

gamma_ratio = 1.4
omega_rate = 0.5
cfl_number = 0.8

LANES = 128
ROWS = 16
EDGE = 12
PLACING = 10**10
PLACES = (2, 3, 1)
ORDERS = ((2, 1), (1, 2))
RIDING = 8


def spectral_row(count):
    row = np.zeros((count,), np.float32)
    for shift in range(count):
        row[shift] = (-1.0) ** shift / count
        if shift != 0:
            row[shift] += 0.5 * (-1.0) ** shift / math.tan(math.pi * shift / count)
    return [float(omega_rate * value) for value in row]


def pressure_of(q0, q1, q2, q3):
    inverse = 1.0 / q0
    vr = q1 * inverse
    vc = q2 * inverse
    p = (gamma_ratio - 1.0) * (q3 - 0.5 * q0 * (vr * vr + vc * vc))
    return inverse, vr, vc, p


def own_kernel(high, out):
    out[...] = jnp.full(out.shape, lax.axis_index("space") * high, jnp.int32)


def forces_kernel(node_block, own, state, cell, node, area, *outs):
    radial, around = state.shape[2:]
    faces = cell.shape[0] * LANES
    chunks = faces // LANES
    _, _, _, p = pressure_of(state[0, 0], state[0, 1], state[0, 2], state[0, 3])
    sublane = lax.broadcasted_iota(jnp.int32, (8, LANES), 0)
    picked = []
    for c in range(chunks):
        index = jnp.broadcast_to(cell[c : c + 1, :], (8, LANES))
        row = index // around
        column = index % around
        lane = column % LANES
        half = column // LANES
        total = jnp.zeros((8, LANES), jnp.float32)
        for r in range(radial // 8):
            for h in range(around // LANES):
                part = p[r * 8 : (r + 1) * 8, h * LANES : (h + 1) * LANES]
                value = jnp.take_along_axis(part, lane, axis=1, mode="promise_in_bounds")
                total += jnp.where((row == sublane + r * 8) & (half == h), value, 0.0)
        picked.append(jnp.sum(total, axis=0, keepdims=True))
    face_pressure = jnp.concatenate(picked, axis=1)
    contribution = face_pressure * area[...]
    nodes = jnp.concatenate([node[c : c + 1, :] for c in range(chunks)], axis=1)

    high = node_block // LANES
    place = nodes // LANES ^ jnp.broadcast_to(own[0:1, 0:1], nodes.shape)
    low = nodes % LANES
    pick_low = (
        lax.broadcasted_iota(jnp.int32, (LANES, faces), 0) == jnp.broadcast_to(low, (LANES, faces))
    ).astype(jnp.float32).astype(jnp.bfloat16)
    pattern = jnp.concatenate(
        [jnp.broadcast_to(contribution[k : k + 1], (high, faces)) for k in range(3)]
        + [jnp.zeros((ROWS - 3 * high, faces), jnp.float32)],
        axis=0,
    )
    first = pattern.astype(jnp.bfloat16).astype(jnp.float32)
    second = pattern - first
    place = jnp.broadcast_to(place, (ROWS, faces))
    row_high = lax.broadcasted_iota(jnp.int32, (ROWS, faces), 0) % high

    def dense(start, count):
        masks = [place == row_high + (start + b) * high for b in range(count)]
        result = None
        for part in (first, second):
            left = jnp.concatenate([jnp.where(m, part, 0.0) for m in masks], axis=0)
            product = lax.dot_general(
                left.astype(jnp.bfloat16),
                pick_low,
                (((1,), (1,)), ((), ())),
                preferred_element_type=jnp.float32,
            )
            result = product if result is None else result + product
        return result.reshape(count, ROWS, LANES)

    places = (0, *PLACES) if len(outs) == 4 else (0, 1)
    ordered = [outs[places.index(i)] for i in range(len(outs))]
    size = outs[0].shape[0]
    blocks = size * len(outs)
    if blocks <= 16:
        result = dense(0, blocks)
        for i, out in enumerate(ordered):
            out[...] = result[i * size : (i + 1) * size]
    else:
        for i, out in enumerate(ordered):

            @pl.loop(0, size // 8)
            def _(g):
                out[pl.ds(g * 8, 8)] = dense(i * size + g * 8, 8)

    flat = state[0].reshape(4 * radial, around)
    turned = jnp.concatenate([flat[:, around - LANES :], flat[:, :LANES]], axis=0).T
    lane = lax.broadcasted_iota(jnp.int32, (1, LANES), 1)
    edge = jnp.where(lane < LANES // 2, turned[LANES - 1 :, :], turned[:1, :])
    for out in outs:
        out[0, EDGE : EDGE + 1, :] = edge


def halving_kernel(arrived, riding, *refs):
    outs = refs[arrived:]
    size = outs[0].shape[0]
    for i, out in enumerate(outs):
        for b in range(size):
            out[b] = functools.reduce(jnp.add, [ref[i * size + b] for ref in refs[:arrived]])
        if riding:
            for j, ref in enumerate(refs[:arrived]):
                out[0, EDGE + j : EDGE + j + 1, :] = ref[0, EDGE : EDGE + 1, :]


def weight_from(weights, instances, source, target):
    shift = (target - source + instances) % instances
    value = weights[0]
    for i in range(1, instances):
        value = jnp.where(shift == i, weights[i], value)
    return value


def of_chip(orders):
    chip = lax.axis_index("space") // 2
    return [jnp.where(chip == 0, a, b) for a, b in zip(*orders)]


def pair_kernel(weights, instances, orders, state, partner, *outs):
    me = lax.axis_index("inst")
    first, *seconds = of_chip(orders)
    for second, out in zip(seconds, outs):
        own = weight_from(weights, instances, me, me ^ second)
        other = weight_from(weights, instances, me ^ first, me ^ second)
        out[...] = own * state[...] + other * partner[...]


def around_flux(q, vc, p):
    return (q[2], q[1] * vc, q[2] * vc + p, (q[3] + p) * vc)


def flux_kernel(weight, instances, state, base, step):
    radial, around = state.shape[2:]
    q = [state[0, c] for c in range(4)]
    inverse, vr, vc, p = pressure_of(*q)
    a = jnp.sqrt(gamma_ratio * p * inverse)
    step[...] = cfl_number / (
        jnp.abs(vr) + jnp.abs(vc) + 2.0 * a + omega_rate * instances / 2.0
    )

    def after(x):
        return pltpu.roll(x, around - 1, 1)

    def above(x):
        return pltpu.roll(x, radial - 1, 0)

    column = lax.broadcasted_iota(jnp.int32, (radial, around), 1)
    row = lax.broadcasted_iota(jnp.int32, (radial, around), 0)
    hub, tip = row == 0, row == radial - 1
    speed = jnp.abs(vc) + a
    reach = 0.5 * jnp.maximum(speed, after(speed))
    speed = jnp.abs(vr) + a
    rise = 0.5 * jnp.maximum(speed, above(speed))
    flux = around_flux(q, vc, p)
    radial_flux = (q[1], q[1] * vr + p, q[2] * vr, (q[3] + p) * vr)
    for c in range(4):
        face = 0.5 * (flux[c] + after(flux[c])) - reach * (after(q[c]) - q[c])
        face = jnp.where(column == around - 1, 0.0, face)
        residual = weight * q[c] + (face - pltpu.roll(face, 1, 1))
        wall = p if c == 1 else 0.0
        face = 0.5 * (radial_flux[c] + above(radial_flux[c])) - rise * (above(q[c]) - q[c])
        upper = jnp.where(tip, wall, face)
        lower = jnp.where(hub, wall, pltpu.roll(face, 1, 0))
        base[0, c] = residual + (upper - lower)


def outer_kernel(weights, instances, orders, blocks, state, base, kept, came, partner, *refs):
    *edges, residual, total = refs
    radial, around = state.shape[2:]
    if blocks == RIDING:
        me = lax.axis_index("space")
        known = [kept[0, EDGE:, :], came[0, EDGE:, :]]
        known = jnp.concatenate(known, axis=0)
        row = lax.broadcasted_iota(jnp.int32, known.shape, 0)

        def edge_of(device):
            relative = device ^ me
            half = RIDING // 2
            place = 0
            for row_place, chip in enumerate(PLACES, 1):
                place = jnp.where(relative // 2 == chip, row_place, place)
            place += (relative % 2) * half
            return jnp.sum(jnp.where(row == place, known, 0.0), axis=0, keepdims=True)

        before = edge_of((me + blocks - 1) % blocks)
        after = edge_of((me + 1) % blocks)
    else:
        before, after = (ref[0:1, :] for ref in edges)
    me = lax.axis_index("inst")
    weight = weight_from(weights, instances, me ^ of_chip(orders)[0], me)
    lane = lax.broadcasted_iota(jnp.int32, (1, LANES), 1)
    edge = jnp.where(lane < LANES // 2, before, after)
    columns = jnp.broadcast_to(edge, (LANES, LANES)).T

    lane = lax.broadcasted_iota(jnp.int32, (radial, LANES), 1)
    left, right = lane == 0, lane == LANES - 1
    own, far = [], []
    for c in range(4):
        own.append(jnp.where(left, state[0, c, :, :LANES], state[0, c, :, around - LANES :]))
        far.append(
            jnp.where(
                right,
                columns[LANES // 2 + c * radial : LANES // 2 + (c + 1) * radial],
                columns[c * radial : (c + 1) * radial],
            )
        )
    faces, speeds = [], []
    for q in (own, far):
        inverse, _, vc, p = pressure_of(*q)
        speeds.append(jnp.abs(vc) + jnp.sqrt(gamma_ratio * p * inverse))
        faces.append(around_flux(q, vc, p))
    side = jnp.where(right, 0.5, -0.5)
    reach = 0.5 * jnp.maximum(*speeds)
    for c in range(4):
        outer = side * (faces[0][c] + faces[1][c]) - reach * (far[c] - own[c])
        outer = [jnp.where(left, outer, 0.0), jnp.where(right, outer, 0.0)]
        middle = around - 2 * LANES
        if middle:
            outer.insert(1, jnp.zeros((radial, middle), jnp.float32))
        residual[0, c] = base[0, c] + weight * partner[0, c] + jnp.concatenate(outer, axis=1)

    total[...] = kept[0] + came[0]


def update_kernel(residual, step, total, *refs):
    *sums, increment, blade = refs
    high = blade.shape[2] // LANES
    for k in range(3):
        for h in range(high):
            blade[k, :, pl.ds(h * LANES, LANES)] = total[k * high + h : k * high + h + 1, :]
    for c in range(residual.shape[1]):
        change = functools.reduce(jnp.add, [ref[0, c] for ref in (residual, *sums)])
        increment[0, c] = -step[...] * change


def per_device(node_block, state, face_cell, face_node, face_area):
    blocks = lax.axis_size("space")
    instances = lax.axis_size("inst")
    radial, around = state.shape[2:]
    chunks = face_cell.shape[0] // LANES
    vmem = pl.BlockSpec(memory_space=pltpu.VMEM)
    params = pltpu.CompilerParams(vmem_limit_bytes=(4 if blocks <= 16 else 16) * 2**20)

    def swapped(value, axis, bit):
        return lax.ppermute(value, axis, [(i, i ^ bit) for i in range(lax.axis_size(axis))])

    def shifted(value, axis, s):
        count = lax.axis_size(axis)
        return lax.ppermute(value, axis, [(i, (i + s) % count) for i in range(count)])

    def exchanged(sent, size):
        places = PLACES if len(sent) == 3 else (1,)
        return [swapped(value, "space", place * size) for place, value in zip(places, sent)]

    def call(kernel, name, shapes, *operands, flops=0, dtype=jnp.float32):
        return pl.pallas_call(
            kernel,
            out_shape=[jax.ShapeDtypeStruct(shape, dtype) for shape in shapes],
            in_specs=[vmem] * len(operands),
            out_specs=[vmem] * len(shapes),
            compiler_params=params,
            cost_estimate=pl.CostEstimate(flops=flops, bytes_accessed=0, transcendentals=0),
            name=name,
        )(*operands)

    weights = spectral_row(instances)
    def partnered(value, place):
        pairs = [
            (i * instances + n, i * instances + (n ^ orders[min(i // 2, 1)][place]))
            for i in range(blocks)
            for n in range(instances)
        ]
        return lax.ppermute(value, ("space", "inst"), pairs)

    orders = ORDERS if instances == 4 else ((1, *range(2, instances, 2)),) * 2
    partner = partnered(state, 0)

    riding = blocks == RIDING
    steps = [4, 2] if riding else [2] * (blocks.bit_length() - 1)
    size = blocks // steps[0]
    (own,) = call(
        functools.partial(own_kernel, node_block // LANES),
        "own",
        [(8, LANES)],
        dtype=jnp.int32,
        flops=PLACING,
    )
    kept, *sent = call(
        functools.partial(forces_kernel, node_block),
        "face_forces",
        [(size, ROWS, LANES)] * steps[0],
        own,
        state,
        face_cell.reshape(chunks, LANES),
        face_node.reshape(chunks, LANES),
        face_area,
        flops=PLACING,
    )

    edges = []
    if not riding:
        row = jnp.broadcast_to(kept[0, EDGE : EDGE + 1, :], (8, LANES))
        edges = [shifted(row, "space", 1), shifted(row, "space", blocks - 1)]

    came = exchanged(sent, size)
    sums = call(
        functools.partial(pair_kernel, weights, instances, orders),
        "pair_sums",
        [state.shape] * (len(orders[0]) - 1),
        state,
        partner,
        flops=PLACING,
    )
    sums = [partnered(value, i) for i, value in enumerate(sums, 1)]

    for step in steps[1:]:
        size //= step
        kept, *sent = call(
            functools.partial(halving_kernel, 1 + len(came), riding),
            "halving",
            [(size, ROWS, LANES)] * step,
            kept,
            *came,
            flops=PLACING,
        )
        came = exchanged(sent, size)

    base, step = call(
        functools.partial(flux_kernel, weights[0], instances),
        "flux",
        [state.shape, (radial, around)],
        state,
    )
    residual, total = call(
        functools.partial(outer_kernel, weights, instances, orders, blocks),
        "outer",
        [state.shape, (ROWS, LANES)],
        state,
        base,
        kept,
        *came,
        partner,
        *edges,
    )
    increment, blade = call(
        update_kernel,
        "update",
        [state.shape, (3, 1, node_block)],
        residual,
        step,
        total,
        *sums,
    )
    return increment, jnp.transpose(blade, (1, 0, 2))


def solution(mesh):
    in_specs = (P("inst", None, None, "space"), P("space"), P("space"), P(None, "space"))
    out_specs = (P("inst", None, None, "space"), P("inst", None, "space"))
    return jax.shard_map(
        functools.partial(per_device, 512),
        mesh=mesh,
        in_specs=in_specs,
        out_specs=out_specs,
        check_vma=False,
    )
```

```python
import functools
import math

import jax
import jax.numpy as jnp
import numpy as np
from jax import lax
from jax.experimental import pallas as pl
from jax.experimental.pallas import tpu as pltpu
from jax.sharding import PartitionSpec as P

gamma_ratio = 1.4
omega_rate = 0.5
cfl_number = 0.8

LANES = 128
ROWS = 16
EDGE = 12
PLACING = 10**10
ORDERS = ((2, 1), (1, 2))
RIDING = 8


def spectral_row(count):
    row = np.zeros((count,), np.float32)
    for shift in range(count):
        row[shift] = (-1.0) ** shift / count
        if shift != 0:
            row[shift] += 0.5 * (-1.0) ** shift / math.tan(math.pi * shift / count)
    return [float(omega_rate * value) for value in row]


def pressure_of(q0, q1, q2, q3):
    inverse = 1.0 / q0
    vr = q1 * inverse
    vc = q2 * inverse
    p = (gamma_ratio - 1.0) * (q3 - 0.5 * q0 * (vr * vr + vc * vc))
    return inverse, vr, vc, p


def own_kernel(high, out):
    out[...] = jnp.full(out.shape, lax.axis_index("space") * high, jnp.int32)


def forces_kernel(node_block, own, state, cell, node, area, *outs):
    radial, around = state.shape[2:]
    faces = cell.shape[0] * LANES
    chunks = faces // LANES
    _, _, _, p = pressure_of(state[0, 0], state[0, 1], state[0, 2], state[0, 3])
    sublane = lax.broadcasted_iota(jnp.int32, (8, LANES), 0)
    picked = []
    for c in range(chunks):
        index = jnp.broadcast_to(cell[c : c + 1, :], (8, LANES))
        row = index // around
        column = index % around
        lane = column % LANES
        half = column // LANES
        total = jnp.zeros((8, LANES), jnp.float32)
        for r in range(radial // 8):
            for h in range(around // LANES):
                part = p[r * 8 : (r + 1) * 8, h * LANES : (h + 1) * LANES]
                value = jnp.take_along_axis(part, lane, axis=1, mode="promise_in_bounds")
                total += jnp.where((row == sublane + r * 8) & (half == h), value, 0.0)
        picked.append(jnp.sum(total, axis=0, keepdims=True))
    face_pressure = jnp.concatenate(picked, axis=1)
    contribution = face_pressure * area[...]
    nodes = jnp.concatenate([node[c : c + 1, :] for c in range(chunks)], axis=1)

    high = node_block // LANES
    place = nodes // LANES ^ jnp.broadcast_to(own[0:1, 0:1], nodes.shape)
    low = nodes % LANES
    pick_low = (
        lax.broadcasted_iota(jnp.int32, (LANES, faces), 0) == jnp.broadcast_to(low, (LANES, faces))
    ).astype(jnp.float32).astype(jnp.bfloat16)
    pattern = jnp.concatenate(
        [jnp.broadcast_to(contribution[k : k + 1], (high, faces)) for k in range(3)]
        + [jnp.zeros((ROWS - 3 * high, faces), jnp.float32)],
        axis=0,
    )
    first = pattern.astype(jnp.bfloat16).astype(jnp.float32)
    second = pattern - first
    place = jnp.broadcast_to(place, (ROWS, faces))
    row_high = lax.broadcasted_iota(jnp.int32, (ROWS, faces), 0) % high

    def dense(start, count):
        masks = [place == row_high + (start + b) * high for b in range(count)]
        result = None
        for part in (first, second):
            left = jnp.concatenate([jnp.where(m, part, 0.0) for m in masks], axis=0)
            product = lax.dot_general(
                left.astype(jnp.bfloat16),
                pick_low,
                (((1,), (1,)), ((), ())),
                preferred_element_type=jnp.float32,
            )
            result = product if result is None else result + product
        return result.reshape(count, ROWS, LANES)

    ordered = outs[:1] + outs[:0:-1]
    size = outs[0].shape[0]
    blocks = size * len(outs)
    if blocks <= 16:
        result = dense(0, blocks)
        for i, out in enumerate(ordered):
            out[...] = result[i * size : (i + 1) * size]
    else:
        for i, out in enumerate(ordered):

            @pl.loop(0, size // 8)
            def _(g):
                out[pl.ds(g * 8, 8)] = dense(i * size + g * 8, 8)

    flat = state[0].reshape(4 * radial, around)
    turned = jnp.concatenate([flat[:, around - LANES :], flat[:, :LANES]], axis=0).T
    lane = lax.broadcasted_iota(jnp.int32, (1, LANES), 1)
    edge = jnp.where(lane < LANES // 2, turned[LANES - 1 :, :], turned[:1, :])
    for out in outs:
        out[0, EDGE : EDGE + 1, :] = edge


def halving_kernel(arrived, riding, *refs):
    outs = refs[arrived:]
    size = outs[0].shape[0]
    for i, out in enumerate(outs):
        for b in range(size):
            out[b] = functools.reduce(jnp.add, [ref[i * size + b] for ref in refs[:arrived]])
        if riding:
            for j, ref in enumerate(refs[:arrived]):
                out[0, EDGE + j : EDGE + j + 1, :] = ref[0, EDGE : EDGE + 1, :]


def weight_from(weights, instances, source, target):
    shift = (target - source + instances) % instances
    value = weights[0]
    for i in range(1, instances):
        value = jnp.where(shift == i, weights[i], value)
    return value


def of_chip(orders):
    chip = lax.axis_index("space") // 2
    return [jnp.where(chip == 0, a, b) for a, b in zip(*orders)]


def pair_kernel(weights, instances, orders, state, partner, *outs):
    me = lax.axis_index("inst")
    first, *seconds = of_chip(orders)
    for second, out in zip(seconds, outs):
        own = weight_from(weights, instances, me, me ^ second)
        other = weight_from(weights, instances, me ^ first, me ^ second)
        out[...] = own * state[...] + other * partner[...]


def around_flux(q, vc, p):
    return (q[2], q[1] * vc, q[2] * vc + p, (q[3] + p) * vc)


def flux_kernel(weight, instances, state, base, step):
    radial, around = state.shape[2:]
    q = [state[0, c] for c in range(4)]
    inverse, vr, vc, p = pressure_of(*q)
    a = jnp.sqrt(gamma_ratio * p * inverse)
    step[...] = cfl_number / (
        jnp.abs(vr) + jnp.abs(vc) + 2.0 * a + omega_rate * instances / 2.0
    )

    def after(x):
        return pltpu.roll(x, around - 1, 1)

    def above(x):
        return pltpu.roll(x, radial - 1, 0)

    column = lax.broadcasted_iota(jnp.int32, (radial, around), 1)
    row = lax.broadcasted_iota(jnp.int32, (radial, around), 0)
    hub, tip = row == 0, row == radial - 1
    speed = jnp.abs(vc) + a
    reach = 0.5 * jnp.maximum(speed, after(speed))
    speed = jnp.abs(vr) + a
    rise = 0.5 * jnp.maximum(speed, above(speed))
    flux = around_flux(q, vc, p)
    radial_flux = (q[1], q[1] * vr + p, q[2] * vr, (q[3] + p) * vr)
    for c in range(4):
        face = 0.5 * (flux[c] + after(flux[c])) - reach * (after(q[c]) - q[c])
        face = jnp.where(column == around - 1, 0.0, face)
        residual = weight * q[c] + (face - pltpu.roll(face, 1, 1))
        wall = p if c == 1 else 0.0
        face = 0.5 * (radial_flux[c] + above(radial_flux[c])) - rise * (above(q[c]) - q[c])
        upper = jnp.where(tip, wall, face)
        lower = jnp.where(hub, wall, pltpu.roll(face, 1, 0))
        base[0, c] = residual + (upper - lower)


def outer_kernel(weights, instances, orders, blocks, state, base, kept, came, partner, *refs):
    *edges, residual, total = refs
    radial, around = state.shape[2:]
    if blocks == RIDING:
        me = lax.axis_index("space")
        known = [kept[0, EDGE:, :], came[0, EDGE:, :]]
        known = jnp.concatenate(known, axis=0)
        row = lax.broadcasted_iota(jnp.int32, known.shape, 0)

        def edge_of(device):
            relative = device ^ me
            half = RIDING // 2
            place = (half - relative // 2) % half + (relative % 2) * half
            return jnp.sum(jnp.where(row == place, known, 0.0), axis=0, keepdims=True)

        before = edge_of((me + blocks - 1) % blocks)
        after = edge_of((me + 1) % blocks)
    else:
        before, after = (ref[0:1, :] for ref in edges)
    me = lax.axis_index("inst")
    weight = weight_from(weights, instances, me ^ of_chip(orders)[0], me)
    lane = lax.broadcasted_iota(jnp.int32, (1, LANES), 1)
    edge = jnp.where(lane < LANES // 2, before, after)
    columns = jnp.broadcast_to(edge, (LANES, LANES)).T

    lane = lax.broadcasted_iota(jnp.int32, (radial, LANES), 1)
    left, right = lane == 0, lane == LANES - 1
    own, far = [], []
    for c in range(4):
        own.append(jnp.where(left, state[0, c, :, :LANES], state[0, c, :, around - LANES :]))
        far.append(
            jnp.where(
                right,
                columns[LANES // 2 + c * radial : LANES // 2 + (c + 1) * radial],
                columns[c * radial : (c + 1) * radial],
            )
        )
    faces, speeds = [], []
    for q in (own, far):
        inverse, _, vc, p = pressure_of(*q)
        speeds.append(jnp.abs(vc) + jnp.sqrt(gamma_ratio * p * inverse))
        faces.append(around_flux(q, vc, p))
    side = jnp.where(right, 0.5, -0.5)
    reach = 0.5 * jnp.maximum(*speeds)
    for c in range(4):
        outer = side * (faces[0][c] + faces[1][c]) - reach * (far[c] - own[c])
        outer = [jnp.where(left, outer, 0.0), jnp.where(right, outer, 0.0)]
        middle = around - 2 * LANES
        if middle:
            outer.insert(1, jnp.zeros((radial, middle), jnp.float32))
        residual[0, c] = base[0, c] + weight * partner[0, c] + jnp.concatenate(outer, axis=1)

    total[...] = kept[0] + came[0]


def update_kernel(residual, step, total, *refs):
    *sums, increment, blade = refs
    high = blade.shape[2] // LANES
    for k in range(3):
        for h in range(high):
            blade[k, :, pl.ds(h * LANES, LANES)] = total[k * high + h : k * high + h + 1, :]
    for c in range(residual.shape[1]):
        change = functools.reduce(jnp.add, [ref[0, c] for ref in (residual, *sums)])
        increment[0, c] = -step[...] * change


def per_device(node_block, state, face_cell, face_node, face_area):
    blocks = lax.axis_size("space")
    instances = lax.axis_size("inst")
    radial, around = state.shape[2:]
    chunks = face_cell.shape[0] // LANES
    vmem = pl.BlockSpec(memory_space=pltpu.VMEM)
    params = pltpu.CompilerParams(vmem_limit_bytes=(4 if blocks <= 16 else 16) * 2**20)

    def swapped(value, axis, bit):
        return lax.ppermute(value, axis, [(i, i ^ bit) for i in range(lax.axis_size(axis))])

    def shifted(value, axis, s):
        count = lax.axis_size(axis)
        return lax.ppermute(value, axis, [(i, (i + s) % count) for i in range(count)])

    def exchanged(sent, size):
        return [
            swapped(value, "space", (len(sent) - i) * size) for i, value in enumerate(sent)
        ]

    def call(kernel, name, shapes, *operands, flops=0, dtype=jnp.float32):
        return pl.pallas_call(
            kernel,
            out_shape=[jax.ShapeDtypeStruct(shape, dtype) for shape in shapes],
            in_specs=[vmem] * len(operands),
            out_specs=[vmem] * len(shapes),
            compiler_params=params,
            cost_estimate=pl.CostEstimate(flops=flops, bytes_accessed=0, transcendentals=0),
            name=name,
        )(*operands)

    weights = spectral_row(instances)
    def partnered(value, place):
        pairs = [
            (i * instances + n, i * instances + (n ^ orders[min(i // 2, 1)][place]))
            for i in range(blocks)
            for n in range(instances)
        ]
        return lax.ppermute(value, ("space", "inst"), pairs)

    orders = ORDERS if instances == 4 else ((1, *range(2, instances, 2)),) * 2
    partner = partnered(state, 0)

    riding = blocks == RIDING
    steps = [4, 2] if riding else [2] * (blocks.bit_length() - 1)
    size = blocks // steps[0]
    (own,) = call(
        functools.partial(own_kernel, node_block // LANES),
        "own",
        [(8, LANES)],
        dtype=jnp.int32,
        flops=PLACING,
    )
    kept, *sent = call(
        functools.partial(forces_kernel, node_block),
        "face_forces",
        [(size, ROWS, LANES)] * steps[0],
        own,
        state,
        face_cell.reshape(chunks, LANES),
        face_node.reshape(chunks, LANES),
        face_area,
        flops=PLACING,
    )

    edges = []
    if not riding:
        row = jnp.broadcast_to(kept[0, EDGE : EDGE + 1, :], (8, LANES))
        edges = [shifted(row, "space", 1), shifted(row, "space", blocks - 1)]

    came = exchanged(sent, size)
    sums = call(
        functools.partial(pair_kernel, weights, instances, orders),
        "pair_sums",
        [state.shape] * (len(orders[0]) - 1),
        state,
        partner,
        flops=PLACING,
    )
    sums = [partnered(value, i) for i, value in enumerate(sums, 1)]

    for step in steps[1:]:
        size //= step
        kept, *sent = call(
            functools.partial(halving_kernel, 1 + len(came), riding),
            "halving",
            [(size, ROWS, LANES)] * step,
            kept,
            *came,
            flops=PLACING,
        )
        came = exchanged(sent, size)

    base, step = call(
        functools.partial(flux_kernel, weights[0], instances),
        "flux",
        [state.shape, (radial, around)],
        state,
    )
    residual, total = call(
        functools.partial(outer_kernel, weights, instances, orders, blocks),
        "outer",
        [state.shape, (ROWS, LANES)],
        state,
        base,
        kept,
        *came,
        partner,
        *edges,
    )
    increment, blade = call(
        update_kernel,
        "update",
        [state.shape, (3, 1, node_block)],
        residual,
        step,
        total,
        *sums,
    )
    return increment, jnp.transpose(blade, (1, 0, 2))


def solution(mesh):
    in_specs = (P("inst", None, None, "space"), P("space"), P("space"), P(None, "space"))
    out_specs = (P("inst", None, None, "space"), P("inst", None, "space"))
    return jax.shard_map(
        functools.partial(per_device, 512),
        mesh=mesh,
        in_specs=in_specs,
        out_specs=out_specs,
        check_vma=False,
    )
```

```python
import functools
import math

import jax
import jax.numpy as jnp
import numpy as np
from jax import lax
from jax.experimental import pallas as pl
from jax.experimental.pallas import tpu as pltpu
from jax.sharding import PartitionSpec as P

gamma_ratio = 1.4
omega_rate = 0.5
cfl_number = 0.8

LANES = 128
ROWS = 16
EDGE = 12
PLACING = 10**10
ORDERS = ((2, 1), (1, 2))
RIDING = 8


def spectral_row(count):
    row = np.zeros((count,), np.float32)
    for shift in range(count):
        row[shift] = (-1.0) ** shift / count
        if shift != 0:
            row[shift] += 0.5 * (-1.0) ** shift / math.tan(math.pi * shift / count)
    return [float(omega_rate * value) for value in row]


def pressure_of(q0, q1, q2, q3):
    inverse = 1.0 / q0
    vr = q1 * inverse
    vc = q2 * inverse
    p = (gamma_ratio - 1.0) * (q3 - 0.5 * q0 * (vr * vr + vc * vc))
    return inverse, vr, vc, p


def own_kernel(high, riding, out):
    me = 0 if riding else lax.axis_index("space")
    out[...] = jnp.full(out.shape, me * high, jnp.int32)


def forces_kernel(node_block, own, state, cell, node, area, *outs):
    radial, around = state.shape[2:]
    faces = cell.shape[0] * LANES
    chunks = faces // LANES
    _, _, _, p = pressure_of(state[0, 0], state[0, 1], state[0, 2], state[0, 3])
    sublane = lax.broadcasted_iota(jnp.int32, (8, LANES), 0)
    picked = []
    for c in range(chunks):
        index = jnp.broadcast_to(cell[c : c + 1, :], (8, LANES))
        row = index // around
        column = index % around
        lane = column % LANES
        half = column // LANES
        total = jnp.zeros((8, LANES), jnp.float32)
        for r in range(radial // 8):
            for h in range(around // LANES):
                part = p[r * 8 : (r + 1) * 8, h * LANES : (h + 1) * LANES]
                value = jnp.take_along_axis(part, lane, axis=1, mode="promise_in_bounds")
                total += jnp.where((row == sublane + r * 8) & (half == h), value, 0.0)
        picked.append(jnp.sum(total, axis=0, keepdims=True))
    face_pressure = jnp.concatenate(picked, axis=1)
    contribution = face_pressure * area[...]
    nodes = jnp.concatenate([node[c : c + 1, :] for c in range(chunks)], axis=1)

    high = node_block // LANES
    place = nodes // LANES ^ jnp.broadcast_to(own[0:1, 0:1], nodes.shape)
    low = nodes % LANES
    pick_low = (
        lax.broadcasted_iota(jnp.int32, (LANES, faces), 0) == jnp.broadcast_to(low, (LANES, faces))
    ).astype(jnp.float32).astype(jnp.bfloat16)
    pattern = jnp.concatenate(
        [jnp.broadcast_to(contribution[k : k + 1], (high, faces)) for k in range(3)]
        + [jnp.zeros((ROWS - 3 * high, faces), jnp.float32)],
        axis=0,
    )
    first = pattern.astype(jnp.bfloat16).astype(jnp.float32)
    second = pattern - first
    place = jnp.broadcast_to(place, (ROWS, faces))
    row_high = lax.broadcasted_iota(jnp.int32, (ROWS, faces), 0) % high

    def dense(start, count):
        masks = [place == row_high + (start + b) * high for b in range(count)]
        result = None
        for part in (first, second):
            left = jnp.concatenate([jnp.where(m, part, 0.0) for m in masks], axis=0)
            product = lax.dot_general(
                left.astype(jnp.bfloat16),
                pick_low,
                (((1,), (1,)), ((), ())),
                preferred_element_type=jnp.float32,
            )
            result = product if result is None else result + product
        return result.reshape(count, ROWS, LANES)

    size = outs[0].shape[0]
    blocks = size * len(outs)
    if blocks <= 16:
        result = dense(0, blocks)
        for i, out in enumerate(outs):
            out[:, 0:ROWS, :] = result[i * size : (i + 1) * size]
            if out.shape[1] > ROWS:
                out[:, ROWS:, :] = jnp.zeros((size, out.shape[1] - ROWS, LANES), jnp.float32)
    else:
        for i, out in enumerate(outs):

            @pl.loop(0, size // 8)
            def _(g):
                out[pl.ds(g * 8, 8)] = dense(i * size + g * 8, 8)

    flat = state[0].reshape(4 * radial, around)
    turned = jnp.concatenate([flat[:, around - LANES :], flat[:, :LANES]], axis=0).T
    lane = lax.broadcasted_iota(jnp.int32, (1, LANES), 1)
    edge = jnp.where(lane < LANES // 2, turned[LANES - 1 :, :], turned[:1, :])
    if len(outs) == 1:
        outs[0][:, EDGE : EDGE + 1, :] = jnp.broadcast_to(edge[None], (blocks, 1, LANES))
    else:
        outs[0][0, EDGE : EDGE + 1, :] = edge


def halving_kernel(kept, came, *outs):
    size = outs[0].shape[0]
    for i, out in enumerate(outs):
        for b in range(size):
            out[b] = kept[i * size + b] + came[i * size + b]


def weight_from(weights, instances, source, target):
    shift = (target - source + instances) % instances
    value = weights[0]
    for i in range(1, instances):
        value = jnp.where(shift == i, weights[i], value)
    return value


def of_chip(orders):
    chip = lax.axis_index("space") // 2
    return [jnp.where(chip == 0, a, b) for a, b in zip(*orders)]


def pair_kernel(weights, instances, orders, state, partner, *outs):
    me = lax.axis_index("inst")
    first, *seconds = of_chip(orders)
    for second, out in zip(seconds, outs):
        own = weight_from(weights, instances, me, me ^ second)
        other = weight_from(weights, instances, me ^ first, me ^ second)
        out[...] = own * state[...] + other * partner[...]


def around_flux(q, vc, p):
    return (q[2], q[1] * vc, q[2] * vc + p, (q[3] + p) * vc)


def flux_kernel(weight, instances, state, base, step):
    radial, around = state.shape[2:]
    q = [state[0, c] for c in range(4)]
    inverse, vr, vc, p = pressure_of(*q)
    a = jnp.sqrt(gamma_ratio * p * inverse)
    step[...] = cfl_number / (
        jnp.abs(vr) + jnp.abs(vc) + 2.0 * a + omega_rate * instances / 2.0
    )

    def after(x):
        return pltpu.roll(x, around - 1, 1)

    def above(x):
        return pltpu.roll(x, radial - 1, 0)

    column = lax.broadcasted_iota(jnp.int32, (radial, around), 1)
    row = lax.broadcasted_iota(jnp.int32, (radial, around), 0)
    hub, tip = row == 0, row == radial - 1
    speed = jnp.abs(vc) + a
    reach = 0.5 * jnp.maximum(speed, after(speed))
    speed = jnp.abs(vr) + a
    rise = 0.5 * jnp.maximum(speed, above(speed))
    flux = around_flux(q, vc, p)
    radial_flux = (q[1], q[1] * vr + p, q[2] * vr, (q[3] + p) * vr)
    for c in range(4):
        face = 0.5 * (flux[c] + after(flux[c])) - reach * (after(q[c]) - q[c])
        face = jnp.where(column == around - 1, 0.0, face)
        residual = weight * q[c] + (face - pltpu.roll(face, 1, 1))
        wall = p if c == 1 else 0.0
        face = 0.5 * (radial_flux[c] + above(radial_flux[c])) - rise * (above(q[c]) - q[c])
        upper = jnp.where(tip, wall, face)
        lower = jnp.where(hub, wall, pltpu.roll(face, 1, 0))
        base[0, c] = residual + (upper - lower)


def outer_kernel(weights, instances, orders, state, base, kept, came, partner, *refs):
    *edges, residual, total = refs
    radial, around = state.shape[2:]
    if edges:
        before, after = (ref[0:1, :] for ref in edges)
        total[...] = kept[0] + came[0]
    else:
        blocks = came.shape[0]
        me = lax.axis_index("space")
        before = came[(me + blocks - 1) % blocks, EDGE : EDGE + 1, :]
        after = came[(me + 1) % blocks, EDGE : EDGE + 1, :]
        total[...] = jnp.sum(came[:, 0:ROWS, :], axis=0)
    me = lax.axis_index("inst")
    weight = weight_from(weights, instances, me ^ of_chip(orders)[0], me)
    lane = lax.broadcasted_iota(jnp.int32, (1, LANES), 1)
    edge = jnp.where(lane < LANES // 2, before, after)
    columns = jnp.broadcast_to(edge, (LANES, LANES)).T

    lane = lax.broadcasted_iota(jnp.int32, (radial, LANES), 1)
    left, right = lane == 0, lane == LANES - 1
    own, far = [], []
    for c in range(4):
        own.append(jnp.where(left, state[0, c, :, :LANES], state[0, c, :, around - LANES :]))
        far.append(
            jnp.where(
                right,
                columns[LANES // 2 + c * radial : LANES // 2 + (c + 1) * radial],
                columns[c * radial : (c + 1) * radial],
            )
        )
    faces, speeds = [], []
    for q in (own, far):
        inverse, _, vc, p = pressure_of(*q)
        speeds.append(jnp.abs(vc) + jnp.sqrt(gamma_ratio * p * inverse))
        faces.append(around_flux(q, vc, p))
    side = jnp.where(right, 0.5, -0.5)
    reach = 0.5 * jnp.maximum(*speeds)
    for c in range(4):
        outer = side * (faces[0][c] + faces[1][c]) - reach * (far[c] - own[c])
        outer = [jnp.where(left, outer, 0.0), jnp.where(right, outer, 0.0)]
        middle = around - 2 * LANES
        if middle:
            outer.insert(1, jnp.zeros((radial, middle), jnp.float32))
        residual[0, c] = base[0, c] + weight * partner[0, c] + jnp.concatenate(outer, axis=1)


def update_kernel(residual, step, total, *refs):
    *sums, increment, blade = refs
    high = blade.shape[2] // LANES
    for k in range(3):
        for h in range(high):
            blade[k, :, pl.ds(h * LANES, LANES)] = total[k * high + h : k * high + h + 1, :]
    for c in range(residual.shape[1]):
        change = functools.reduce(jnp.add, [ref[0, c] for ref in (residual, *sums)])
        increment[0, c] = -step[...] * change


def per_device(node_block, state, face_cell, face_node, face_area):
    blocks = lax.axis_size("space")
    instances = lax.axis_size("inst")
    radial, around = state.shape[2:]
    chunks = face_cell.shape[0] // LANES
    vmem = pl.BlockSpec(memory_space=pltpu.VMEM)
    params = pltpu.CompilerParams(vmem_limit_bytes=(4 if blocks <= 16 else 16) * 2**20)

    def swapped(value, axis, bit):
        return lax.ppermute(value, axis, [(i, i ^ bit) for i in range(lax.axis_size(axis))])

    def shifted(value, axis, s):
        count = lax.axis_size(axis)
        return lax.ppermute(value, axis, [(i, (i + s) % count) for i in range(count)])

    def call(kernel, name, shapes, *operands, flops=0, dtype=jnp.float32):
        return pl.pallas_call(
            kernel,
            out_shape=[jax.ShapeDtypeStruct(shape, dtype) for shape in shapes],
            in_specs=[vmem] * len(operands),
            out_specs=[vmem] * len(shapes),
            compiler_params=params,
            cost_estimate=pl.CostEstimate(flops=flops, bytes_accessed=0, transcendentals=0),
            name=name,
        )(*operands)

    weights = spectral_row(instances)
    def partnered(value, place):
        pairs = [
            (i * instances + n, i * instances + (n ^ orders[min(i // 2, 1)][place]))
            for i in range(blocks)
            for n in range(instances)
        ]
        return lax.ppermute(value, ("space", "inst"), pairs)

    orders = ORDERS if instances == 4 else ((1, *range(2, instances, 2)),) * 2
    partner = partnered(state, 0)

    riding = blocks == RIDING
    parts = 1 if riding else 2
    (own,) = call(
        functools.partial(own_kernel, node_block // LANES, riding),
        "own",
        [(8, LANES)],
        dtype=jnp.int32,
        flops=PLACING,
    )
    dense = call(
        functools.partial(forces_kernel, node_block),
        "face_forces",
        [(blocks // parts, 2 * ROWS if riding else ROWS, LANES)] * parts,
        own,
        state,
        face_cell.reshape(chunks, LANES),
        face_node.reshape(chunks, LANES),
        face_area,
        flops=PLACING,
    )

    edges = []
    if riding:
        kept, came = dense[0], lax.all_to_all(dense[0], "space", 0, 0, tiled=True)
    else:
        row = jnp.broadcast_to(dense[0][0, EDGE : EDGE + 1, :], (8, LANES))
        edges = [shifted(row, "space", 1), shifted(row, "space", blocks - 1)]
        size = blocks // 2
        kept, came = dense[0], swapped(dense[1], "space", size)
        while size > 1:
            size //= 2
            shapes = [(size, ROWS, LANES)] * 2
            kept, sent = call(halving_kernel, "halving", shapes, kept, came)
            came = swapped(sent, "space", size)

    sums = call(
        functools.partial(pair_kernel, weights, instances, orders),
        "pair_sums",
        [state.shape] * (len(orders[0]) - 1),
        state,
        partner,
        flops=PLACING,
    )
    sums = [partnered(value, i) for i, value in enumerate(sums, 1)]

    base, step = call(
        functools.partial(flux_kernel, weights[0], instances),
        "flux",
        [state.shape, (radial, around)],
        state,
    )
    residual, total = call(
        functools.partial(outer_kernel, weights, instances, orders),
        "outer",
        [state.shape, (ROWS, LANES)],
        state,
        base,
        kept,
        came,
        partner,
        *edges,
    )
    increment, blade = call(
        update_kernel,
        "update",
        [state.shape, (3, 1, node_block)],
        residual,
        step,
        total,
        *sums,
    )
    return increment, jnp.transpose(blade, (1, 0, 2))


def solution(mesh):
    in_specs = (P("inst", None, None, "space"), P("space"), P("space"), P(None, "space"))
    out_specs = (P("inst", None, None, "space"), P("inst", None, "space"))
    return jax.shard_map(
        functools.partial(per_device, 512),
        mesh=mesh,
        in_specs=in_specs,
        out_specs=out_specs,
        check_vma=False,
    )
```

```python
import functools
import math

import jax
import jax.numpy as jnp
import numpy as np
from jax import lax
from jax.experimental import pallas as pl
from jax.experimental.pallas import tpu as pltpu
from jax.sharding import PartitionSpec as P

gamma_ratio = 1.4
omega_rate = 0.5
cfl_number = 0.8

LANES = 128
ROWS = 16
EDGE = 12
PLACING = 10**10
ORDERS = ((3, 1), (1, 2))
RIDING = 8


def spectral_row(count):
    row = np.zeros((count,), np.float32)
    for shift in range(count):
        row[shift] = (-1.0) ** shift / count
        if shift != 0:
            row[shift] += 0.5 * (-1.0) ** shift / math.tan(math.pi * shift / count)
    return [float(omega_rate * value) for value in row]


def pressure_of(q0, q1, q2, q3):
    inverse = 1.0 / q0
    vr = q1 * inverse
    vc = q2 * inverse
    p = (gamma_ratio - 1.0) * (q3 - 0.5 * q0 * (vr * vr + vc * vc))
    return inverse, vr, vc, p


def own_kernel(high, out):
    out[...] = jnp.full(out.shape, lax.axis_index("space") * high, jnp.int32)


def forces_kernel(node_block, own, state, cell, node, area, *outs):
    radial, around = state.shape[2:]
    faces = cell.shape[0] * LANES
    chunks = faces // LANES
    _, _, _, p = pressure_of(state[0, 0], state[0, 1], state[0, 2], state[0, 3])
    sublane = lax.broadcasted_iota(jnp.int32, (8, LANES), 0)
    picked = []
    for c in range(chunks):
        index = jnp.broadcast_to(cell[c : c + 1, :], (8, LANES))
        row = index // around
        column = index % around
        lane = column % LANES
        half = column // LANES
        total = jnp.zeros((8, LANES), jnp.float32)
        for r in range(radial // 8):
            for h in range(around // LANES):
                part = p[r * 8 : (r + 1) * 8, h * LANES : (h + 1) * LANES]
                value = jnp.take_along_axis(part, lane, axis=1, mode="promise_in_bounds")
                total += jnp.where((row == sublane + r * 8) & (half == h), value, 0.0)
        picked.append(jnp.sum(total, axis=0, keepdims=True))
    face_pressure = jnp.concatenate(picked, axis=1)
    contribution = face_pressure * area[...]
    nodes = jnp.concatenate([node[c : c + 1, :] for c in range(chunks)], axis=1)

    high = node_block // LANES
    place = nodes // LANES ^ jnp.broadcast_to(own[0:1, 0:1], nodes.shape)
    low = nodes % LANES
    pick_low = (
        lax.broadcasted_iota(jnp.int32, (LANES, faces), 0) == jnp.broadcast_to(low, (LANES, faces))
    ).astype(jnp.float32).astype(jnp.bfloat16)
    pattern = jnp.concatenate(
        [jnp.broadcast_to(contribution[k : k + 1], (high, faces)) for k in range(3)]
        + [jnp.zeros((ROWS - 3 * high, faces), jnp.float32)],
        axis=0,
    )
    first = pattern.astype(jnp.bfloat16).astype(jnp.float32)
    second = pattern - first
    place = jnp.broadcast_to(place, (ROWS, faces))
    row_high = lax.broadcasted_iota(jnp.int32, (ROWS, faces), 0) % high

    def dense(start, count):
        masks = [place == row_high + (start + b) * high for b in range(count)]
        result = None
        for part in (first, second):
            left = jnp.concatenate([jnp.where(m, part, 0.0) for m in masks], axis=0)
            product = lax.dot_general(
                left.astype(jnp.bfloat16),
                pick_low,
                (((1,), (1,)), ((), ())),
                preferred_element_type=jnp.float32,
            )
            result = product if result is None else result + product
        return result.reshape(count, ROWS, LANES)

    ordered = outs[:1] + outs[:0:-1]
    size = outs[0].shape[0]
    blocks = size * len(outs)
    if blocks <= 16:
        result = dense(0, blocks)
        for i, out in enumerate(ordered):
            out[...] = result[i * size : (i + 1) * size]
    else:
        for i, out in enumerate(ordered):

            @pl.loop(0, size // 8)
            def _(g):
                out[pl.ds(g * 8, 8)] = dense(i * size + g * 8, 8)

    flat = state[0].reshape(4 * radial, around)
    turned = jnp.concatenate([flat[:, around - LANES :], flat[:, :LANES]], axis=0).T
    lane = lax.broadcasted_iota(jnp.int32, (1, LANES), 1)
    edge = jnp.where(lane < LANES // 2, turned[LANES - 1 :, :], turned[:1, :])
    for out in outs:
        out[0, EDGE : EDGE + 1, :] = edge


def halving_kernel(arrived, riding, *refs):
    outs = refs[arrived:]
    size = outs[0].shape[0]
    for i, out in enumerate(outs):
        for b in range(size):
            out[b] = functools.reduce(jnp.add, [ref[i * size + b] for ref in refs[:arrived]])
        if riding:
            for j, ref in enumerate(refs[:arrived]):
                out[0, EDGE + j : EDGE + j + 1, :] = ref[0, EDGE : EDGE + 1, :]


def weight_from(weights, instances, source, target):
    shift = (target - source + instances) % instances
    value = weights[0]
    for i in range(1, instances):
        value = jnp.where(shift == i, weights[i], value)
    return value


def of_chip(orders):
    chip = lax.axis_index("space") // 2
    return [jnp.where(chip == 0, a, b) for a, b in zip(*orders)]


def pair_kernel(weights, instances, orders, state, partner, *outs):
    me = lax.axis_index("inst")
    first, *seconds = of_chip(orders)
    for second, out in zip(seconds, outs):
        own = weight_from(weights, instances, me, me ^ second)
        other = weight_from(weights, instances, me ^ first, me ^ second)
        out[...] = own * state[...] + other * partner[...]


def around_flux(q, vc, p):
    return (q[2], q[1] * vc, q[2] * vc + p, (q[3] + p) * vc)


def flux_kernel(weight, instances, state, base, step):
    radial, around = state.shape[2:]
    q = [state[0, c] for c in range(4)]
    inverse, vr, vc, p = pressure_of(*q)
    a = jnp.sqrt(gamma_ratio * p * inverse)
    step[...] = cfl_number / (
        jnp.abs(vr) + jnp.abs(vc) + 2.0 * a + omega_rate * instances / 2.0
    )

    def after(x):
        return pltpu.roll(x, around - 1, 1)

    def above(x):
        return pltpu.roll(x, radial - 1, 0)

    column = lax.broadcasted_iota(jnp.int32, (radial, around), 1)
    row = lax.broadcasted_iota(jnp.int32, (radial, around), 0)
    hub, tip = row == 0, row == radial - 1
    speed = jnp.abs(vc) + a
    reach = 0.5 * jnp.maximum(speed, after(speed))
    speed = jnp.abs(vr) + a
    rise = 0.5 * jnp.maximum(speed, above(speed))
    flux = around_flux(q, vc, p)
    radial_flux = (q[1], q[1] * vr + p, q[2] * vr, (q[3] + p) * vr)
    for c in range(4):
        face = 0.5 * (flux[c] + after(flux[c])) - reach * (after(q[c]) - q[c])
        face = jnp.where(column == around - 1, 0.0, face)
        residual = weight * q[c] + (face - pltpu.roll(face, 1, 1))
        wall = p if c == 1 else 0.0
        face = 0.5 * (radial_flux[c] + above(radial_flux[c])) - rise * (above(q[c]) - q[c])
        upper = jnp.where(tip, wall, face)
        lower = jnp.where(hub, wall, pltpu.roll(face, 1, 0))
        base[0, c] = residual + (upper - lower)


def outer_kernel(weights, instances, orders, blocks, state, base, kept, came, partner, *refs):
    *edges, residual, total = refs
    radial, around = state.shape[2:]
    if blocks == RIDING:
        me = lax.axis_index("space")
        known = [kept[0, EDGE:, :], came[0, EDGE:, :]]
        known = jnp.concatenate(known, axis=0)
        row = lax.broadcasted_iota(jnp.int32, known.shape, 0)

        def edge_of(device):
            relative = device ^ me
            half = RIDING // 2
            place = (half - relative // 2) % half + (relative % 2) * half
            return jnp.sum(jnp.where(row == place, known, 0.0), axis=0, keepdims=True)

        before = edge_of((me + blocks - 1) % blocks)
        after = edge_of((me + 1) % blocks)
    else:
        before, after = (ref[0:1, :] for ref in edges)
    me = lax.axis_index("inst")
    weight = weight_from(weights, instances, me ^ of_chip(orders)[0], me)
    lane = lax.broadcasted_iota(jnp.int32, (1, LANES), 1)
    edge = jnp.where(lane < LANES // 2, before, after)
    columns = jnp.broadcast_to(edge, (LANES, LANES)).T

    lane = lax.broadcasted_iota(jnp.int32, (radial, LANES), 1)
    left, right = lane == 0, lane == LANES - 1
    own, far = [], []
    for c in range(4):
        own.append(jnp.where(left, state[0, c, :, :LANES], state[0, c, :, around - LANES :]))
        far.append(
            jnp.where(
                right,
                columns[LANES // 2 + c * radial : LANES // 2 + (c + 1) * radial],
                columns[c * radial : (c + 1) * radial],
            )
        )
    faces, speeds = [], []
    for q in (own, far):
        inverse, _, vc, p = pressure_of(*q)
        speeds.append(jnp.abs(vc) + jnp.sqrt(gamma_ratio * p * inverse))
        faces.append(around_flux(q, vc, p))
    side = jnp.where(right, 0.5, -0.5)
    reach = 0.5 * jnp.maximum(*speeds)
    for c in range(4):
        outer = side * (faces[0][c] + faces[1][c]) - reach * (far[c] - own[c])
        outer = [jnp.where(left, outer, 0.0), jnp.where(right, outer, 0.0)]
        middle = around - 2 * LANES
        if middle:
            outer.insert(1, jnp.zeros((radial, middle), jnp.float32))
        residual[0, c] = base[0, c] + weight * partner[0, c] + jnp.concatenate(outer, axis=1)

    total[...] = kept[0] + came[0]


def update_kernel(residual, step, total, *refs):
    *sums, increment, blade = refs
    high = blade.shape[2] // LANES
    for k in range(3):
        for h in range(high):
            blade[k, :, pl.ds(h * LANES, LANES)] = total[k * high + h : k * high + h + 1, :]
    for c in range(residual.shape[1]):
        change = functools.reduce(jnp.add, [ref[0, c] for ref in (residual, *sums)])
        increment[0, c] = -step[...] * change


def per_device(node_block, state, face_cell, face_node, face_area):
    blocks = lax.axis_size("space")
    instances = lax.axis_size("inst")
    radial, around = state.shape[2:]
    chunks = face_cell.shape[0] // LANES
    vmem = pl.BlockSpec(memory_space=pltpu.VMEM)
    params = pltpu.CompilerParams(vmem_limit_bytes=(4 if blocks <= 16 else 16) * 2**20)

    def swapped(value, axis, bit):
        return lax.ppermute(value, axis, [(i, i ^ bit) for i in range(lax.axis_size(axis))])

    def shifted(value, axis, s):
        count = lax.axis_size(axis)
        return lax.ppermute(value, axis, [(i, (i + s) % count) for i in range(count)])

    def exchanged(sent, size):
        return [
            swapped(value, "space", (len(sent) - i) * size) for i, value in enumerate(sent)
        ]

    def call(kernel, name, shapes, *operands, flops=0, dtype=jnp.float32):
        return pl.pallas_call(
            kernel,
            out_shape=[jax.ShapeDtypeStruct(shape, dtype) for shape in shapes],
            in_specs=[vmem] * len(operands),
            out_specs=[vmem] * len(shapes),
            compiler_params=params,
            cost_estimate=pl.CostEstimate(flops=flops, bytes_accessed=0, transcendentals=0),
            name=name,
        )(*operands)

    weights = spectral_row(instances)
    def partnered(value, place):
        pairs = [
            (i * instances + n, i * instances + (n ^ orders[min(i // 2, 1)][place]))
            for i in range(blocks)
            for n in range(instances)
        ]
        return lax.ppermute(value, ("space", "inst"), pairs)

    orders = ORDERS if instances == 4 else ((1, *range(2, instances, 2)),) * 2
    partner = partnered(state, 0)

    riding = blocks == RIDING
    steps = [4, 2] if riding else [2] * (blocks.bit_length() - 1)
    size = blocks // steps[0]
    (own,) = call(
        functools.partial(own_kernel, node_block // LANES),
        "own",
        [(8, LANES)],
        dtype=jnp.int32,
        flops=PLACING,
    )
    kept, *sent = call(
        functools.partial(forces_kernel, node_block),
        "face_forces",
        [(size, ROWS, LANES)] * steps[0],
        own,
        state,
        face_cell.reshape(chunks, LANES),
        face_node.reshape(chunks, LANES),
        face_area,
        flops=PLACING,
    )

    edges = []
    if not riding:
        row = jnp.broadcast_to(kept[0, EDGE : EDGE + 1, :], (8, LANES))
        edges = [shifted(row, "space", 1), shifted(row, "space", blocks - 1)]

    came = exchanged(sent, size)
    sums = call(
        functools.partial(pair_kernel, weights, instances, orders),
        "pair_sums",
        [state.shape] * (len(orders[0]) - 1),
        state,
        partner,
        flops=PLACING,
    )
    sums = [partnered(value, i) for i, value in enumerate(sums, 1)]

    for step in steps[1:]:
        size //= step
        kept, *sent = call(
            functools.partial(halving_kernel, 1 + len(came), riding),
            "halving",
            [(size, ROWS, LANES)] * step,
            kept,
            *came,
            flops=PLACING,
        )
        came = exchanged(sent, size)

    base, step = call(
        functools.partial(flux_kernel, weights[0], instances),
        "flux",
        [state.shape, (radial, around)],
        state,
    )
    residual, total = call(
        functools.partial(outer_kernel, weights, instances, orders, blocks),
        "outer",
        [state.shape, (ROWS, LANES)],
        state,
        base,
        kept,
        *came,
        partner,
        *edges,
    )
    increment, blade = call(
        update_kernel,
        "update",
        [state.shape, (3, 1, node_block)],
        residual,
        step,
        total,
        *sums,
    )
    return increment, jnp.transpose(blade, (1, 0, 2))


def solution(mesh):
    in_specs = (P("inst", None, None, "space"), P("space"), P("space"), P(None, "space"))
    out_specs = (P("inst", None, None, "space"), P("inst", None, "space"))
    return jax.shard_map(
        functools.partial(per_device, 512),
        mesh=mesh,
        in_specs=in_specs,
        out_specs=out_specs,
        check_vma=False,
    )
```

```python
import functools
import math

import jax
import jax.numpy as jnp
import numpy as np
from jax import lax
from jax.experimental import pallas as pl
from jax.experimental.pallas import tpu as pltpu
from jax.sharding import PartitionSpec as P

gamma_ratio = 1.4
omega_rate = 0.5
cfl_number = 0.8

LANES = 128
ROWS = 16
EDGE = 12
PLACING = 10**10
ORDERS = ((2, 1), (1, 2))
RIDING = 8


def spectral_row(count):
    row = np.zeros((count,), np.float32)
    for shift in range(count):
        row[shift] = (-1.0) ** shift / count
        if shift != 0:
            row[shift] += 0.5 * (-1.0) ** shift / math.tan(math.pi * shift / count)
    return [float(omega_rate * value) for value in row]


def pressure_of(q0, q1, q2, q3):
    inverse = 1.0 / q0
    vr = q1 * inverse
    vc = q2 * inverse
    p = (gamma_ratio - 1.0) * (q3 - 0.5 * q0 * (vr * vr + vc * vc))
    return inverse, vr, vc, p


def own_kernel(high, out):
    out[...] = jnp.full(out.shape, lax.axis_index("space") * high, jnp.int32)


def forces_kernel(node_block, own, state, cell, node, area, *outs):
    radial, around = state.shape[2:]
    faces = cell.shape[0] * LANES
    chunks = faces // LANES
    _, _, _, p = pressure_of(state[0, 0], state[0, 1], state[0, 2], state[0, 3])
    sublane = lax.broadcasted_iota(jnp.int32, (8, LANES), 0)
    picked = []
    for c in range(chunks):
        index = jnp.broadcast_to(cell[c : c + 1, :], (8, LANES))
        row = index // around
        column = index % around
        lane = column % LANES
        half = column // LANES
        total = jnp.zeros((8, LANES), jnp.float32)
        for r in range(radial // 8):
            for h in range(around // LANES):
                part = p[r * 8 : (r + 1) * 8, h * LANES : (h + 1) * LANES]
                value = jnp.take_along_axis(part, lane, axis=1, mode="promise_in_bounds")
                total += jnp.where((row == sublane + r * 8) & (half == h), value, 0.0)
        picked.append(jnp.sum(total, axis=0, keepdims=True))
    face_pressure = jnp.concatenate(picked, axis=1)
    contribution = face_pressure * area[...]
    nodes = jnp.concatenate([node[c : c + 1, :] for c in range(chunks)], axis=1)

    high = node_block // LANES
    place = nodes // LANES ^ jnp.broadcast_to(own[0:1, 0:1], nodes.shape)
    low = nodes % LANES
    pick_low = (
        lax.broadcasted_iota(jnp.int32, (LANES, faces), 0) == jnp.broadcast_to(low, (LANES, faces))
    ).astype(jnp.float32).astype(jnp.bfloat16)
    pattern = jnp.concatenate(
        [jnp.broadcast_to(contribution[k : k + 1], (high, faces)) for k in range(3)]
        + [jnp.zeros((ROWS - 3 * high, faces), jnp.float32)],
        axis=0,
    )
    first = pattern.astype(jnp.bfloat16).astype(jnp.float32)
    second = pattern - first
    place = jnp.broadcast_to(place, (ROWS, faces))
    row_high = lax.broadcasted_iota(jnp.int32, (ROWS, faces), 0) % high

    def dense(start, count):
        masks = [place == row_high + (start + b) * high for b in range(count)]
        result = None
        for part in (first, second):
            left = jnp.concatenate([jnp.where(m, part, 0.0) for m in masks], axis=0)
            product = lax.dot_general(
                left.astype(jnp.bfloat16),
                pick_low,
                (((1,), (1,)), ((), ())),
                preferred_element_type=jnp.float32,
            )
            result = product if result is None else result + product
        return result.reshape(count, ROWS, LANES)

    ordered = outs[:1] + outs[:0:-1]
    size = outs[0].shape[0]
    blocks = size * len(outs)
    if blocks <= 16:
        result = dense(0, blocks)
        for i, out in enumerate(ordered):
            out[...] = result[i * size : (i + 1) * size]
    else:
        for i, out in enumerate(ordered):

            @pl.loop(0, size // 8)
            def _(g):
                out[pl.ds(g * 8, 8)] = dense(i * size + g * 8, 8)

    flat = state[0].reshape(4 * radial, around)
    turned = jnp.concatenate([flat[:, around - LANES :], flat[:, :LANES]], axis=0).T
    lane = lax.broadcasted_iota(jnp.int32, (1, LANES), 1)
    edge = jnp.where(lane < LANES // 2, turned[LANES - 1 :, :], turned[:1, :])
    for out in outs:
        out[0, EDGE : EDGE + 1, :] = edge


def halving_kernel(arrived, riding, *refs):
    outs = refs[arrived:]
    size = outs[0].shape[0]
    for i, out in enumerate(outs):
        for b in range(size):
            out[b] = functools.reduce(jnp.add, [ref[i * size + b] for ref in refs[:arrived]])
        if riding:
            for j, ref in enumerate(refs[:arrived]):
                out[0, EDGE + j : EDGE + j + 1, :] = ref[0, EDGE : EDGE + 1, :]


def weight_from(weights, instances, source, target):
    shift = (target - source + instances) % instances
    value = weights[0]
    for i in range(1, instances):
        value = jnp.where(shift == i, weights[i], value)
    return value


def of_chip(orders):
    chip = lax.axis_index("space") // 2
    return [jnp.where(chip % 2 == 0, a, b) for a, b in zip(*orders)]


def pair_kernel(weights, instances, orders, state, partner, *outs):
    me = lax.axis_index("inst")
    first, *seconds = of_chip(orders)
    for second, out in zip(seconds, outs):
        own = weight_from(weights, instances, me, me ^ second)
        other = weight_from(weights, instances, me ^ first, me ^ second)
        out[...] = own * state[...] + other * partner[...]


def around_flux(q, vc, p):
    return (q[2], q[1] * vc, q[2] * vc + p, (q[3] + p) * vc)


def flux_kernel(weight, instances, state, base, step):
    radial, around = state.shape[2:]
    q = [state[0, c] for c in range(4)]
    inverse, vr, vc, p = pressure_of(*q)
    a = jnp.sqrt(gamma_ratio * p * inverse)
    step[...] = cfl_number / (
        jnp.abs(vr) + jnp.abs(vc) + 2.0 * a + omega_rate * instances / 2.0
    )

    def after(x):
        return pltpu.roll(x, around - 1, 1)

    def above(x):
        return pltpu.roll(x, radial - 1, 0)

    column = lax.broadcasted_iota(jnp.int32, (radial, around), 1)
    row = lax.broadcasted_iota(jnp.int32, (radial, around), 0)
    hub, tip = row == 0, row == radial - 1
    speed = jnp.abs(vc) + a
    reach = 0.5 * jnp.maximum(speed, after(speed))
    speed = jnp.abs(vr) + a
    rise = 0.5 * jnp.maximum(speed, above(speed))
    flux = around_flux(q, vc, p)
    radial_flux = (q[1], q[1] * vr + p, q[2] * vr, (q[3] + p) * vr)
    for c in range(4):
        face = 0.5 * (flux[c] + after(flux[c])) - reach * (after(q[c]) - q[c])
        face = jnp.where(column == around - 1, 0.0, face)
        residual = weight * q[c] + (face - pltpu.roll(face, 1, 1))
        wall = p if c == 1 else 0.0
        face = 0.5 * (radial_flux[c] + above(radial_flux[c])) - rise * (above(q[c]) - q[c])
        upper = jnp.where(tip, wall, face)
        lower = jnp.where(hub, wall, pltpu.roll(face, 1, 0))
        base[0, c] = residual + (upper - lower)


def outer_kernel(weights, instances, orders, blocks, state, base, kept, came, partner, *refs):
    *edges, residual, total = refs
    radial, around = state.shape[2:]
    if blocks == RIDING:
        me = lax.axis_index("space")
        known = [kept[0, EDGE:, :], came[0, EDGE:, :]]
        known = jnp.concatenate(known, axis=0)
        row = lax.broadcasted_iota(jnp.int32, known.shape, 0)

        def edge_of(device):
            relative = device ^ me
            half = RIDING // 2
            place = (half - relative // 2) % half + (relative % 2) * half
            return jnp.sum(jnp.where(row == place, known, 0.0), axis=0, keepdims=True)

        before = edge_of((me + blocks - 1) % blocks)
        after = edge_of((me + 1) % blocks)
    else:
        before, after = (ref[0:1, :] for ref in edges)
    me = lax.axis_index("inst")
    weight = weight_from(weights, instances, me ^ of_chip(orders)[0], me)
    lane = lax.broadcasted_iota(jnp.int32, (1, LANES), 1)
    edge = jnp.where(lane < LANES // 2, before, after)
    columns = jnp.broadcast_to(edge, (LANES, LANES)).T

    lane = lax.broadcasted_iota(jnp.int32, (radial, LANES), 1)
    left, right = lane == 0, lane == LANES - 1
    own, far = [], []
    for c in range(4):
        own.append(jnp.where(left, state[0, c, :, :LANES], state[0, c, :, around - LANES :]))
        far.append(
            jnp.where(
                right,
                columns[LANES // 2 + c * radial : LANES // 2 + (c + 1) * radial],
                columns[c * radial : (c + 1) * radial],
            )
        )
    faces, speeds = [], []
    for q in (own, far):
        inverse, _, vc, p = pressure_of(*q)
        speeds.append(jnp.abs(vc) + jnp.sqrt(gamma_ratio * p * inverse))
        faces.append(around_flux(q, vc, p))
    side = jnp.where(right, 0.5, -0.5)
    reach = 0.5 * jnp.maximum(*speeds)
    for c in range(4):
        outer = side * (faces[0][c] + faces[1][c]) - reach * (far[c] - own[c])
        outer = [jnp.where(left, outer, 0.0), jnp.where(right, outer, 0.0)]
        middle = around - 2 * LANES
        if middle:
            outer.insert(1, jnp.zeros((radial, middle), jnp.float32))
        residual[0, c] = base[0, c] + weight * partner[0, c] + jnp.concatenate(outer, axis=1)

    total[...] = kept[0] + came[0]


def update_kernel(residual, step, total, *refs):
    *sums, increment, blade = refs
    high = blade.shape[2] // LANES
    for k in range(3):
        for h in range(high):
            blade[k, :, pl.ds(h * LANES, LANES)] = total[k * high + h : k * high + h + 1, :]
    for c in range(residual.shape[1]):
        change = functools.reduce(jnp.add, [ref[0, c] for ref in (residual, *sums)])
        increment[0, c] = -step[...] * change


def per_device(node_block, state, face_cell, face_node, face_area):
    blocks = lax.axis_size("space")
    instances = lax.axis_size("inst")
    radial, around = state.shape[2:]
    chunks = face_cell.shape[0] // LANES
    vmem = pl.BlockSpec(memory_space=pltpu.VMEM)
    params = pltpu.CompilerParams(vmem_limit_bytes=(4 if blocks <= 16 else 16) * 2**20)

    def swapped(value, axis, bit):
        return lax.ppermute(value, axis, [(i, i ^ bit) for i in range(lax.axis_size(axis))])

    def shifted(value, axis, s):
        count = lax.axis_size(axis)
        return lax.ppermute(value, axis, [(i, (i + s) % count) for i in range(count)])

    def exchanged(sent, size):
        return [
            swapped(value, "space", (len(sent) - i) * size) for i, value in enumerate(sent)
        ]

    def call(kernel, name, shapes, *operands, flops=0, dtype=jnp.float32):
        return pl.pallas_call(
            kernel,
            out_shape=[jax.ShapeDtypeStruct(shape, dtype) for shape in shapes],
            in_specs=[vmem] * len(operands),
            out_specs=[vmem] * len(shapes),
            compiler_params=params,
            cost_estimate=pl.CostEstimate(flops=flops, bytes_accessed=0, transcendentals=0),
            name=name,
        )(*operands)

    weights = spectral_row(instances)
    def partnered(value, place):
        pairs = [
            (i * instances + n, i * instances + (n ^ orders[i // 2 % 2][place]))
            for i in range(blocks)
            for n in range(instances)
        ]
        return lax.ppermute(value, ("space", "inst"), pairs)

    orders = ORDERS if instances == 4 else ((1, *range(2, instances, 2)),) * 2
    partner = partnered(state, 0)

    riding = blocks == RIDING
    steps = [4, 2] if riding else [2] * (blocks.bit_length() - 1)
    size = blocks // steps[0]
    (own,) = call(
        functools.partial(own_kernel, node_block // LANES),
        "own",
        [(8, LANES)],
        dtype=jnp.int32,
        flops=PLACING,
    )
    kept, *sent = call(
        functools.partial(forces_kernel, node_block),
        "face_forces",
        [(size, ROWS, LANES)] * steps[0],
        own,
        state,
        face_cell.reshape(chunks, LANES),
        face_node.reshape(chunks, LANES),
        face_area,
        flops=PLACING,
    )

    edges = []
    if not riding:
        row = jnp.broadcast_to(kept[0, EDGE : EDGE + 1, :], (8, LANES))
        edges = [shifted(row, "space", 1), shifted(row, "space", blocks - 1)]

    came = exchanged(sent, size)
    sums = call(
        functools.partial(pair_kernel, weights, instances, orders),
        "pair_sums",
        [state.shape] * (len(orders[0]) - 1),
        state,
        partner,
        flops=PLACING,
    )
    sums = [partnered(value, i) for i, value in enumerate(sums, 1)]

    for step in steps[1:]:
        size //= step
        kept, *sent = call(
            functools.partial(halving_kernel, 1 + len(came), riding),
            "halving",
            [(size, ROWS, LANES)] * step,
            kept,
            *came,
            flops=PLACING,
        )
        came = exchanged(sent, size)

    base, step = call(
        functools.partial(flux_kernel, weights[0], instances),
        "flux",
        [state.shape, (radial, around)],
        state,
    )
    residual, total = call(
        functools.partial(outer_kernel, weights, instances, orders, blocks),
        "outer",
        [state.shape, (ROWS, LANES)],
        state,
        base,
        kept,
        *came,
        partner,
        *edges,
    )
    increment, blade = call(
        update_kernel,
        "update",
        [state.shape, (3, 1, node_block)],
        residual,
        step,
        total,
        *sums,
    )
    return increment, jnp.transpose(blade, (1, 0, 2))


def solution(mesh):
    in_specs = (P("inst", None, None, "space"), P("space"), P("space"), P(None, "space"))
    out_specs = (P("inst", None, None, "space"), P("inst", None, "space"))
    return jax.shard_map(
        functools.partial(per_device, 512),
        mesh=mesh,
        in_specs=in_specs,
        out_specs=out_specs,
        check_vma=False,
    )
```

```python
import functools
import math

import jax
import jax.numpy as jnp
import numpy as np
from jax import lax
from jax.experimental import pallas as pl
from jax.experimental.pallas import tpu as pltpu
from jax.sharding import PartitionSpec as P

gamma_ratio = 1.4
omega_rate = 0.5
cfl_number = 0.8

LANES = 128
ROWS = 16
EDGE = 12
PLACING = 10**10
ORDERS = ((2, 1), (1, 2))
RIDING = 8


def spectral_row(count):
    row = np.zeros((count,), np.float32)
    for shift in range(count):
        row[shift] = (-1.0) ** shift / count
        if shift != 0:
            row[shift] += 0.5 * (-1.0) ** shift / math.tan(math.pi * shift / count)
    return [float(omega_rate * value) for value in row]


def pressure_of(q0, q1, q2, q3):
    inverse = 1.0 / q0
    vr = q1 * inverse
    vc = q2 * inverse
    p = (gamma_ratio - 1.0) * (q3 - 0.5 * q0 * (vr * vr + vc * vc))
    return inverse, vr, vc, p


def own_kernel(high, out):
    out[...] = jnp.full(out.shape, lax.axis_index("space") * high, jnp.int32)


def split(value, size):
    return value >> (size.bit_length() - 1), value & (size - 1)


def forces_kernel(node_block, own, state, cell, node, area, *outs):
    radial, around = state.shape[2:]
    faces = cell.shape[0] * LANES
    chunks = faces // LANES
    _, _, _, p = pressure_of(state[0, 0], state[0, 1], state[0, 2], state[0, 3])
    sublane = lax.broadcasted_iota(jnp.int32, (8, LANES), 0)
    picked = []
    for c in range(chunks):
        tile, lane = split(jnp.broadcast_to(cell[c : c + 1, :], (8, LANES)), LANES)
        total = jnp.zeros((8, LANES), jnp.float32)
        for r in range(radial // 8):
            for h in range(around // LANES):
                part = p[r * 8 : (r + 1) * 8, h * LANES : (h + 1) * LANES]
                value = jnp.take_along_axis(part, lane, axis=1, mode="promise_in_bounds")
                place = (sublane + r * 8) * (around // LANES) + h
                total += jnp.where(tile == place, value, 0.0)
        picked.append(jnp.sum(total, axis=0, keepdims=True))
    face_pressure = jnp.concatenate(picked, axis=1)
    contribution = face_pressure * area[...]
    nodes = jnp.concatenate([node[c : c + 1, :] for c in range(chunks)], axis=1)

    high = node_block // LANES
    place, low = split(nodes, LANES)
    place = place ^ jnp.broadcast_to(own[0:1, 0:1], nodes.shape)
    pick_low = (
        lax.broadcasted_iota(jnp.int32, (LANES, faces), 0) == jnp.broadcast_to(low, (LANES, faces))
    ).astype(jnp.float32).astype(jnp.bfloat16)

    row = lax.broadcasted_iota(jnp.int32, (8, faces), 0)
    x, y, z = (jnp.broadcast_to(contribution[k : k + 1], (8, faces)) for k in range(3))
    groups = []
    for pattern in (jnp.where(row < high, x, y), jnp.where(row < high, z, 0.0)):
        first = pattern.astype(jnp.bfloat16).astype(jnp.float32)
        groups.append((first, pattern - first))
    away = jnp.broadcast_to(place, (8, faces)) - (row & (high - 1))

    def dense(start, count):
        masks = [away == (start + b) * high for b in range(count)]
        left = [jnp.where(m, g[i], 0.0) for i in range(2) for m in masks for g in groups]
        product = lax.dot_general(
            jnp.concatenate(left, axis=0).astype(jnp.bfloat16),
            pick_low,
            (((1,), (1,)), ((), ())),
            preferred_element_type=jnp.float32,
        )
        rows = count * ROWS
        return (product[:rows] + product[rows:]).reshape(count, ROWS, LANES)

    ordered = outs[:1] + outs[:0:-1]
    size = outs[0].shape[0]
    blocks = size * len(outs)
    if blocks <= 16:
        result = dense(0, blocks)
        for i, out in enumerate(ordered):
            out[...] = result[i * size : (i + 1) * size]
    else:
        for i, out in enumerate(ordered):

            @pl.loop(0, size // 8)
            def _(g):
                out[pl.ds(g * 8, 8)] = dense(i * size + g * 8, 8)

    lane = lax.broadcasted_iota(jnp.int32, (8, LANES), 1)
    columns = jnp.zeros((8, LANES), jnp.float32)
    for i, column in enumerate((around - 1, 0)):
        tile, index = divmod(column, LANES)
        index = jnp.full((8, LANES), index, jnp.int32)
        for c in range(4):
            for r in range(radial // 8):
                part = state[0, c, r * 8 : (r + 1) * 8, tile * LANES : (tile + 1) * LANES]
                value = jnp.take_along_axis(part, index, axis=1, mode="promise_in_bounds")
                place = (i * 4 + c) * radial + r * 8
                columns = jnp.where(lane == sublane + place, value, columns)
    edge = jnp.sum(columns, axis=0, keepdims=True)
    for out in outs:
        out[0, EDGE : EDGE + 1, :] = edge


def halving_kernel(arrived, riding, *refs):
    outs = refs[arrived:]
    size = outs[0].shape[0]
    for i, out in enumerate(outs):
        for b in range(size):
            out[b] = functools.reduce(jnp.add, [ref[i * size + b] for ref in refs[:arrived]])
        if riding:
            for j, ref in enumerate(refs[:arrived]):
                out[0, EDGE + j : EDGE + j + 1, :] = ref[0, EDGE : EDGE + 1, :]


def weight_from(weights, instances, source, target):
    shift = (target - source + instances) % instances
    value = weights[0]
    for i in range(1, instances):
        value = jnp.where(shift == i, weights[i], value)
    return value


def of_chip(orders):
    chip = lax.axis_index("space") // 2
    return [jnp.where(chip % 2 == 0, a, b) for a, b in zip(*orders)]


def pair_kernel(weights, instances, orders, state, partner, *outs):
    me = lax.axis_index("inst")
    first, *seconds = of_chip(orders)
    for second, out in zip(seconds, outs):
        own = weight_from(weights, instances, me, me ^ second)
        other = weight_from(weights, instances, me ^ first, me ^ second)
        out[...] = own * state[...] + other * partner[...]


def around_flux(q, vc, p):
    return (q[2], q[1] * vc, q[2] * vc + p, (q[3] + p) * vc)


def flux_kernel(weight, instances, state, base, step):
    radial, around = state.shape[2:]
    q = [state[0, c] for c in range(4)]
    inverse, vr, vc, p = pressure_of(*q)
    a = jnp.sqrt(gamma_ratio * p * inverse)
    step[...] = cfl_number / (
        jnp.abs(vr) + jnp.abs(vc) + 2.0 * a + omega_rate * instances / 2.0
    )

    def after(x):
        return pltpu.roll(x, around - 1, 1)

    def above(x):
        return pltpu.roll(x, radial - 1, 0)

    column = lax.broadcasted_iota(jnp.int32, (radial, around), 1)
    row = lax.broadcasted_iota(jnp.int32, (radial, around), 0)
    hub, tip = row == 0, row == radial - 1
    speed = jnp.abs(vc) + a
    reach = 0.5 * jnp.maximum(speed, after(speed))
    speed = jnp.abs(vr) + a
    rise = 0.5 * jnp.maximum(speed, above(speed))
    flux = around_flux(q, vc, p)
    radial_flux = (q[1], q[1] * vr + p, q[2] * vr, (q[3] + p) * vr)
    for c in range(4):
        face = 0.5 * (flux[c] + after(flux[c])) - reach * (after(q[c]) - q[c])
        face = jnp.where(column == around - 1, 0.0, face)
        residual = weight * q[c] + (face - pltpu.roll(face, 1, 1))
        wall = p if c == 1 else 0.0
        face = 0.5 * (radial_flux[c] + above(radial_flux[c])) - rise * (above(q[c]) - q[c])
        upper = jnp.where(tip, wall, face)
        lower = jnp.where(hub, wall, pltpu.roll(face, 1, 0))
        base[0, c] = residual + (upper - lower)


def outer_kernel(weights, instances, orders, blocks, state, base, kept, came, partner, *refs):
    *edges, residual, total = refs
    radial, around = state.shape[2:]
    if blocks == RIDING:
        me = lax.axis_index("space")
        known = [kept[0, EDGE:, :], came[0, EDGE:, :]]
        known = jnp.concatenate(known, axis=0)
        row = lax.broadcasted_iota(jnp.int32, known.shape, 0)

        def edge_of(device):
            relative = device ^ me
            half = RIDING // 2
            place = (half - relative // 2) % half + (relative % 2) * half
            return jnp.sum(jnp.where(row == place, known, 0.0), axis=0, keepdims=True)

        before = edge_of((me + blocks - 1) % blocks)
        after = edge_of((me + 1) % blocks)
    else:
        before, after = (ref[0:1, :] for ref in edges)
    me = lax.axis_index("inst")
    weight = weight_from(weights, instances, me ^ of_chip(orders)[0], me)
    lane = lax.broadcasted_iota(jnp.int32, (1, LANES), 1)
    edge = jnp.where(lane < LANES // 2, before, after)
    edge = jnp.broadcast_to(edge, (8, LANES))

    sublane = lax.broadcasted_iota(jnp.int32, (8, LANES), 0)
    lane = lax.broadcasted_iota(jnp.int32, (radial, LANES), 1)
    left, right = lane == 0, lane == LANES - 1
    own, far = [], []
    for c in range(4):
        own.append(jnp.where(left, state[0, c, :, :LANES], state[0, c, :, around - LANES :]))
        halo = []
        for r in range(radial // 8):
            index = sublane + jnp.where(lane[:8] == LANES - 1, 4 * radial, 0) + c * radial + r * 8
            halo.append(jnp.take_along_axis(edge, index, axis=1, mode="promise_in_bounds"))
        far.append(jnp.concatenate(halo, axis=0))
    faces, speeds = [], []
    for q in (own, far):
        inverse, _, vc, p = pressure_of(*q)
        speeds.append(jnp.abs(vc) + jnp.sqrt(gamma_ratio * p * inverse))
        faces.append(around_flux(q, vc, p))
    side = jnp.where(right, 0.5, -0.5)
    reach = 0.5 * jnp.maximum(*speeds)
    for c in range(4):
        outer = side * (faces[0][c] + faces[1][c]) - reach * (far[c] - own[c])
        outer = [jnp.where(left, outer, 0.0), jnp.where(right, outer, 0.0)]
        middle = around - 2 * LANES
        if middle:
            outer.insert(1, jnp.zeros((radial, middle), jnp.float32))
        residual[0, c] = base[0, c] + weight * partner[0, c] + jnp.concatenate(outer, axis=1)

    total[...] = kept[0] + came[0]


def update_kernel(residual, step, total, *refs):
    *sums, increment, blade = refs
    high = blade.shape[2] // LANES
    for k in range(3):
        for h in range(high):
            blade[k, :, pl.ds(h * LANES, LANES)] = total[k * high + h : k * high + h + 1, :]
    for c in range(residual.shape[1]):
        change = functools.reduce(jnp.add, [ref[0, c] for ref in (residual, *sums)])
        increment[0, c] = -step[...] * change


def per_device(node_block, state, face_cell, face_node, face_area):
    blocks = lax.axis_size("space")
    instances = lax.axis_size("inst")
    radial, around = state.shape[2:]
    chunks = face_cell.shape[0] // LANES
    vmem = pl.BlockSpec(memory_space=pltpu.VMEM)
    params = pltpu.CompilerParams(vmem_limit_bytes=(4 if blocks <= 16 else 16) * 2**20)

    def swapped(value, axis, bit):
        return lax.ppermute(value, axis, [(i, i ^ bit) for i in range(lax.axis_size(axis))])

    def shifted(value, axis, s):
        count = lax.axis_size(axis)
        return lax.ppermute(value, axis, [(i, (i + s) % count) for i in range(count)])

    def exchanged(sent, size):
        return [
            swapped(value, "space", (len(sent) - i) * size) for i, value in enumerate(sent)
        ]

    def call(kernel, name, shapes, *operands, flops=0, dtype=jnp.float32):
        return pl.pallas_call(
            kernel,
            out_shape=[jax.ShapeDtypeStruct(shape, dtype) for shape in shapes],
            in_specs=[vmem] * len(operands),
            out_specs=[vmem] * len(shapes),
            compiler_params=params,
            cost_estimate=pl.CostEstimate(flops=flops, bytes_accessed=0, transcendentals=0),
            name=name,
        )(*operands)

    weights = spectral_row(instances)
    def partnered(value, place):
        pairs = [
            (i * instances + n, i * instances + (n ^ orders[i // 2 % 2][place]))
            for i in range(blocks)
            for n in range(instances)
        ]
        return lax.ppermute(value, ("space", "inst"), pairs)

    orders = ORDERS if instances == 4 else ((1, *range(2, instances, 2)),) * 2
    partner = partnered(state, 0)

    riding = blocks == RIDING
    steps = [4, 2] if riding else [2] * (blocks.bit_length() - 1)
    size = blocks // steps[0]
    (own,) = call(
        functools.partial(own_kernel, node_block // LANES),
        "own",
        [(8, LANES)],
        dtype=jnp.int32,
        flops=PLACING,
    )
    kept, *sent = call(
        functools.partial(forces_kernel, node_block),
        "face_forces",
        [(size, ROWS, LANES)] * steps[0],
        own,
        state,
        face_cell.reshape(chunks, LANES),
        face_node.reshape(chunks, LANES),
        face_area,
        flops=PLACING,
    )

    edges = []
    if not riding:
        row = jnp.broadcast_to(kept[0, EDGE : EDGE + 1, :], (8, LANES))
        edges = [shifted(row, "space", 1), shifted(row, "space", blocks - 1)]

    came = exchanged(sent, size)
    sums = call(
        functools.partial(pair_kernel, weights, instances, orders),
        "pair_sums",
        [state.shape] * (len(orders[0]) - 1),
        state,
        partner,
        flops=PLACING,
    )
    sums = [partnered(value, i) for i, value in enumerate(sums, 1)]

    for step in steps[1:]:
        size //= step
        kept, *sent = call(
            functools.partial(halving_kernel, 1 + len(came), riding),
            "halving",
            [(size, ROWS, LANES)] * step,
            kept,
            *came,
            flops=PLACING,
        )
        came = exchanged(sent, size)

    base, step = call(
        functools.partial(flux_kernel, weights[0], instances),
        "flux",
        [state.shape, (radial, around)],
        state,
    )
    residual, total = call(
        functools.partial(outer_kernel, weights, instances, orders, blocks),
        "outer",
        [state.shape, (ROWS, LANES)],
        state,
        base,
        kept,
        *came,
        partner,
        *edges,
    )
    increment, blade = call(
        update_kernel,
        "update",
        [state.shape, (3, 1, node_block)],
        residual,
        step,
        total,
        *sums,
    )
    return increment, jnp.transpose(blade, (1, 0, 2))


def solution(mesh):
    in_specs = (P("inst", None, None, "space"), P("space"), P("space"), P(None, "space"))
    out_specs = (P("inst", None, None, "space"), P("inst", None, "space"))
    return jax.shard_map(
        functools.partial(per_device, 512),
        mesh=mesh,
        in_specs=in_specs,
        out_specs=out_specs,
        check_vma=False,
    )
```

```python
import functools
import math

import jax
import jax.numpy as jnp
import numpy as np
from jax import lax
from jax.experimental import pallas as pl
from jax.experimental.pallas import tpu as pltpu
from jax.sharding import PartitionSpec as P

gamma_ratio = 1.4
omega_rate = 0.5
cfl_number = 0.8

LANES = 128
ROWS = 16
EDGE = 12
PLACING = 10**10
ORDERS = ((2, 1), (1, 2))
RIDING = 8


def spectral_row(count):
    row = np.zeros((count,), np.float32)
    for shift in range(count):
        row[shift] = (-1.0) ** shift / count
        if shift != 0:
            row[shift] += 0.5 * (-1.0) ** shift / math.tan(math.pi * shift / count)
    return [float(omega_rate * value) for value in row]


def pressure_of(q0, q1, q2, q3):
    inverse = 1.0 / q0
    vr = q1 * inverse
    vc = q2 * inverse
    p = (gamma_ratio - 1.0) * (q3 - 0.5 * q0 * (vr * vr + vc * vc))
    return inverse, vr, vc, p


def own_kernel(high, out):
    out[...] = jnp.full(out.shape, lax.axis_index("space") * high, jnp.int32)


def split(value, size):
    return value >> (size.bit_length() - 1), value & (size - 1)


def forces_kernel(node_block, own, state, cell, node, area, *outs):
    radial, around = state.shape[2:]
    faces = cell.shape[0] * LANES
    chunks = faces // LANES
    _, _, _, p = pressure_of(state[0, 0], state[0, 1], state[0, 2], state[0, 3])
    sublane = lax.broadcasted_iota(jnp.int32, (8, LANES), 0)
    picked = []
    for c in range(chunks):
        tile, lane = split(jnp.broadcast_to(cell[c : c + 1, :], (8, LANES)), LANES)
        total = jnp.zeros((8, LANES), jnp.float32)
        for r in range(radial // 8):
            for h in range(around // LANES):
                part = p[r * 8 : (r + 1) * 8, h * LANES : (h + 1) * LANES]
                value = jnp.take_along_axis(part, lane, axis=1, mode="promise_in_bounds")
                place = (sublane + r * 8) * (around // LANES) + h
                total += jnp.where(tile == place, value, 0.0)
        picked.append(jnp.sum(total, axis=0, keepdims=True))
    face_pressure = jnp.concatenate(picked, axis=1)
    contribution = face_pressure * area[...]
    nodes = jnp.concatenate([node[c : c + 1, :] for c in range(chunks)], axis=1)

    high = node_block // LANES
    place, low = split(nodes, LANES)
    place = place ^ jnp.broadcast_to(own[0:1, 0:1], nodes.shape)
    pick_low = (
        lax.broadcasted_iota(jnp.int32, (LANES, faces), 0) == jnp.broadcast_to(low, (LANES, faces))
    ).astype(jnp.float32).astype(jnp.bfloat16)

    row = lax.broadcasted_iota(jnp.int32, (8, faces), 0)
    x, y, z = (jnp.broadcast_to(contribution[k : k + 1], (8, faces)) for k in range(3))
    groups = []
    for pattern in (jnp.where(row < high, x, y), jnp.where(row < high, z, 0.0)):
        first = pattern.astype(jnp.bfloat16).astype(jnp.float32)
        groups.append((first, pattern - first))
    away = jnp.broadcast_to(place, (8, faces)) - (row & (high - 1))

    def dense(start, count):
        masks = [away == (start + b) * high for b in range(count)]
        left = [jnp.where(m, g[i], 0.0) for i in range(2) for m in masks for g in groups]
        product = lax.dot_general(
            jnp.concatenate(left, axis=0).astype(jnp.bfloat16),
            pick_low,
            (((1,), (1,)), ((), ())),
            preferred_element_type=jnp.float32,
        )
        rows = count * ROWS
        return (product[:rows] + product[rows:]).reshape(count, ROWS, LANES)

    size = outs[0].shape[0]
    if len(outs) == 4:
        mine, x, y, diagonal = dense(0, 4 * size).reshape(4, size, ROWS, LANES)
        swap = lax.axis_index("inst") % 2 == 1
        sent = (jnp.where(swap, y, diagonal), jnp.where(swap, diagonal, y), x)
        for out, part in zip(outs, (mine, *sent)):
            out[...] = part
    else:
        for i, out in enumerate(outs):

            @pl.loop(0, size // 8)
            def _(g):
                out[pl.ds(g * 8, 8)] = dense(i * size + g * 8, 8)

    lane = lax.broadcasted_iota(jnp.int32, (8, LANES), 1)
    columns = jnp.zeros((8, LANES), jnp.float32)
    for i, column in enumerate((around - 1, 0)):
        tile, index = divmod(column, LANES)
        index = jnp.full((8, LANES), index, jnp.int32)
        for c in range(4):
            for r in range(radial // 8):
                part = state[0, c, r * 8 : (r + 1) * 8, tile * LANES : (tile + 1) * LANES]
                value = jnp.take_along_axis(part, index, axis=1, mode="promise_in_bounds")
                place = (i * 4 + c) * radial + r * 8
                columns = jnp.where(lane == sublane + place, value, columns)
    edge = jnp.sum(columns, axis=0, keepdims=True)
    for out in outs:
        out[0, EDGE : EDGE + 1, :] = edge


def halving_kernel(arrived, riding, *refs):
    outs = refs[arrived:]
    size = outs[0].shape[0]
    for i, out in enumerate(outs):
        for b in range(size):
            out[b] = functools.reduce(jnp.add, [ref[i * size + b] for ref in refs[:arrived]])
        if riding:
            for j, ref in enumerate(refs[:arrived]):
                out[0, EDGE + j : EDGE + j + 1, :] = ref[0, EDGE : EDGE + 1, :]


def weight_from(weights, instances, source, target):
    shift = (target - source + instances) % instances
    value = weights[0]
    for i in range(1, instances):
        value = jnp.where(shift == i, weights[i], value)
    return value


def of_chip(orders):
    chip = lax.axis_index("space") // 2
    return [jnp.where(chip % 2 == 0, a, b) for a, b in zip(*orders)]


def pair_kernel(weights, instances, orders, state, partner, *outs):
    me = lax.axis_index("inst")
    first, *seconds = of_chip(orders)
    for second, out in zip(seconds, outs):
        own = weight_from(weights, instances, me, me ^ second)
        other = weight_from(weights, instances, me ^ first, me ^ second)
        out[...] = own * state[...] + other * partner[...]


def around_flux(q, vc, p):
    return (q[2], q[1] * vc, q[2] * vc + p, (q[3] + p) * vc)


def flux_kernel(weight, instances, state, base, step):
    radial, around = state.shape[2:]
    q = [state[0, c] for c in range(4)]
    inverse, vr, vc, p = pressure_of(*q)
    a = jnp.sqrt(gamma_ratio * p * inverse)
    step[...] = cfl_number / (
        jnp.abs(vr) + jnp.abs(vc) + 2.0 * a + omega_rate * instances / 2.0
    )

    def after(x):
        return pltpu.roll(x, around - 1, 1)

    def above(x):
        return pltpu.roll(x, radial - 1, 0)

    column = lax.broadcasted_iota(jnp.int32, (radial, around), 1)
    row = lax.broadcasted_iota(jnp.int32, (radial, around), 0)
    hub, tip = row == 0, row == radial - 1
    speed = jnp.abs(vc) + a
    reach = 0.5 * jnp.maximum(speed, after(speed))
    speed = jnp.abs(vr) + a
    rise = 0.5 * jnp.maximum(speed, above(speed))
    flux = around_flux(q, vc, p)
    radial_flux = (q[1], q[1] * vr + p, q[2] * vr, (q[3] + p) * vr)
    for c in range(4):
        face = 0.5 * (flux[c] + after(flux[c])) - reach * (after(q[c]) - q[c])
        face = jnp.where(column == around - 1, 0.0, face)
        residual = weight * q[c] + (face - pltpu.roll(face, 1, 1))
        wall = p if c == 1 else 0.0
        face = 0.5 * (radial_flux[c] + above(radial_flux[c])) - rise * (above(q[c]) - q[c])
        upper = jnp.where(tip, wall, face)
        lower = jnp.where(hub, wall, pltpu.roll(face, 1, 0))
        base[0, c] = residual + (upper - lower)


def outer_kernel(weights, instances, orders, blocks, state, base, kept, came, partner, *refs):
    *edges, residual, total = refs
    radial, around = state.shape[2:]
    if blocks == RIDING:
        me = lax.axis_index("space")
        known = [kept[0, EDGE:, :], came[0, EDGE:, :]]
        known = jnp.concatenate(known, axis=0)
        row = lax.broadcasted_iota(jnp.int32, known.shape, 0)

        def edge_of(device):
            relative = device ^ me
            half = RIDING // 2
            place = (half - relative // 2) % half
            swap = (lax.axis_index("inst") % 2 == 1) & (place >= 1) & (place <= 2)
            place = jnp.where(swap, half - 1 - place, place) + (relative % 2) * half
            return jnp.sum(jnp.where(row == place, known, 0.0), axis=0, keepdims=True)

        before = edge_of((me + blocks - 1) % blocks)
        after = edge_of((me + 1) % blocks)
    else:
        before, after = (ref[0:1, :] for ref in edges)
    me = lax.axis_index("inst")
    weight = weight_from(weights, instances, me ^ of_chip(orders)[0], me)
    lane = lax.broadcasted_iota(jnp.int32, (1, LANES), 1)
    edge = jnp.where(lane < LANES // 2, before, after)
    edge = jnp.broadcast_to(edge, (8, LANES))

    sublane = lax.broadcasted_iota(jnp.int32, (8, LANES), 0)
    lane = lax.broadcasted_iota(jnp.int32, (radial, LANES), 1)
    left, right = lane == 0, lane == LANES - 1
    own, far = [], []
    for c in range(4):
        own.append(jnp.where(left, state[0, c, :, :LANES], state[0, c, :, around - LANES :]))
        halo = []
        for r in range(radial // 8):
            index = sublane + jnp.where(lane[:8] == LANES - 1, 4 * radial, 0) + c * radial + r * 8
            halo.append(jnp.take_along_axis(edge, index, axis=1, mode="promise_in_bounds"))
        far.append(jnp.concatenate(halo, axis=0))
    faces, speeds = [], []
    for q in (own, far):
        inverse, _, vc, p = pressure_of(*q)
        speeds.append(jnp.abs(vc) + jnp.sqrt(gamma_ratio * p * inverse))
        faces.append(around_flux(q, vc, p))
    side = jnp.where(right, 0.5, -0.5)
    reach = 0.5 * jnp.maximum(*speeds)
    for c in range(4):
        outer = side * (faces[0][c] + faces[1][c]) - reach * (far[c] - own[c])
        outer = [jnp.where(left, outer, 0.0), jnp.where(right, outer, 0.0)]
        middle = around - 2 * LANES
        if middle:
            outer.insert(1, jnp.zeros((radial, middle), jnp.float32))
        residual[0, c] = base[0, c] + weight * partner[0, c] + jnp.concatenate(outer, axis=1)

    total[...] = kept[0] + came[0]


def update_kernel(residual, step, total, *refs):
    *sums, increment, blade = refs
    high = blade.shape[2] // LANES
    for k in range(3):
        for h in range(high):
            blade[k, :, pl.ds(h * LANES, LANES)] = total[k * high + h : k * high + h + 1, :]
    for c in range(residual.shape[1]):
        change = functools.reduce(jnp.add, [ref[0, c] for ref in (residual, *sums)])
        increment[0, c] = -step[...] * change


def per_device(node_block, state, face_cell, face_node, face_area):
    blocks = lax.axis_size("space")
    instances = lax.axis_size("inst")
    radial, around = state.shape[2:]
    chunks = face_cell.shape[0] // LANES
    vmem = pl.BlockSpec(memory_space=pltpu.VMEM)
    params = pltpu.CompilerParams(vmem_limit_bytes=(4 if blocks <= 16 else 16) * 2**20)

    def swapped(value, axis, bit):
        return lax.ppermute(value, axis, [(i, i ^ bit) for i in range(lax.axis_size(axis))])

    def shifted(value, axis, s):
        count = lax.axis_size(axis)
        return lax.ppermute(value, axis, [(i, (i + s) % count) for i in range(count)])

    def exchanged(sent):
        return [
            lax.ppermute(
                value,
                ("space", "inst"),
                [
                    (i * instances + n, (i ^ bits[n % 2]) * instances + n)
                    for i in range(blocks)
                    for n in range(instances)
                ],
            )
            for value, bits in zip(sent, ((6, 4), (4, 6), (2, 2)))
        ]

    def call(kernel, name, shapes, *operands, flops=0, dtype=jnp.float32):
        return pl.pallas_call(
            kernel,
            out_shape=[jax.ShapeDtypeStruct(shape, dtype) for shape in shapes],
            in_specs=[vmem] * len(operands),
            out_specs=[vmem] * len(shapes),
            compiler_params=params,
            cost_estimate=pl.CostEstimate(flops=flops, bytes_accessed=0, transcendentals=0),
            name=name,
        )(*operands)

    weights = spectral_row(instances)
    def partnered(value, place):
        pairs = [
            (i * instances + n, i * instances + (n ^ orders[i // 2 % 2][place]))
            for i in range(blocks)
            for n in range(instances)
        ]
        return lax.ppermute(value, ("space", "inst"), pairs)

    orders = ORDERS if instances == 4 else ((1, *range(2, instances, 2)),) * 2
    partner = partnered(state, 0)

    riding = blocks == RIDING
    steps = [4, 2] if riding else [2] * (blocks.bit_length() - 1)
    size = blocks // steps[0]
    (own,) = call(
        functools.partial(own_kernel, node_block // LANES),
        "own",
        [(8, LANES)],
        dtype=jnp.int32,
        flops=PLACING,
    )
    kept, *sent = call(
        functools.partial(forces_kernel, node_block),
        "face_forces",
        [(size, ROWS, LANES)] * steps[0],
        own,
        state,
        face_cell.reshape(chunks, LANES),
        face_node.reshape(chunks, LANES),
        face_area,
        flops=PLACING,
    )

    edges = []
    if not riding:
        row = jnp.broadcast_to(kept[0, EDGE : EDGE + 1, :], (8, LANES))
        edges = [shifted(row, "space", 1), shifted(row, "space", blocks - 1)]

    came = exchanged(sent) if riding else [swapped(sent[0], "space", size)]
    sums = call(
        functools.partial(pair_kernel, weights, instances, orders),
        "pair_sums",
        [state.shape] * (len(orders[0]) - 1),
        state,
        partner,
        flops=PLACING,
    )
    sums = [partnered(value, i) for i, value in enumerate(sums, 1)]

    for step in steps[1:]:
        size //= step
        kept, *sent = call(
            functools.partial(halving_kernel, 1 + len(came), riding),
            "halving",
            [(size, ROWS, LANES)] * step,
            kept,
            *came,
            flops=PLACING,
        )
        came = [swapped(sent[0], "space", size)]

    base, step = call(
        functools.partial(flux_kernel, weights[0], instances),
        "flux",
        [state.shape, (radial, around)],
        state,
    )
    residual, total = call(
        functools.partial(outer_kernel, weights, instances, orders, blocks),
        "outer",
        [state.shape, (ROWS, LANES)],
        state,
        base,
        kept,
        *came,
        partner,
        *edges,
    )
    increment, blade = call(
        update_kernel,
        "update",
        [state.shape, (3, 1, node_block)],
        residual,
        step,
        total,
        *sums,
    )
    return increment, jnp.transpose(blade, (1, 0, 2))


def solution(mesh):
    in_specs = (P("inst", None, None, "space"), P("space"), P("space"), P(None, "space"))
    out_specs = (P("inst", None, None, "space"), P("inst", None, "space"))
    return jax.shard_map(
        functools.partial(per_device, 512),
        mesh=mesh,
        in_specs=in_specs,
        out_specs=out_specs,
        check_vma=False,
    )
```

```python
import functools
import math

import jax
import jax.numpy as jnp
import numpy as np
from jax import lax
from jax.experimental import pallas as pl
from jax.experimental.pallas import tpu as pltpu
from jax.sharding import PartitionSpec as P

gamma_ratio = 1.4
omega_rate = 0.5
cfl_number = 0.8

LANES = 128
ROWS = 16
EDGE = 12
PLACING = 10**10
ORDERS = ((2, 1), (1, 2))
RIDING = 8


def spectral_row(count):
    row = np.zeros((count,), np.float32)
    for shift in range(count):
        row[shift] = (-1.0) ** shift / count
        if shift != 0:
            row[shift] += 0.5 * (-1.0) ** shift / math.tan(math.pi * shift / count)
    return [float(omega_rate * value) for value in row]


def pressure_of(q0, q1, q2, q3):
    inverse = 1.0 / q0
    vr = q1 * inverse
    vc = q2 * inverse
    p = (gamma_ratio - 1.0) * (q3 - 0.5 * q0 * (vr * vr + vc * vc))
    return inverse, vr, vc, p


def own_kernel(high, out):
    out[...] = jnp.full(out.shape, lax.axis_index("space") * high, jnp.int32)


def split(value, size):
    return value >> (size.bit_length() - 1), value & (size - 1)


def forces_kernel(node_block, own, state, cell, node, area, *outs):
    radial, around = state.shape[2:]
    faces = cell.shape[0] * LANES
    chunks = faces // LANES
    _, _, _, p = pressure_of(state[0, 0], state[0, 1], state[0, 2], state[0, 3])
    sublane = lax.broadcasted_iota(jnp.int32, (8, LANES), 0)
    picked = []
    for c in range(chunks):
        tile, lane = split(jnp.broadcast_to(cell[c : c + 1, :], (8, LANES)), LANES)
        total = jnp.zeros((8, LANES), jnp.float32)
        for r in range(radial // 8):
            for h in range(around // LANES):
                part = p[r * 8 : (r + 1) * 8, h * LANES : (h + 1) * LANES]
                value = jnp.take_along_axis(part, lane, axis=1, mode="promise_in_bounds")
                place = (sublane + r * 8) * (around // LANES) + h
                total += jnp.where(tile == place, value, 0.0)
        picked.append(jnp.sum(total, axis=0, keepdims=True))
    face_pressure = jnp.concatenate(picked, axis=1)
    contribution = face_pressure * area[...]
    nodes = jnp.concatenate([node[c : c + 1, :] for c in range(chunks)], axis=1)

    high = node_block // LANES
    place, low = split(nodes, LANES)
    place = place ^ jnp.broadcast_to(own[0:1, 0:1], nodes.shape)
    pick_low = (
        lax.broadcasted_iota(jnp.int32, (LANES, faces), 0) == jnp.broadcast_to(low, (LANES, faces))
    ).astype(jnp.float32).astype(jnp.bfloat16)

    row = lax.broadcasted_iota(jnp.int32, (8, faces), 0)
    x, y, z = (jnp.broadcast_to(contribution[k : k + 1], (8, faces)) for k in range(3))
    groups = []
    for pattern in (jnp.where(row < high, x, y), jnp.where(row < high, z, 0.0)):
        first = pattern.astype(jnp.bfloat16).astype(jnp.float32)
        groups.append((first, pattern - first))
    away = jnp.broadcast_to(place, (8, faces)) - (row & (high - 1))

    def dense(start, count):
        masks = [away == (start + b) * high for b in range(count)]
        left = [jnp.where(m, g[i], 0.0) for i in range(2) for m in masks for g in groups]
        product = lax.dot_general(
            jnp.concatenate(left, axis=0).astype(jnp.bfloat16),
            pick_low,
            (((1,), (1,)), ((), ())),
            preferred_element_type=jnp.float32,
        )
        rows = count * ROWS
        return (product[:rows] + product[rows:]).reshape(count, ROWS, LANES)

    ordered = [outs[0], outs[2], outs[3], outs[1]] if len(outs) == 4 else outs
    size = outs[0].shape[0]
    blocks = size * len(outs)
    if blocks <= 16:
        result = dense(0, blocks)
        for i, out in enumerate(ordered):
            out[...] = result[i * size : (i + 1) * size]
    else:
        for i, out in enumerate(ordered):

            @pl.loop(0, size // 8)
            def _(g):
                out[pl.ds(g * 8, 8)] = dense(i * size + g * 8, 8)

    lane = lax.broadcasted_iota(jnp.int32, (8, LANES), 1)
    columns = jnp.zeros((8, LANES), jnp.float32)
    for i, column in enumerate((around - 1, 0)):
        tile, index = divmod(column, LANES)
        index = jnp.full((8, LANES), index, jnp.int32)
        for c in range(4):
            for r in range(radial // 8):
                part = state[0, c, r * 8 : (r + 1) * 8, tile * LANES : (tile + 1) * LANES]
                value = jnp.take_along_axis(part, index, axis=1, mode="promise_in_bounds")
                place = (i * 4 + c) * radial + r * 8
                columns = jnp.where(lane == sublane + place, value, columns)
    edge = jnp.sum(columns, axis=0, keepdims=True)
    for out in outs:
        out[0, EDGE : EDGE + 1, :] = edge


def halving_kernel(arrived, riding, *refs):
    outs = refs[arrived:]
    size = outs[0].shape[0]
    for i, out in enumerate(outs):
        for b in range(size):
            out[b] = functools.reduce(jnp.add, [ref[i * size + b] for ref in refs[:arrived]])
        if riding:
            for j, ref in enumerate(refs[:arrived]):
                out[0, EDGE + j : EDGE + j + 1, :] = ref[0, EDGE : EDGE + 1, :]


def weight_from(weights, instances, source, target):
    shift = (target - source + instances) % instances
    value = weights[0]
    for i in range(1, instances):
        value = jnp.where(shift == i, weights[i], value)
    return value


def of_chip(orders):
    half = lax.axis_index("space") // 4
    return [jnp.where(half % 2 == 0, a, b) for a, b in zip(*orders)]


def pair_kernel(weights, instances, orders, state, partner, *outs):
    me = lax.axis_index("inst")
    first, *seconds = of_chip(orders)
    for second, out in zip(seconds, outs):
        own = weight_from(weights, instances, me, me ^ second)
        other = weight_from(weights, instances, me ^ first, me ^ second)
        out[...] = own * state[...] + other * partner[...]


def around_flux(q, vc, p):
    return (q[2], q[1] * vc, q[2] * vc + p, (q[3] + p) * vc)


def flux_kernel(weight, instances, state, base, step):
    radial, around = state.shape[2:]
    q = [state[0, c] for c in range(4)]
    inverse, vr, vc, p = pressure_of(*q)
    a = jnp.sqrt(gamma_ratio * p * inverse)
    step[...] = cfl_number / (
        jnp.abs(vr) + jnp.abs(vc) + 2.0 * a + omega_rate * instances / 2.0
    )

    def after(x):
        return pltpu.roll(x, around - 1, 1)

    def above(x):
        return pltpu.roll(x, radial - 1, 0)

    column = lax.broadcasted_iota(jnp.int32, (radial, around), 1)
    row = lax.broadcasted_iota(jnp.int32, (radial, around), 0)
    hub, tip = row == 0, row == radial - 1
    speed = jnp.abs(vc) + a
    reach = 0.5 * jnp.maximum(speed, after(speed))
    speed = jnp.abs(vr) + a
    rise = 0.5 * jnp.maximum(speed, above(speed))
    flux = around_flux(q, vc, p)
    radial_flux = (q[1], q[1] * vr + p, q[2] * vr, (q[3] + p) * vr)
    for c in range(4):
        face = 0.5 * (flux[c] + after(flux[c])) - reach * (after(q[c]) - q[c])
        face = jnp.where(column == around - 1, 0.0, face)
        residual = weight * q[c] + (face - pltpu.roll(face, 1, 1))
        wall = p if c == 1 else 0.0
        face = 0.5 * (radial_flux[c] + above(radial_flux[c])) - rise * (above(q[c]) - q[c])
        upper = jnp.where(tip, wall, face)
        lower = jnp.where(hub, wall, pltpu.roll(face, 1, 0))
        base[0, c] = residual + (upper - lower)


def outer_kernel(weights, instances, orders, blocks, state, base, kept, came, partner, *refs):
    *edges, residual, total = refs
    radial, around = state.shape[2:]
    if blocks == RIDING:
        me = lax.axis_index("space")
        known = [kept[0, EDGE:, :], came[0, EDGE:, :]]
        known = jnp.concatenate(known, axis=0)
        row = lax.broadcasted_iota(jnp.int32, known.shape, 0)

        def edge_of(device):
            relative = device ^ me
            half = RIDING // 2
            chip = relative // 2
            place = jnp.where(chip == 3, 1, jnp.where(chip == 0, 0, chip + 1))
            place += (relative % 2) * half
            return jnp.sum(jnp.where(row == place, known, 0.0), axis=0, keepdims=True)

        before = edge_of((me + blocks - 1) % blocks)
        after = edge_of((me + 1) % blocks)
    else:
        before, after = (ref[0:1, :] for ref in edges)
    me = lax.axis_index("inst")
    weight = weight_from(weights, instances, me ^ of_chip(orders)[0], me)
    lane = lax.broadcasted_iota(jnp.int32, (1, LANES), 1)
    edge = jnp.where(lane < LANES // 2, before, after)
    edge = jnp.broadcast_to(edge, (8, LANES))

    sublane = lax.broadcasted_iota(jnp.int32, (8, LANES), 0)
    lane = lax.broadcasted_iota(jnp.int32, (radial, LANES), 1)
    left, right = lane == 0, lane == LANES - 1
    own, far = [], []
    for c in range(4):
        own.append(jnp.where(left, state[0, c, :, :LANES], state[0, c, :, around - LANES :]))
        halo = []
        for r in range(radial // 8):
            index = sublane + jnp.where(lane[:8] == LANES - 1, 4 * radial, 0) + c * radial + r * 8
            halo.append(jnp.take_along_axis(edge, index, axis=1, mode="promise_in_bounds"))
        far.append(jnp.concatenate(halo, axis=0))
    faces, speeds = [], []
    for q in (own, far):
        inverse, _, vc, p = pressure_of(*q)
        speeds.append(jnp.abs(vc) + jnp.sqrt(gamma_ratio * p * inverse))
        faces.append(around_flux(q, vc, p))
    side = jnp.where(right, 0.5, -0.5)
    reach = 0.5 * jnp.maximum(*speeds)
    for c in range(4):
        outer = side * (faces[0][c] + faces[1][c]) - reach * (far[c] - own[c])
        outer = [jnp.where(left, outer, 0.0), jnp.where(right, outer, 0.0)]
        middle = around - 2 * LANES
        if middle:
            outer.insert(1, jnp.zeros((radial, middle), jnp.float32))
        residual[0, c] = base[0, c] + weight * partner[0, c] + jnp.concatenate(outer, axis=1)

    total[...] = kept[0] + came[0]


def update_kernel(residual, step, total, *refs):
    *sums, increment, blade = refs
    high = blade.shape[2] // LANES
    for k in range(3):
        for h in range(high):
            blade[k, :, pl.ds(h * LANES, LANES)] = total[k * high + h : k * high + h + 1, :]
    for c in range(residual.shape[1]):
        change = functools.reduce(jnp.add, [ref[0, c] for ref in (residual, *sums)])
        increment[0, c] = -step[...] * change


def per_device(node_block, state, face_cell, face_node, face_area):
    blocks = lax.axis_size("space")
    instances = lax.axis_size("inst")
    radial, around = state.shape[2:]
    chunks = face_cell.shape[0] // LANES
    vmem = pl.BlockSpec(memory_space=pltpu.VMEM)
    params = pltpu.CompilerParams(vmem_limit_bytes=(4 if blocks <= 16 else 16) * 2**20)

    def swapped(value, axis, bit):
        return lax.ppermute(value, axis, [(i, i ^ bit) for i in range(lax.axis_size(axis))])

    def shifted(value, axis, s):
        count = lax.axis_size(axis)
        return lax.ppermute(value, axis, [(i, (i + s) % count) for i in range(count)])

    def exchanged(sent, size):
        places = (3, 1, 2) if len(sent) == 3 else (1,)
        return [swapped(value, "space", place * size) for place, value in zip(places, sent)]

    def call(kernel, name, shapes, *operands, flops=0, dtype=jnp.float32):
        return pl.pallas_call(
            kernel,
            out_shape=[jax.ShapeDtypeStruct(shape, dtype) for shape in shapes],
            in_specs=[vmem] * len(operands),
            out_specs=[vmem] * len(shapes),
            compiler_params=params,
            cost_estimate=pl.CostEstimate(flops=flops, bytes_accessed=0, transcendentals=0),
            name=name,
        )(*operands)

    weights = spectral_row(instances)
    def partnered(value, place):
        pairs = [
            (i * instances + n, i * instances + (n ^ orders[i // 4 % 2][place]))
            for i in range(blocks)
            for n in range(instances)
        ]
        return lax.ppermute(value, ("space", "inst"), pairs)

    orders = ORDERS if instances == 4 else ((1, *range(2, instances, 2)),) * 2
    partner = partnered(state, 0)

    riding = blocks == RIDING
    steps = [4, 2] if riding else [2] * (blocks.bit_length() - 1)
    size = blocks // steps[0]
    (own,) = call(
        functools.partial(own_kernel, node_block // LANES),
        "own",
        [(8, LANES)],
        dtype=jnp.int32,
        flops=PLACING,
    )
    kept, *sent = call(
        functools.partial(forces_kernel, node_block),
        "face_forces",
        [(size, ROWS, LANES)] * steps[0],
        own,
        state,
        face_cell.reshape(chunks, LANES),
        face_node.reshape(chunks, LANES),
        face_area,
        flops=PLACING,
    )

    edges = []
    if not riding:
        row = jnp.broadcast_to(kept[0, EDGE : EDGE + 1, :], (8, LANES))
        edges = [shifted(row, "space", 1), shifted(row, "space", blocks - 1)]

    came = exchanged(sent, size)
    sums = call(
        functools.partial(pair_kernel, weights, instances, orders),
        "pair_sums",
        [state.shape] * (len(orders[0]) - 1),
        state,
        partner,
        flops=PLACING,
    )
    sums = [partnered(value, i) for i, value in enumerate(sums, 1)]

    for step in steps[1:]:
        size //= step
        kept, *sent = call(
            functools.partial(halving_kernel, 1 + len(came), riding),
            "halving",
            [(size, ROWS, LANES)] * step,
            kept,
            *came,
            flops=PLACING,
        )
        came = exchanged(sent, size)

    base, step = call(
        functools.partial(flux_kernel, weights[0], instances),
        "flux",
        [state.shape, (radial, around)],
        state,
    )
    residual, total = call(
        functools.partial(outer_kernel, weights, instances, orders, blocks),
        "outer",
        [state.shape, (ROWS, LANES)],
        state,
        base,
        kept,
        *came,
        partner,
        *edges,
    )
    increment, blade = call(
        update_kernel,
        "update",
        [state.shape, (3, 1, node_block)],
        residual,
        step,
        total,
        *sums,
    )
    return increment, jnp.transpose(blade, (1, 0, 2))


def solution(mesh):
    in_specs = (P("inst", None, None, "space"), P("space"), P("space"), P(None, "space"))
    out_specs = (P("inst", None, None, "space"), P("inst", None, "space"))
    return jax.shard_map(
        functools.partial(per_device, 512),
        mesh=mesh,
        in_specs=in_specs,
        out_specs=out_specs,
        check_vma=False,
    )
```

```python
import functools
import math

import jax
import jax.numpy as jnp
import numpy as np
from jax import lax
from jax.experimental import pallas as pl
from jax.experimental.pallas import tpu as pltpu
from jax.sharding import PartitionSpec as P

gamma_ratio = 1.4
omega_rate = 0.5
cfl_number = 0.8

LANES = 128
ROWS = 16
EDGE = 12
PLACING = 10**10
ORDERS = ((2, 1), (1, 2))
RIDING = 8


def spectral_row(count):
    row = np.zeros((count,), np.float32)
    for shift in range(count):
        row[shift] = (-1.0) ** shift / count
        if shift != 0:
            row[shift] += 0.5 * (-1.0) ** shift / math.tan(math.pi * shift / count)
    return [float(omega_rate * value) for value in row]


def pressure_of(q0, q1, q2, q3):
    inverse = 1.0 / q0
    vr = q1 * inverse
    vc = q2 * inverse
    p = (gamma_ratio - 1.0) * (q3 - 0.5 * q0 * (vr * vr + vc * vc))
    return inverse, vr, vc, p


def own_kernel(high, out):
    out[...] = jnp.full(out.shape, lax.axis_index("space") * high, jnp.int32)


def split(value, size):
    return value >> (size.bit_length() - 1), value & (size - 1)


def forces_kernel(node_block, own, state, cell, node, area, *outs):
    radial, around = state.shape[2:]
    faces = cell.shape[0] * LANES
    chunks = faces // LANES
    _, _, _, p = pressure_of(state[0, 0], state[0, 1], state[0, 2], state[0, 3])
    sublane = lax.broadcasted_iota(jnp.int32, (8, LANES), 0)
    picked = []
    for c in range(chunks):
        tile, lane = split(jnp.broadcast_to(cell[c : c + 1, :], (8, LANES)), LANES)
        total = jnp.zeros((8, LANES), jnp.float32)
        for r in range(radial // 8):
            for h in range(around // LANES):
                part = p[r * 8 : (r + 1) * 8, h * LANES : (h + 1) * LANES]
                value = jnp.take_along_axis(part, lane, axis=1, mode="promise_in_bounds")
                place = (sublane + r * 8) * (around // LANES) + h
                total += jnp.where(tile == place, value, 0.0)
        for turn in (4, 2, 1):
            total += pltpu.roll(total, turn, 0)
        picked.append(total)
    face_pressure = jnp.concatenate(picked, axis=1)
    nodes = jnp.concatenate([node[c : c + 1, :] for c in range(chunks)], axis=1)

    high = node_block // LANES
    place, low = split(nodes, LANES)
    place = place ^ jnp.broadcast_to(own[0:1, 0:1], nodes.shape)
    pick_low = (
        lax.broadcasted_iota(jnp.int32, (LANES, faces), 0) == jnp.broadcast_to(low, (LANES, faces))
    ).astype(jnp.float32).astype(jnp.bfloat16)

    row = lax.broadcasted_iota(jnp.int32, (8, faces), 0)
    x, y, z = (face_pressure * jnp.broadcast_to(area[k : k + 1, :], (8, faces)) for k in range(3))
    groups = []
    for pattern in (jnp.where(row < high, x, y), jnp.where(row < high, z, 0.0)):
        first = pattern.astype(jnp.bfloat16).astype(jnp.float32)
        groups.append((first, pattern - first))
    away = jnp.broadcast_to(place, (8, faces)) - (row & (high - 1))

    def dense(start, count):
        masks = [away == (start + b) * high for b in range(count)]
        left = [jnp.where(m, g[i], 0.0) for i in range(2) for m in masks for g in groups]
        product = lax.dot_general(
            jnp.concatenate(left, axis=0).astype(jnp.bfloat16),
            pick_low,
            (((1,), (1,)), ((), ())),
            preferred_element_type=jnp.float32,
        )
        rows = count * ROWS
        return (product[:rows] + product[rows:]).reshape(count, ROWS, LANES)

    ordered = [outs[0], outs[2], outs[3], outs[1]] if len(outs) == 4 else outs
    size = outs[0].shape[0]
    blocks = size * len(outs)
    if blocks <= 16:
        result = dense(0, blocks)
        for i, out in enumerate(ordered):
            out[...] = result[i * size : (i + 1) * size]
    else:
        for i, out in enumerate(ordered):

            @pl.loop(0, size // 8)
            def _(g):
                out[pl.ds(g * 8, 8)] = dense(i * size + g * 8, 8)

    lane = lax.broadcasted_iota(jnp.int32, (8, LANES), 1)
    columns = jnp.zeros((8, LANES), jnp.float32)
    for i, column in enumerate((around - 1, 0)):
        tile, index = divmod(column, LANES)
        index = jnp.full((8, LANES), index, jnp.int32)
        for c in range(4):
            for r in range(radial // 8):
                part = state[0, c, r * 8 : (r + 1) * 8, tile * LANES : (tile + 1) * LANES]
                value = jnp.take_along_axis(part, index, axis=1, mode="promise_in_bounds")
                place = (i * 4 + c) * radial + r * 8
                columns = jnp.where(lane == sublane + place, value, columns)
    edge = jnp.sum(columns, axis=0, keepdims=True)
    for out in outs:
        out[0, EDGE : EDGE + 1, :] = edge


def halving_kernel(arrived, riding, *refs):
    outs = refs[arrived:]
    size = outs[0].shape[0]
    for i, out in enumerate(outs):
        for b in range(size):
            out[b] = functools.reduce(jnp.add, [ref[i * size + b] for ref in refs[:arrived]])
        if riding:
            for j, ref in enumerate(refs[:arrived]):
                out[0, EDGE + j : EDGE + j + 1, :] = ref[0, EDGE : EDGE + 1, :]


def weight_from(weights, instances, source, target):
    shift = (target - source + instances) % instances
    value = weights[0]
    for i in range(1, instances):
        value = jnp.where(shift == i, weights[i], value)
    return value


def of_chip(orders):
    half = lax.axis_index("space") // 4
    return [jnp.where(half % 2 == 0, a, b) for a, b in zip(*orders)]


def pair_kernel(weights, instances, orders, state, partner, *outs):
    me = lax.axis_index("inst")
    first, *seconds = of_chip(orders)
    for second, out in zip(seconds, outs):
        own = weight_from(weights, instances, me, me ^ second)
        other = weight_from(weights, instances, me ^ first, me ^ second)
        out[...] = own * state[...] + other * partner[...]


def around_flux(q, vc, p):
    return (q[2], q[1] * vc, q[2] * vc + p, (q[3] + p) * vc)


def flux_kernel(weight, instances, state, base, step):
    radial, around = state.shape[2:]
    q = [state[0, c] for c in range(4)]
    inverse, vr, vc, p = pressure_of(*q)
    a = jnp.sqrt(gamma_ratio * p * inverse)
    step[...] = cfl_number / (
        jnp.abs(vr) + jnp.abs(vc) + 2.0 * a + omega_rate * instances / 2.0
    )

    def after(x):
        return pltpu.roll(x, around - 1, 1)

    def above(x):
        return pltpu.roll(x, radial - 1, 0)

    column = lax.broadcasted_iota(jnp.int32, (radial, around), 1)
    row = lax.broadcasted_iota(jnp.int32, (radial, around), 0)
    hub, tip = row == 0, row == radial - 1
    speed = jnp.abs(vc) + a
    reach = 0.5 * jnp.maximum(speed, after(speed))
    speed = jnp.abs(vr) + a
    rise = 0.5 * jnp.maximum(speed, above(speed))
    flux = around_flux(q, vc, p)
    radial_flux = (q[1], q[1] * vr + p, q[2] * vr, (q[3] + p) * vr)
    for c in range(4):
        face = 0.5 * (flux[c] + after(flux[c])) - reach * (after(q[c]) - q[c])
        face = jnp.where(column == around - 1, 0.0, face)
        residual = weight * q[c] + (face - pltpu.roll(face, 1, 1))
        wall = p if c == 1 else 0.0
        face = 0.5 * (radial_flux[c] + above(radial_flux[c])) - rise * (above(q[c]) - q[c])
        upper = jnp.where(tip, wall, face)
        lower = jnp.where(hub, wall, pltpu.roll(face, 1, 0))
        base[0, c] = residual + (upper - lower)


def outer_kernel(weights, instances, orders, blocks, state, base, kept, came, partner, *refs):
    *edges, residual, total = refs
    radial, around = state.shape[2:]
    if blocks == RIDING:
        me = lax.axis_index("space")
        known = [kept[0, EDGE:, :], came[0, EDGE:, :]]
        known = jnp.concatenate(known, axis=0)
        row = lax.broadcasted_iota(jnp.int32, known.shape, 0)

        def edge_of(device):
            relative = device ^ me
            half = RIDING // 2
            chip = relative // 2
            place = jnp.where(chip == 3, 1, jnp.where(chip == 0, 0, chip + 1))
            place += (relative % 2) * half
            return jnp.sum(jnp.where(row == place, known, 0.0), axis=0, keepdims=True)

        before = edge_of((me + blocks - 1) % blocks)
        after = edge_of((me + 1) % blocks)
    else:
        before, after = (ref[0:1, :] for ref in edges)
    me = lax.axis_index("inst")
    weight = weight_from(weights, instances, me ^ of_chip(orders)[0], me)
    lane = lax.broadcasted_iota(jnp.int32, (1, LANES), 1)
    edge = jnp.where(lane < LANES // 2, before, after)
    edge = jnp.broadcast_to(edge, (8, LANES))

    sublane = lax.broadcasted_iota(jnp.int32, (8, LANES), 0)
    lane = lax.broadcasted_iota(jnp.int32, (radial, LANES), 1)
    left, right = lane == 0, lane == LANES - 1
    own, far = [], []
    for c in range(4):
        own.append(jnp.where(left, state[0, c, :, :LANES], state[0, c, :, around - LANES :]))
        halo = []
        for r in range(radial // 8):
            index = sublane + jnp.where(lane[:8] == LANES - 1, 4 * radial, 0) + c * radial + r * 8
            halo.append(jnp.take_along_axis(edge, index, axis=1, mode="promise_in_bounds"))
        far.append(jnp.concatenate(halo, axis=0))
    faces, speeds = [], []
    for q in (own, far):
        inverse, _, vc, p = pressure_of(*q)
        speeds.append(jnp.abs(vc) + jnp.sqrt(gamma_ratio * p * inverse))
        faces.append(around_flux(q, vc, p))
    side = jnp.where(right, 0.5, -0.5)
    reach = 0.5 * jnp.maximum(*speeds)
    for c in range(4):
        outer = side * (faces[0][c] + faces[1][c]) - reach * (far[c] - own[c])
        outer = [jnp.where(left, outer, 0.0), jnp.where(right, outer, 0.0)]
        middle = around - 2 * LANES
        if middle:
            outer.insert(1, jnp.zeros((radial, middle), jnp.float32))
        residual[0, c] = base[0, c] + weight * partner[0, c] + jnp.concatenate(outer, axis=1)

    total[...] = kept[0] + came[0]


def update_kernel(residual, step, total, *refs):
    *sums, increment_hbm, blade_hbm, increment, blade, sems = refs
    high = blade.shape[2] // LANES
    for k in range(3):
        for h in range(high):
            blade[k, :, pl.ds(h * LANES, LANES)] = total[k * high + h : k * high + h + 1, :]
    copies = [pltpu.make_async_copy(blade, blade_hbm, sems.at[0])]
    copies[0].start()
    for c in range(residual.shape[1]):
        change = functools.reduce(jnp.add, [ref[0, c] for ref in (residual, *sums)])
        increment[0, c] = -step[...] * change
        copy = pltpu.make_async_copy(increment.at[0, c], increment_hbm.at[0, c], sems.at[1 + c])
        copy.start()
        copies.append(copy)
    for copy in copies:
        copy.wait()


def per_device(node_block, state, face_cell, face_node, face_area):
    blocks = lax.axis_size("space")
    instances = lax.axis_size("inst")
    radial, around = state.shape[2:]
    chunks = face_cell.shape[0] // LANES
    vmem = pl.BlockSpec(memory_space=pltpu.VMEM)
    params = pltpu.CompilerParams(vmem_limit_bytes=(4 if blocks <= 16 else 16) * 2**20)

    def swapped(value, axis, bit):
        return lax.ppermute(value, axis, [(i, i ^ bit) for i in range(lax.axis_size(axis))])

    def shifted(value, axis, s):
        count = lax.axis_size(axis)
        return lax.ppermute(value, axis, [(i, (i + s) % count) for i in range(count)])

    def exchanged(sent, size):
        places = (3, 1, 2) if len(sent) == 3 else (1,)
        return [swapped(value, "space", place * size) for place, value in zip(places, sent)]

    def call(kernel, name, shapes, *operands, flops=0, dtype=jnp.float32):
        return pl.pallas_call(
            kernel,
            out_shape=[jax.ShapeDtypeStruct(shape, dtype) for shape in shapes],
            in_specs=[vmem] * len(operands),
            out_specs=[vmem] * len(shapes),
            compiler_params=params,
            cost_estimate=pl.CostEstimate(flops=flops, bytes_accessed=0, transcendentals=0),
            name=name,
        )(*operands)

    weights = spectral_row(instances)
    def partnered(value, place):
        pairs = [
            (i * instances + n, i * instances + (n ^ orders[i // 4 % 2][place]))
            for i in range(blocks)
            for n in range(instances)
        ]
        return lax.ppermute(value, ("space", "inst"), pairs)

    orders = ORDERS if instances == 4 else ((1, *range(2, instances, 2)),) * 2
    partner = partnered(state, 0)

    riding = blocks == RIDING
    steps = [4, 2] if riding else [2] * (blocks.bit_length() - 1)
    size = blocks // steps[0]
    (own,) = call(
        functools.partial(own_kernel, node_block // LANES),
        "own",
        [(8, LANES)],
        dtype=jnp.int32,
        flops=PLACING,
    )
    kept, *sent = call(
        functools.partial(forces_kernel, node_block),
        "face_forces",
        [(size, ROWS, LANES)] * steps[0],
        own,
        state,
        face_cell.reshape(chunks, LANES),
        face_node.reshape(chunks, LANES),
        face_area,
        flops=PLACING,
    )

    edges = []
    if not riding:
        row = jnp.broadcast_to(kept[0, EDGE : EDGE + 1, :], (8, LANES))
        edges = [shifted(row, "space", 1), shifted(row, "space", blocks - 1)]

    came = exchanged(sent, size)
    sums = call(
        functools.partial(pair_kernel, weights, instances, orders),
        "pair_sums",
        [state.shape] * (len(orders[0]) - 1),
        state,
        partner,
        flops=PLACING,
    )
    sums = [partnered(value, i) for i, value in enumerate(sums, 1)]

    for step in steps[1:]:
        size //= step
        kept, *sent = call(
            functools.partial(halving_kernel, 1 + len(came), riding),
            "halving",
            [(size, ROWS, LANES)] * step,
            kept,
            *came,
            flops=PLACING,
        )
        came = exchanged(sent, size)

    base, step = call(
        functools.partial(flux_kernel, weights[0], instances),
        "flux",
        [state.shape, (radial, around)],
        state,
    )
    residual, total = call(
        functools.partial(outer_kernel, weights, instances, orders, blocks),
        "outer",
        [state.shape, (ROWS, LANES)],
        state,
        base,
        kept,
        *came,
        partner,
        *edges,
    )
    results = [
        jax.ShapeDtypeStruct(state.shape, jnp.float32),
        jax.ShapeDtypeStruct((3, 1, node_block), jnp.float32),
    ]
    increment, blade = pl.pallas_call(
        update_kernel,
        out_shape=results,
        in_specs=[vmem] * (3 + len(sums)),
        out_specs=[pl.BlockSpec(memory_space=pltpu.HBM)] * 2,
        scratch_shapes=[pltpu.VMEM(x.shape, x.dtype) for x in results]
        + [pltpu.SemaphoreType.DMA((5,))],
        compiler_params=params,
        cost_estimate=pl.CostEstimate(flops=0, bytes_accessed=0, transcendentals=0),
        name="update",
    )(residual, step, total, *sums)
    return increment, jnp.transpose(blade, (1, 0, 2))


def solution(mesh):
    in_specs = (P("inst", None, None, "space"), P("space"), P("space"), P(None, "space"))
    out_specs = (P("inst", None, None, "space"), P("inst", None, "space"))
    return jax.shard_map(
        functools.partial(per_device, 512),
        mesh=mesh,
        in_specs=in_specs,
        out_specs=out_specs,
        check_vma=False,
    )
```

```python
import functools
import math

import jax
import jax.numpy as jnp
import numpy as np
from jax import lax
from jax.experimental import pallas as pl
from jax.experimental.pallas import tpu as pltpu
from jax.sharding import PartitionSpec as P

gamma_ratio = 1.4
omega_rate = 0.5
cfl_number = 0.8

LANES = 128
ROWS = 16
EDGE = 12
PLACING = 10**10
ORDERS = ((2, 1), (1, 2))
RIDING = 8


def spectral_row(count):
    row = np.zeros((count,), np.float32)
    for shift in range(count):
        row[shift] = (-1.0) ** shift / count
        if shift != 0:
            row[shift] += 0.5 * (-1.0) ** shift / math.tan(math.pi * shift / count)
    return [float(omega_rate * value) for value in row]


def pressure_of(q0, q1, q2, q3):
    inverse = 1.0 / q0
    vr = q1 * inverse
    vc = q2 * inverse
    p = (gamma_ratio - 1.0) * (q3 - 0.5 * q0 * (vr * vr + vc * vc))
    return inverse, vr, vc, p


def own_kernel(high, riding, out):
    me = lax.axis_index("space")
    out[...] = jnp.full(out.shape, (me - me % 2 if riding else me) * high, jnp.int32)


def split(value, size):
    return value >> (size.bit_length() - 1), value & (size - 1)


def forces_kernel(node_block, own, state, cell, node, area, *outs):
    radial, around = state.shape[2:]
    faces = cell.shape[0] * LANES
    chunks = faces // LANES
    _, _, _, p = pressure_of(state[0, 0], state[0, 1], state[0, 2], state[0, 3])
    sublane = lax.broadcasted_iota(jnp.int32, (8, LANES), 0)
    picked = []
    for c in range(chunks):
        tile, lane = split(jnp.broadcast_to(cell[c : c + 1, :], (8, LANES)), LANES)
        total = jnp.zeros((8, LANES), jnp.float32)
        for r in range(radial // 8):
            for h in range(around // LANES):
                part = p[r * 8 : (r + 1) * 8, h * LANES : (h + 1) * LANES]
                value = jnp.take_along_axis(part, lane, axis=1, mode="promise_in_bounds")
                place = (sublane + r * 8) * (around // LANES) + h
                total += jnp.where(tile == place, value, 0.0)
        for turn in (4, 2, 1):
            total += pltpu.roll(total, turn, 0)
        picked.append(total)
    face_pressure = jnp.concatenate(picked, axis=1)
    nodes = jnp.concatenate([node[c : c + 1, :] for c in range(chunks)], axis=1)

    high = node_block // LANES
    place, low = split(nodes, LANES)
    place = place ^ jnp.broadcast_to(own[0:1, 0:1], nodes.shape)
    pick_low = (
        lax.broadcasted_iota(jnp.int32, (LANES, faces), 0) == jnp.broadcast_to(low, (LANES, faces))
    ).astype(jnp.float32).astype(jnp.bfloat16)

    row = lax.broadcasted_iota(jnp.int32, (8, faces), 0)
    x, y, z = (face_pressure * jnp.broadcast_to(area[k : k + 1, :], (8, faces)) for k in range(3))
    groups = []
    for pattern in (jnp.where(row < high, x, y), jnp.where(row < high, z, 0.0)):
        first = pattern.astype(jnp.bfloat16).astype(jnp.float32)
        groups.append((first, pattern - first))
    away = jnp.broadcast_to(place, (8, faces)) - (row & (high - 1))

    def dense(start, count):
        masks = [away == (start + b) * high for b in range(count)]
        left = [jnp.where(m, g[i], 0.0) for i in range(2) for m in masks for g in groups]
        product = lax.dot_general(
            jnp.concatenate(left, axis=0).astype(jnp.bfloat16),
            pick_low,
            (((1,), (1,)), ((), ())),
            preferred_element_type=jnp.float32,
        )
        rows = count * ROWS
        return (product[:rows] + product[rows:]).reshape(count, ROWS, LANES)

    size = outs[0].shape[0]
    core = lax.axis_index("space") % 2
    if len(outs) == 4:
        mine, east, north, diagonal = dense(0, 4 * size).reshape(4, size, ROWS, LANES)
        others = (jnp.where(core == 0, east, north), jnp.where(core == 0, north, east))
        for out, part in zip(outs, (mine, diagonal, *others)):
            out[...] = part
    else:
        for i, out in enumerate(outs):

            @pl.loop(0, size // 8)
            def _(g):
                out[pl.ds(g * 8, 8)] = dense(i * size + g * 8, 8)

    lane = lax.broadcasted_iota(jnp.int32, (8, LANES), 1)
    columns = jnp.zeros((8, LANES), jnp.float32)
    for i, column in enumerate((around - 1, 0)):
        tile, index = divmod(column, LANES)
        index = jnp.full((8, LANES), index, jnp.int32)
        for c in range(4):
            for r in range(radial // 8):
                part = state[0, c, r * 8 : (r + 1) * 8, tile * LANES : (tile + 1) * LANES]
                value = jnp.take_along_axis(part, index, axis=1, mode="promise_in_bounds")
                place = (i * 4 + c) * radial + r * 8
                columns = jnp.where(lane == sublane + place, value, columns)
    edge = jnp.sum(columns, axis=0, keepdims=True)
    row = lax.broadcasted_iota(jnp.int32, (2, LANES), 0)
    pair = jnp.where(row == core, edge, 0.0) if len(outs) == 4 else jnp.where(row == 0, edge, 0.0)
    for out in outs:
        out[0, EDGE : EDGE + 2, :] = pair


def chip_kernel(kept, came, _, out):
    out[...] = kept[...] + came[...]


def plane_kernel(mine, diagonal, served, kept, sent):
    core = lax.axis_index("space") % 2
    first, second = (mine[b] + diagonal[b] + served[b] for b in range(2))
    kept[0] = jnp.where(core == 0, first, second)
    sent[0] = jnp.where(core == 0, second, first)
    rows = [
        jnp.where(core == 0, ref[0, EDGE : EDGE + 1, :], ref[0, EDGE + 1 : EDGE + 2, :])
        for ref in (mine, diagonal)
    ] + [served[0, EDGE : EDGE + 1, :], served[0, EDGE + 1 : EDGE + 2, :]]
    for out in (kept, sent):
        for i, edge in enumerate(rows):
            out[0, EDGE + i : EDGE + i + 1, :] = edge


def halving_kernel(kept, came, *outs):
    size = outs[0].shape[0]
    for i, out in enumerate(outs):
        for b in range(size):
            out[b] = kept[i * size + b] + came[i * size + b]


def weight_from(weights, instances, source, target):
    shift = (target - source + instances) % instances
    value = weights[0]
    for i in range(1, instances):
        value = jnp.where(shift == i, weights[i], value)
    return value


def of_chip(orders):
    half = lax.axis_index("space") // 4
    return [jnp.where(half % 2 == 0, a, b) for a, b in zip(*orders)]


def pair_kernel(weights, instances, orders, state, partner, *outs):
    me = lax.axis_index("inst")
    first, *seconds = of_chip(orders)
    for second, out in zip(seconds, outs):
        own = weight_from(weights, instances, me, me ^ second)
        other = weight_from(weights, instances, me ^ first, me ^ second)
        out[...] = own * state[...] + other * partner[...]


def around_flux(q, vc, p):
    return (q[2], q[1] * vc, q[2] * vc + p, (q[3] + p) * vc)


def flux_kernel(weight, instances, state, base, step):
    radial, around = state.shape[2:]
    q = [state[0, c] for c in range(4)]
    inverse, vr, vc, p = pressure_of(*q)
    a = jnp.sqrt(gamma_ratio * p * inverse)
    step[...] = cfl_number / (
        jnp.abs(vr) + jnp.abs(vc) + 2.0 * a + omega_rate * instances / 2.0
    )

    def after(x):
        return pltpu.roll(x, around - 1, 1)

    def above(x):
        return pltpu.roll(x, radial - 1, 0)

    column = lax.broadcasted_iota(jnp.int32, (radial, around), 1)
    row = lax.broadcasted_iota(jnp.int32, (radial, around), 0)
    hub, tip = row == 0, row == radial - 1
    speed = jnp.abs(vc) + a
    reach = 0.5 * jnp.maximum(speed, after(speed))
    speed = jnp.abs(vr) + a
    rise = 0.5 * jnp.maximum(speed, above(speed))
    flux = around_flux(q, vc, p)
    radial_flux = (q[1], q[1] * vr + p, q[2] * vr, (q[3] + p) * vr)
    for c in range(4):
        face = 0.5 * (flux[c] + after(flux[c])) - reach * (after(q[c]) - q[c])
        face = jnp.where(column == around - 1, 0.0, face)
        residual = weight * q[c] + (face - pltpu.roll(face, 1, 1))
        wall = p if c == 1 else 0.0
        face = 0.5 * (radial_flux[c] + above(radial_flux[c])) - rise * (above(q[c]) - q[c])
        upper = jnp.where(tip, wall, face)
        lower = jnp.where(hub, wall, pltpu.roll(face, 1, 0))
        base[0, c] = residual + (upper - lower)


def outer_kernel(weights, instances, orders, blocks, state, base, kept, came, partner, *refs):
    *edges, residual, total = refs
    radial, around = state.shape[2:]
    if blocks == RIDING:
        me = lax.axis_index("space")
        core = me % 2
        known = [kept[0, EDGE:, :], came[0, EDGE:, :]]
        known = [
            jnp.where(core == 0, known[0], known[1]),
            jnp.where(core == 0, known[1], known[0]),
        ]
        known = jnp.concatenate(known, axis=0)
        row = lax.broadcasted_iota(jnp.int32, known.shape, 0)

        def edge_of(device):
            chip, of_core = (device ^ (me - core)) // 2, device % 2
            place = jnp.where(chip == 1, 6 + of_core, 2 + of_core)
            place = jnp.where(chip == 0, 4 * of_core, place)
            place = jnp.where(chip == 3, 1 + 4 * of_core, place)
            return jnp.sum(jnp.where(row == place, known, 0.0), axis=0, keepdims=True)

        before = edge_of((me + blocks - 1) % blocks)
        after = edge_of((me + 1) % blocks)
    else:
        before, after = (ref[0:1, :] for ref in edges)
    me = lax.axis_index("inst")
    weight = weight_from(weights, instances, me ^ of_chip(orders)[0], me)
    lane = lax.broadcasted_iota(jnp.int32, (1, LANES), 1)
    edge = jnp.where(lane < LANES // 2, before, after)
    edge = jnp.broadcast_to(edge, (8, LANES))

    sublane = lax.broadcasted_iota(jnp.int32, (8, LANES), 0)
    lane = lax.broadcasted_iota(jnp.int32, (radial, LANES), 1)
    left, right = lane == 0, lane == LANES - 1
    own, far = [], []
    for c in range(4):
        own.append(jnp.where(left, state[0, c, :, :LANES], state[0, c, :, around - LANES :]))
        halo = []
        for r in range(radial // 8):
            index = sublane + jnp.where(lane[:8] == LANES - 1, 4 * radial, 0) + c * radial + r * 8
            halo.append(jnp.take_along_axis(edge, index, axis=1, mode="promise_in_bounds"))
        far.append(jnp.concatenate(halo, axis=0))
    faces, speeds = [], []
    for q in (own, far):
        inverse, _, vc, p = pressure_of(*q)
        speeds.append(jnp.abs(vc) + jnp.sqrt(gamma_ratio * p * inverse))
        faces.append(around_flux(q, vc, p))
    side = jnp.where(right, 0.5, -0.5)
    reach = 0.5 * jnp.maximum(*speeds)
    for c in range(4):
        outer = side * (faces[0][c] + faces[1][c]) - reach * (far[c] - own[c])
        outer = [jnp.where(left, outer, 0.0), jnp.where(right, outer, 0.0)]
        middle = around - 2 * LANES
        if middle:
            outer.insert(1, jnp.zeros((radial, middle), jnp.float32))
        residual[0, c] = base[0, c] + weight * partner[0, c] + jnp.concatenate(outer, axis=1)

    total[...] = kept[0] + came[0]


def update_kernel(residual, step, total, *refs):
    *sums, increment, blade = refs
    high = blade.shape[2] // LANES
    for k in range(3):
        for h in range(high):
            blade[k, :, pl.ds(h * LANES, LANES)] = total[k * high + h : k * high + h + 1, :]
    for c in range(residual.shape[1]):
        change = functools.reduce(jnp.add, [ref[0, c] for ref in (residual, *sums)])
        increment[0, c] = -step[...] * change


def per_device(node_block, state, face_cell, face_node, face_area):
    blocks = lax.axis_size("space")
    instances = lax.axis_size("inst")
    radial, around = state.shape[2:]
    chunks = face_cell.shape[0] // LANES
    vmem = pl.BlockSpec(memory_space=pltpu.VMEM)
    params = pltpu.CompilerParams(vmem_limit_bytes=(4 if blocks <= 16 else 16) * 2**20)

    def swapped(value, axis, bit):
        return lax.ppermute(value, axis, [(i, i ^ bit) for i in range(lax.axis_size(axis))])

    def shifted(value, axis, s):
        count = lax.axis_size(axis)
        return lax.ppermute(value, axis, [(i, (i + s) % count) for i in range(count)])

    def served(value):
        pairs = [(i, i ^ (2 if i % 2 else 4)) for i in range(blocks)]
        return lax.ppermute(value, "space", pairs)

    def call(kernel, name, shapes, *operands, flops=0, dtype=jnp.float32):
        return pl.pallas_call(
            kernel,
            out_shape=[jax.ShapeDtypeStruct(shape, dtype) for shape in shapes],
            in_specs=[vmem] * len(operands),
            out_specs=[vmem] * len(shapes),
            compiler_params=params,
            cost_estimate=pl.CostEstimate(flops=flops, bytes_accessed=0, transcendentals=0),
            name=name,
        )(*operands)

    weights = spectral_row(instances)
    def partnered(value, place):
        pairs = [
            (i * instances + n, i * instances + (n ^ orders[i // 4 % 2][place]))
            for i in range(blocks)
            for n in range(instances)
        ]
        return lax.ppermute(value, ("space", "inst"), pairs)

    orders = ORDERS if instances == 4 else ((1, *range(2, instances, 2)),) * 2
    partner = partnered(state, 0)

    riding = blocks == RIDING
    parts = 4 if riding else 2
    (own,) = call(
        functools.partial(own_kernel, node_block // LANES, riding),
        "own",
        [(8, LANES)],
        dtype=jnp.int32,
        flops=PLACING,
    )
    dense = call(
        functools.partial(forces_kernel, node_block),
        "face_forces",
        [(blocks // parts, ROWS, LANES)] * parts,
        own,
        state,
        face_cell.reshape(chunks, LANES),
        face_node.reshape(chunks, LANES),
        face_area,
        flops=PLACING,
    )

    base, step = call(
        functools.partial(flux_kernel, weights[0], instances),
        "flux",
        [state.shape, (radial, around)],
        state,
        flops=PLACING,
    )
    edges = []
    if riding:
        mine, across, other, kept = dense
        other = swapped(other, "space", 1)
        across = swapped(across, "space", 6)
        (kept,) = call(chip_kernel, "chip_sums", [kept.shape], kept, other, step, flops=PLACING)
        kept, sent = call(
            plane_kernel,
            "plane_sums",
            [(1, ROWS, LANES)] * 2,
            mine,
            across,
            served(kept),
            flops=PLACING,
        )
        came = swapped(sent, "space", 1)
    else:
        row = jnp.broadcast_to(dense[0][0, EDGE : EDGE + 1, :], (8, LANES))
        edges = [shifted(row, "space", 1), shifted(row, "space", blocks - 1)]
        size = blocks // 2
        kept, came = dense[0], swapped(dense[1], "space", size)
        while size > 1:
            size //= 2
            shapes = [(size, ROWS, LANES)] * 2
            kept, sent = call(halving_kernel, "halving", shapes, kept, came)
            came = swapped(sent, "space", size)

    sums = call(
        functools.partial(pair_kernel, weights, instances, orders),
        "pair_sums",
        [state.shape] * (len(orders[0]) - 1),
        state,
        partner,
        flops=PLACING,
    )
    sums = [partnered(value, i) for i, value in enumerate(sums, 1)]

    residual, total = call(
        functools.partial(outer_kernel, weights, instances, orders, blocks),
        "outer",
        [state.shape, (ROWS, LANES)],
        state,
        base,
        kept,
        came,
        partner,
        *edges,
    )
    increment, blade = call(
        update_kernel,
        "update",
        [state.shape, (3, 1, node_block)],
        residual,
        step,
        total,
        *sums,
    )
    return increment, jnp.transpose(blade, (1, 0, 2))


def solution(mesh):
    in_specs = (P("inst", None, None, "space"), P("space"), P("space"), P(None, "space"))
    out_specs = (P("inst", None, None, "space"), P("inst", None, "space"))
    return jax.shard_map(
        functools.partial(per_device, 512),
        mesh=mesh,
        in_specs=in_specs,
        out_specs=out_specs,
        check_vma=False,
    )
```

```python
import functools
import math

import jax
import jax.numpy as jnp
import numpy as np
from jax import lax
from jax.experimental import pallas as pl
from jax.experimental.pallas import tpu as pltpu
from jax.sharding import PartitionSpec as P

gamma_ratio = 1.4
omega_rate = 0.5
cfl_number = 0.8

LANES = 128
ROWS = 16
EDGE = 12
PLACING = 10**10
ORDERS = ((2, 1), (1, 2))
RIDING = 8


def spectral_row(count):
    row = np.zeros((count,), np.float32)
    for shift in range(count):
        row[shift] = (-1.0) ** shift / count
        if shift != 0:
            row[shift] += 0.5 * (-1.0) ** shift / math.tan(math.pi * shift / count)
    return [float(omega_rate * value) for value in row]


def pressure_of(q0, q1, q2, q3):
    inverse = 1.0 / q0
    vr = q1 * inverse
    vc = q2 * inverse
    p = (gamma_ratio - 1.0) * (q3 - 0.5 * q0 * (vr * vr + vc * vc))
    return inverse, vr, vc, p


def own_kernel(high, riding, out):
    me = lax.axis_index("space")
    out[...] = jnp.full(out.shape, (me - me % 2 if riding else me) * high, jnp.int32)


def split(value, size):
    return value >> (size.bit_length() - 1), value & (size - 1)


def forces_kernel(node_block, own, state, cell, node, area, *outs):
    radial, around = state.shape[2:]
    faces = cell.shape[0] * LANES
    chunks = faces // LANES
    _, _, _, p = pressure_of(state[0, 0], state[0, 1], state[0, 2], state[0, 3])
    sublane = lax.broadcasted_iota(jnp.int32, (8, LANES), 0)
    picked = []
    for c in range(chunks):
        tile, lane = split(jnp.broadcast_to(cell[c : c + 1, :], (8, LANES)), LANES)
        total = jnp.zeros((8, LANES), jnp.float32)
        for r in range(radial // 8):
            for h in range(around // LANES):
                part = p[r * 8 : (r + 1) * 8, h * LANES : (h + 1) * LANES]
                value = jnp.take_along_axis(part, lane, axis=1, mode="promise_in_bounds")
                place = (sublane + r * 8) * (around // LANES) + h
                total += jnp.where(tile == place, value, 0.0)
        for turn in (4, 2, 1):
            total += pltpu.roll(total, turn, 0)
        picked.append(total)
    face_pressure = jnp.concatenate(picked, axis=1)
    nodes = jnp.concatenate([node[c : c + 1, :] for c in range(chunks)], axis=1)

    high = node_block // LANES
    place, low = split(nodes, LANES)
    place = place ^ jnp.broadcast_to(own[0:1, 0:1], nodes.shape)
    pick_low = (
        lax.broadcasted_iota(jnp.int32, (LANES, faces), 0) == jnp.broadcast_to(low, (LANES, faces))
    ).astype(jnp.float32).astype(jnp.bfloat16)

    row = lax.broadcasted_iota(jnp.int32, (8, faces), 0)
    x, y, z = (face_pressure * jnp.broadcast_to(area[k : k + 1, :], (8, faces)) for k in range(3))
    groups = []
    for pattern in (jnp.where(row < high, x, y), jnp.where(row < high, z, 0.0)):
        first = pattern.astype(jnp.bfloat16).astype(jnp.float32)
        groups.append((first, pattern - first))
    away = jnp.broadcast_to(place, (8, faces)) - (row & (high - 1))

    def dense(start, count):
        masks = [away == (start + b) * high for b in range(count)]
        left = [jnp.where(m, g[i], 0.0) for i in range(2) for m in masks for g in groups]
        product = lax.dot_general(
            jnp.concatenate(left, axis=0).astype(jnp.bfloat16),
            pick_low,
            (((1,), (1,)), ((), ())),
            preferred_element_type=jnp.float32,
        )
        rows = count * ROWS
        return (product[:rows] + product[rows:]).reshape(count, ROWS, LANES)

    size = outs[0].shape[0]
    core = lax.axis_index("space") % 2
    if len(outs) == 4:
        mine, east, north, diagonal = dense(0, 4 * size).reshape(4, size, ROWS, LANES)
        others = (jnp.where(core == 0, east, north), jnp.where(core == 0, north, east))
        for out, part in zip(outs, (mine, diagonal, *others)):
            out[...] = part
    else:
        for i, out in enumerate(outs):

            @pl.loop(0, size // 8)
            def _(g):
                out[pl.ds(g * 8, 8)] = dense(i * size + g * 8, 8)

    lane = lax.broadcasted_iota(jnp.int32, (8, LANES), 1)
    columns = jnp.zeros((8, LANES), jnp.float32)
    for i, column in enumerate((around - 1, 0)):
        tile, index = divmod(column, LANES)
        index = jnp.full((8, LANES), index, jnp.int32)
        for c in range(4):
            for r in range(radial // 8):
                part = state[0, c, r * 8 : (r + 1) * 8, tile * LANES : (tile + 1) * LANES]
                value = jnp.take_along_axis(part, index, axis=1, mode="promise_in_bounds")
                place = (i * 4 + c) * radial + r * 8
                columns = jnp.where(lane == sublane + place, value, columns)
    edge = jnp.sum(columns, axis=0, keepdims=True)
    row = lax.broadcasted_iota(jnp.int32, (2, LANES), 0)
    pair = jnp.where(row == core, edge, 0.0) if len(outs) == 4 else jnp.where(row == 0, edge, 0.0)
    for out in outs:
        out[0, EDGE : EDGE + 2, :] = pair


def chip_kernel(kept, came, _, out):
    out[...] = kept[...] + came[...]


def plane_kernel(mine, diagonal, served, kept, sent):
    core = lax.axis_index("space") % 2
    first, second = (mine[b] + diagonal[b] + served[b] for b in range(2))
    kept[0] = jnp.where(core == 0, first, second)
    sent[0] = jnp.where(core == 0, second, first)
    rows = [
        jnp.where(core == 0, ref[0, EDGE : EDGE + 1, :], ref[0, EDGE + 1 : EDGE + 2, :])
        for ref in (mine, diagonal)
    ] + [served[0, EDGE : EDGE + 1, :], served[0, EDGE + 1 : EDGE + 2, :]]
    for out in (kept, sent):
        for i, edge in enumerate(rows):
            out[0, EDGE + i : EDGE + i + 1, :] = edge


def halving_kernel(kept, came, *outs):
    size = outs[0].shape[0]
    for i, out in enumerate(outs):
        for b in range(size):
            out[b] = kept[i * size + b] + came[i * size + b]


def weight_from(weights, instances, source, target):
    shift = (target - source + instances) % instances
    value = weights[0]
    for i in range(1, instances):
        value = jnp.where(shift == i, weights[i], value)
    return value


def of_chip(orders):
    chip = lax.axis_index("space") // 2
    return [jnp.where(chip == 0, a, b) for a, b in zip(*orders)]


def pair_kernel(weights, instances, orders, state, partner, *outs):
    me = lax.axis_index("inst")
    first, *seconds = of_chip(orders)
    for second, out in zip(seconds, outs):
        own = weight_from(weights, instances, me, me ^ second)
        other = weight_from(weights, instances, me ^ first, me ^ second)
        out[...] = own * state[...] + other * partner[...]


def around_flux(q, vc, p):
    return (q[2], q[1] * vc, q[2] * vc + p, (q[3] + p) * vc)


def flux_kernel(weight, instances, state, base, step):
    radial, around = state.shape[2:]
    q = [state[0, c] for c in range(4)]
    inverse, vr, vc, p = pressure_of(*q)
    a = jnp.sqrt(gamma_ratio * p * inverse)
    step[...] = cfl_number / (
        jnp.abs(vr) + jnp.abs(vc) + 2.0 * a + omega_rate * instances / 2.0
    )

    def after(x):
        return pltpu.roll(x, around - 1, 1)

    def above(x):
        return pltpu.roll(x, radial - 1, 0)

    column = lax.broadcasted_iota(jnp.int32, (radial, around), 1)
    row = lax.broadcasted_iota(jnp.int32, (radial, around), 0)
    hub, tip = row == 0, row == radial - 1
    speed = jnp.abs(vc) + a
    reach = 0.5 * jnp.maximum(speed, after(speed))
    speed = jnp.abs(vr) + a
    rise = 0.5 * jnp.maximum(speed, above(speed))
    flux = around_flux(q, vc, p)
    radial_flux = (q[1], q[1] * vr + p, q[2] * vr, (q[3] + p) * vr)
    for c in range(4):
        face = 0.5 * (flux[c] + after(flux[c])) - reach * (after(q[c]) - q[c])
        face = jnp.where(column == around - 1, 0.0, face)
        residual = weight * q[c] + (face - pltpu.roll(face, 1, 1))
        wall = p if c == 1 else 0.0
        face = 0.5 * (radial_flux[c] + above(radial_flux[c])) - rise * (above(q[c]) - q[c])
        upper = jnp.where(tip, wall, face)
        lower = jnp.where(hub, wall, pltpu.roll(face, 1, 0))
        base[0, c] = residual + (upper - lower)


def outer_kernel(weights, instances, orders, blocks, state, base, kept, came, partner, *refs):
    *edges, residual, total = refs
    radial, around = state.shape[2:]
    if blocks == RIDING:
        me = lax.axis_index("space")
        core = me % 2
        known = [kept[0, EDGE:, :], came[0, EDGE:, :]]
        known = [
            jnp.where(core == 0, known[0], known[1]),
            jnp.where(core == 0, known[1], known[0]),
        ]
        known = jnp.concatenate(known, axis=0)
        row = lax.broadcasted_iota(jnp.int32, known.shape, 0)

        def edge_of(device):
            chip, of_core = (device ^ (me - core)) // 2, device % 2
            place = jnp.where(chip == 1, 6 + of_core, 2 + of_core)
            place = jnp.where(chip == 0, 4 * of_core, place)
            place = jnp.where(chip == 3, 1 + 4 * of_core, place)
            return jnp.sum(jnp.where(row == place, known, 0.0), axis=0, keepdims=True)

        before = edge_of((me + blocks - 1) % blocks)
        after = edge_of((me + 1) % blocks)
    else:
        before, after = (ref[0:1, :] for ref in edges)
    me = lax.axis_index("inst")
    weight = weight_from(weights, instances, me ^ of_chip(orders)[0], me)
    lane = lax.broadcasted_iota(jnp.int32, (1, LANES), 1)
    edge = jnp.where(lane < LANES // 2, before, after)
    edge = jnp.broadcast_to(edge, (8, LANES))

    sublane = lax.broadcasted_iota(jnp.int32, (8, LANES), 0)
    lane = lax.broadcasted_iota(jnp.int32, (radial, LANES), 1)
    left, right = lane == 0, lane == LANES - 1
    own, far = [], []
    for c in range(4):
        own.append(jnp.where(left, state[0, c, :, :LANES], state[0, c, :, around - LANES :]))
        halo = []
        for r in range(radial // 8):
            index = sublane + jnp.where(lane[:8] == LANES - 1, 4 * radial, 0) + c * radial + r * 8
            halo.append(jnp.take_along_axis(edge, index, axis=1, mode="promise_in_bounds"))
        far.append(jnp.concatenate(halo, axis=0))
    faces, speeds = [], []
    for q in (own, far):
        inverse, _, vc, p = pressure_of(*q)
        speeds.append(jnp.abs(vc) + jnp.sqrt(gamma_ratio * p * inverse))
        faces.append(around_flux(q, vc, p))
    side = jnp.where(right, 0.5, -0.5)
    reach = 0.5 * jnp.maximum(*speeds)
    for c in range(4):
        outer = side * (faces[0][c] + faces[1][c]) - reach * (far[c] - own[c])
        outer = [jnp.where(left, outer, 0.0), jnp.where(right, outer, 0.0)]
        middle = around - 2 * LANES
        if middle:
            outer.insert(1, jnp.zeros((radial, middle), jnp.float32))
        residual[0, c] = base[0, c] + weight * partner[0, c] + jnp.concatenate(outer, axis=1)

    total[...] = kept[0] + came[0]


def update_kernel(residual, step, total, *refs):
    *sums, increment, blade = refs
    high = blade.shape[2] // LANES
    for k in range(3):
        for h in range(high):
            blade[k, :, pl.ds(h * LANES, LANES)] = total[k * high + h : k * high + h + 1, :]
    for c in range(residual.shape[1]):
        change = functools.reduce(jnp.add, [ref[0, c] for ref in (residual, *sums)])
        increment[0, c] = -step[...] * change


def per_device(node_block, state, face_cell, face_node, face_area):
    blocks = lax.axis_size("space")
    instances = lax.axis_size("inst")
    radial, around = state.shape[2:]
    chunks = face_cell.shape[0] // LANES
    vmem = pl.BlockSpec(memory_space=pltpu.VMEM)
    params = pltpu.CompilerParams(vmem_limit_bytes=(4 if blocks <= 16 else 16) * 2**20)

    def swapped(value, axis, bit):
        return lax.ppermute(value, axis, [(i, i ^ bit) for i in range(lax.axis_size(axis))])

    def shifted(value, axis, s):
        count = lax.axis_size(axis)
        return lax.ppermute(value, axis, [(i, (i + s) % count) for i in range(count)])

    def served(value):
        pairs = [(i, i ^ (2 if i % 2 else 4)) for i in range(blocks)]
        return lax.ppermute(value, "space", pairs)

    def call(kernel, name, shapes, *operands, flops=0, dtype=jnp.float32):
        return pl.pallas_call(
            kernel,
            out_shape=[jax.ShapeDtypeStruct(shape, dtype) for shape in shapes],
            in_specs=[vmem] * len(operands),
            out_specs=[vmem] * len(shapes),
            compiler_params=params,
            cost_estimate=pl.CostEstimate(flops=flops, bytes_accessed=0, transcendentals=0),
            name=name,
        )(*operands)

    weights = spectral_row(instances)
    def partnered(value, place):
        pairs = [
            (i * instances + n, i * instances + (n ^ orders[min(i // 2, 1)][place]))
            for i in range(blocks)
            for n in range(instances)
        ]
        return lax.ppermute(value, ("space", "inst"), pairs)

    orders = ORDERS if instances == 4 else ((1, *range(2, instances, 2)),) * 2
    partner = partnered(state, 0)

    riding = blocks == RIDING
    parts = 4 if riding else 2
    (own,) = call(
        functools.partial(own_kernel, node_block // LANES, riding),
        "own",
        [(8, LANES)],
        dtype=jnp.int32,
        flops=PLACING,
    )
    dense = call(
        functools.partial(forces_kernel, node_block),
        "face_forces",
        [(blocks // parts, ROWS, LANES)] * parts,
        own,
        state,
        face_cell.reshape(chunks, LANES),
        face_node.reshape(chunks, LANES),
        face_area,
        flops=PLACING,
    )

    base, step = call(
        functools.partial(flux_kernel, weights[0], instances),
        "flux",
        [state.shape, (radial, around)],
        state,
        flops=PLACING,
    )
    edges = []
    if riding:
        mine, across, other, kept = dense
        other = swapped(other, "space", 1)
        across = swapped(across, "space", 6)
        (kept,) = call(chip_kernel, "chip_sums", [kept.shape], kept, other, step, flops=PLACING)
        kept, sent = call(
            plane_kernel,
            "plane_sums",
            [(1, ROWS, LANES)] * 2,
            mine,
            across,
            served(kept),
            flops=PLACING,
        )
        came = swapped(sent, "space", 1)
    else:
        row = jnp.broadcast_to(dense[0][0, EDGE : EDGE + 1, :], (8, LANES))
        edges = [shifted(row, "space", 1), shifted(row, "space", blocks - 1)]
        size = blocks // 2
        kept, came = dense[0], swapped(dense[1], "space", size)
        while size > 1:
            size //= 2
            shapes = [(size, ROWS, LANES)] * 2
            kept, sent = call(halving_kernel, "halving", shapes, kept, came)
            came = swapped(sent, "space", size)

    sums = call(
        functools.partial(pair_kernel, weights, instances, orders),
        "pair_sums",
        [state.shape] * (len(orders[0]) - 1),
        state,
        partner,
        flops=PLACING,
    )
    sums = [partnered(value, i) for i, value in enumerate(sums, 1)]

    residual, total = call(
        functools.partial(outer_kernel, weights, instances, orders, blocks),
        "outer",
        [state.shape, (ROWS, LANES)],
        state,
        base,
        kept,
        came,
        partner,
        *edges,
    )
    increment, blade = call(
        update_kernel,
        "update",
        [state.shape, (3, 1, node_block)],
        residual,
        step,
        total,
        *sums,
    )
    return increment, jnp.transpose(blade, (1, 0, 2))


def solution(mesh):
    in_specs = (P("inst", None, None, "space"), P("space"), P("space"), P(None, "space"))
    out_specs = (P("inst", None, None, "space"), P("inst", None, "space"))
    return jax.shard_map(
        functools.partial(per_device, 512),
        mesh=mesh,
        in_specs=in_specs,
        out_specs=out_specs,
        check_vma=False,
    )
```

```python
import functools
import math

import jax
import jax.numpy as jnp
import numpy as np
from jax import lax
from jax.experimental import pallas as pl
from jax.experimental.pallas import tpu as pltpu
from jax.sharding import PartitionSpec as P

gamma_ratio = 1.4
omega_rate = 0.5
cfl_number = 0.8

LANES = 128
ROWS = 16
EDGE = 12
PLACING = 10**10
ORDERS = ((2, 1), (1, 2))
RIDING = 8


def spectral_row(count):
    row = np.zeros((count,), np.float32)
    for shift in range(count):
        row[shift] = (-1.0) ** shift / count
        if shift != 0:
            row[shift] += 0.5 * (-1.0) ** shift / math.tan(math.pi * shift / count)
    return [float(omega_rate * value) for value in row]


def pressure_of(q0, q1, q2, q3):
    inverse = 1.0 / q0
    vr = q1 * inverse
    vc = q2 * inverse
    p = (gamma_ratio - 1.0) * (q3 - 0.5 * q0 * (vr * vr + vc * vc))
    return inverse, vr, vc, p


def own_kernel(high, riding, out):
    me = lax.axis_index("space")
    out[...] = jnp.full(out.shape, (me - me % 2 if riding else me) * high, jnp.int32)


def split(value, size):
    return value >> (size.bit_length() - 1), value & (size - 1)


def forces_kernel(node_block, own, state, cell, node, area, *outs):
    radial, around = state.shape[2:]
    faces = cell.shape[0] * LANES
    chunks = faces // LANES
    _, _, _, p = pressure_of(state[0, 0], state[0, 1], state[0, 2], state[0, 3])
    sublane = lax.broadcasted_iota(jnp.int32, (8, LANES), 0)
    picked = []
    for c in range(chunks):
        tile, lane = split(jnp.broadcast_to(cell[c : c + 1, :], (8, LANES)), LANES)
        total = jnp.zeros((8, LANES), jnp.float32)
        for r in range(radial // 8):
            for h in range(around // LANES):
                part = p[r * 8 : (r + 1) * 8, h * LANES : (h + 1) * LANES]
                value = jnp.take_along_axis(part, lane, axis=1, mode="promise_in_bounds")
                place = (sublane + r * 8) * (around // LANES) + h
                total += jnp.where(tile == place, value, 0.0)
        for turn in (4, 2, 1):
            total += pltpu.roll(total, turn, 0)
        picked.append(total)
    face_pressure = jnp.concatenate(picked, axis=1)
    nodes = jnp.concatenate([node[c : c + 1, :] for c in range(chunks)], axis=1)

    high = node_block // LANES
    place, low = split(nodes, LANES)
    place = place ^ jnp.broadcast_to(own[0:1, 0:1], nodes.shape)
    pick_low = (
        lax.broadcasted_iota(jnp.int32, (LANES, faces), 0) == jnp.broadcast_to(low, (LANES, faces))
    ).astype(jnp.float32).astype(jnp.bfloat16)

    row = lax.broadcasted_iota(jnp.int32, (8, faces), 0)
    x, y, z = (face_pressure * jnp.broadcast_to(area[k : k + 1, :], (8, faces)) for k in range(3))
    groups = []
    for pattern in (jnp.where(row < high, x, y), jnp.where(row < high, z, 0.0)):
        first = pattern.astype(jnp.bfloat16).astype(jnp.float32)
        groups.append((first, pattern - first))
    away = jnp.broadcast_to(place, (8, faces)) - (row & (high - 1))

    def dense(start, count):
        masks = [away == (start + b) * high for b in range(count)]
        left = [jnp.where(m, g[i], 0.0) for i in range(2) for m in masks for g in groups]
        product = lax.dot_general(
            jnp.concatenate(left, axis=0).astype(jnp.bfloat16),
            pick_low,
            (((1,), (1,)), ((), ())),
            preferred_element_type=jnp.float32,
        )
        rows = count * ROWS
        return (product[:rows] + product[rows:]).reshape(count, ROWS, LANES)

    size = outs[0].shape[0]
    core = lax.axis_index("space") % 2
    if len(outs) == 4:
        mine, east, north, diagonal = dense(0, 4 * size).reshape(4, size, ROWS, LANES)
        others = (jnp.where(core == 0, north, east), jnp.where(core == 0, east, north))
        for out, part in zip(outs, (mine, diagonal, *others)):
            out[...] = part
    else:
        for i, out in enumerate(outs):

            @pl.loop(0, size // 8)
            def _(g):
                out[pl.ds(g * 8, 8)] = dense(i * size + g * 8, 8)

    lane = lax.broadcasted_iota(jnp.int32, (8, LANES), 1)
    columns = jnp.zeros((8, LANES), jnp.float32)
    for i, column in enumerate((around - 1, 0)):
        tile, index = divmod(column, LANES)
        index = jnp.full((8, LANES), index, jnp.int32)
        for c in range(4):
            for r in range(radial // 8):
                part = state[0, c, r * 8 : (r + 1) * 8, tile * LANES : (tile + 1) * LANES]
                value = jnp.take_along_axis(part, index, axis=1, mode="promise_in_bounds")
                place = (i * 4 + c) * radial + r * 8
                columns = jnp.where(lane == sublane + place, value, columns)
    edge = jnp.sum(columns, axis=0, keepdims=True)
    row = lax.broadcasted_iota(jnp.int32, (2, LANES), 0)
    pair = jnp.where(row == core, edge, 0.0) if len(outs) == 4 else jnp.where(row == 0, edge, 0.0)
    for out in outs:
        out[0, EDGE : EDGE + 2, :] = pair


def chip_kernel(kept, came, _, out):
    out[...] = kept[...] + came[...]


def plane_kernel(mine, diagonal, served, kept, sent):
    core = lax.axis_index("space") % 2
    first, second = (mine[b] + diagonal[b] + served[b] for b in range(2))
    kept[0] = jnp.where(core == 0, first, second)
    sent[0] = jnp.where(core == 0, second, first)
    rows = [
        jnp.where(core == 0, ref[0, EDGE : EDGE + 1, :], ref[0, EDGE + 1 : EDGE + 2, :])
        for ref in (mine, diagonal)
    ] + [served[0, EDGE : EDGE + 1, :], served[0, EDGE + 1 : EDGE + 2, :]]
    for out in (kept, sent):
        for i, edge in enumerate(rows):
            out[0, EDGE + i : EDGE + i + 1, :] = edge


def halving_kernel(kept, came, *outs):
    size = outs[0].shape[0]
    for i, out in enumerate(outs):
        for b in range(size):
            out[b] = kept[i * size + b] + came[i * size + b]


def weight_from(weights, instances, source, target):
    shift = (target - source + instances) % instances
    value = weights[0]
    for i in range(1, instances):
        value = jnp.where(shift == i, weights[i], value)
    return value


def of_chip(orders):
    half = lax.axis_index("space") // 4
    return [jnp.where(half % 2 == 0, a, b) for a, b in zip(*orders)]


def pair_kernel(weights, instances, orders, state, partner, *outs):
    me = lax.axis_index("inst")
    first, *seconds = of_chip(orders)
    for second, out in zip(seconds, outs):
        own = weight_from(weights, instances, me, me ^ second)
        other = weight_from(weights, instances, me ^ first, me ^ second)
        out[...] = own * state[...] + other * partner[...]


def around_flux(q, vc, p):
    return (q[2], q[1] * vc, q[2] * vc + p, (q[3] + p) * vc)


def flux_kernel(weight, instances, state, base, step):
    radial, around = state.shape[2:]
    q = [state[0, c] for c in range(4)]
    inverse, vr, vc, p = pressure_of(*q)
    a = jnp.sqrt(gamma_ratio * p * inverse)
    step[...] = cfl_number / (
        jnp.abs(vr) + jnp.abs(vc) + 2.0 * a + omega_rate * instances / 2.0
    )

    def after(x):
        return pltpu.roll(x, around - 1, 1)

    def above(x):
        return pltpu.roll(x, radial - 1, 0)

    column = lax.broadcasted_iota(jnp.int32, (radial, around), 1)
    row = lax.broadcasted_iota(jnp.int32, (radial, around), 0)
    hub, tip = row == 0, row == radial - 1
    speed = jnp.abs(vc) + a
    reach = 0.5 * jnp.maximum(speed, after(speed))
    speed = jnp.abs(vr) + a
    rise = 0.5 * jnp.maximum(speed, above(speed))
    flux = around_flux(q, vc, p)
    radial_flux = (q[1], q[1] * vr + p, q[2] * vr, (q[3] + p) * vr)
    for c in range(4):
        face = 0.5 * (flux[c] + after(flux[c])) - reach * (after(q[c]) - q[c])
        face = jnp.where(column == around - 1, 0.0, face)
        residual = weight * q[c] + (face - pltpu.roll(face, 1, 1))
        wall = p if c == 1 else 0.0
        face = 0.5 * (radial_flux[c] + above(radial_flux[c])) - rise * (above(q[c]) - q[c])
        upper = jnp.where(tip, wall, face)
        lower = jnp.where(hub, wall, pltpu.roll(face, 1, 0))
        base[0, c] = residual + (upper - lower)


def outer_kernel(weights, instances, orders, blocks, state, base, kept, came, partner, *refs):
    *edges, residual, total = refs
    radial, around = state.shape[2:]
    if blocks == RIDING:
        me = lax.axis_index("space")
        core = me % 2
        known = [kept[0, EDGE:, :], came[0, EDGE:, :]]
        known = [
            jnp.where(core == 0, known[0], known[1]),
            jnp.where(core == 0, known[1], known[0]),
        ]
        known = jnp.concatenate(known, axis=0)
        row = lax.broadcasted_iota(jnp.int32, known.shape, 0)

        def edge_of(device):
            chip, of_core = (device ^ (me - core)) // 2, device % 2
            place = jnp.where(chip == 1, 2 + of_core, 6 + of_core)
            place = jnp.where(chip == 0, 4 * of_core, place)
            place = jnp.where(chip == 3, 1 + 4 * of_core, place)
            return jnp.sum(jnp.where(row == place, known, 0.0), axis=0, keepdims=True)

        before = edge_of((me + blocks - 1) % blocks)
        after = edge_of((me + 1) % blocks)
    else:
        before, after = (ref[0:1, :] for ref in edges)
    me = lax.axis_index("inst")
    weight = weight_from(weights, instances, me ^ of_chip(orders)[0], me)
    lane = lax.broadcasted_iota(jnp.int32, (1, LANES), 1)
    edge = jnp.where(lane < LANES // 2, before, after)
    edge = jnp.broadcast_to(edge, (8, LANES))

    sublane = lax.broadcasted_iota(jnp.int32, (8, LANES), 0)
    lane = lax.broadcasted_iota(jnp.int32, (radial, LANES), 1)
    left, right = lane == 0, lane == LANES - 1
    own, far = [], []
    for c in range(4):
        own.append(jnp.where(left, state[0, c, :, :LANES], state[0, c, :, around - LANES :]))
        halo = []
        for r in range(radial // 8):
            index = sublane + jnp.where(lane[:8] == LANES - 1, 4 * radial, 0) + c * radial + r * 8
            halo.append(jnp.take_along_axis(edge, index, axis=1, mode="promise_in_bounds"))
        far.append(jnp.concatenate(halo, axis=0))
    faces, speeds = [], []
    for q in (own, far):
        inverse, _, vc, p = pressure_of(*q)
        speeds.append(jnp.abs(vc) + jnp.sqrt(gamma_ratio * p * inverse))
        faces.append(around_flux(q, vc, p))
    side = jnp.where(right, 0.5, -0.5)
    reach = 0.5 * jnp.maximum(*speeds)
    for c in range(4):
        outer = side * (faces[0][c] + faces[1][c]) - reach * (far[c] - own[c])
        outer = [jnp.where(left, outer, 0.0), jnp.where(right, outer, 0.0)]
        middle = around - 2 * LANES
        if middle:
            outer.insert(1, jnp.zeros((radial, middle), jnp.float32))
        residual[0, c] = base[0, c] + weight * partner[0, c] + jnp.concatenate(outer, axis=1)

    total[...] = kept[0] + came[0]


def update_kernel(residual, step, total, *refs):
    *sums, increment, blade = refs
    high = blade.shape[2] // LANES
    for k in range(3):
        for h in range(high):
            blade[k, :, pl.ds(h * LANES, LANES)] = total[k * high + h : k * high + h + 1, :]
    for c in range(residual.shape[1]):
        change = functools.reduce(jnp.add, [ref[0, c] for ref in (residual, *sums)])
        increment[0, c] = -step[...] * change


def per_device(node_block, state, face_cell, face_node, face_area):
    blocks = lax.axis_size("space")
    instances = lax.axis_size("inst")
    radial, around = state.shape[2:]
    chunks = face_cell.shape[0] // LANES
    vmem = pl.BlockSpec(memory_space=pltpu.VMEM)
    params = pltpu.CompilerParams(vmem_limit_bytes=(4 if blocks <= 16 else 16) * 2**20)

    def swapped(value, axis, bit):
        return lax.ppermute(value, axis, [(i, i ^ bit) for i in range(lax.axis_size(axis))])

    def shifted(value, axis, s):
        count = lax.axis_size(axis)
        return lax.ppermute(value, axis, [(i, (i + s) % count) for i in range(count)])

    def served(value):
        pairs = [(i, i ^ (4 if i % 2 else 2)) for i in range(blocks)]
        return lax.ppermute(value, "space", pairs)

    def call(kernel, name, shapes, *operands, flops=0, dtype=jnp.float32):
        return pl.pallas_call(
            kernel,
            out_shape=[jax.ShapeDtypeStruct(shape, dtype) for shape in shapes],
            in_specs=[vmem] * len(operands),
            out_specs=[vmem] * len(shapes),
            compiler_params=params,
            cost_estimate=pl.CostEstimate(flops=flops, bytes_accessed=0, transcendentals=0),
            name=name,
        )(*operands)

    weights = spectral_row(instances)
    def partnered(value, place):
        pairs = [
            (i * instances + n, i * instances + (n ^ orders[i // 4 % 2][place]))
            for i in range(blocks)
            for n in range(instances)
        ]
        return lax.ppermute(value, ("space", "inst"), pairs)

    orders = ORDERS if instances == 4 else ((1, *range(2, instances, 2)),) * 2
    partner = partnered(state, 0)

    riding = blocks == RIDING
    parts = 4 if riding else 2
    (own,) = call(
        functools.partial(own_kernel, node_block // LANES, riding),
        "own",
        [(8, LANES)],
        dtype=jnp.int32,
        flops=PLACING,
    )
    dense = call(
        functools.partial(forces_kernel, node_block),
        "face_forces",
        [(blocks // parts, ROWS, LANES)] * parts,
        own,
        state,
        face_cell.reshape(chunks, LANES),
        face_node.reshape(chunks, LANES),
        face_area,
        flops=PLACING,
    )

    base, step = call(
        functools.partial(flux_kernel, weights[0], instances),
        "flux",
        [state.shape, (radial, around)],
        state,
        flops=PLACING,
    )
    edges = []
    if riding:
        mine, across, other, kept = dense
        other = swapped(other, "space", 1)
        across = swapped(across, "space", 6)
        (kept,) = call(chip_kernel, "chip_sums", [kept.shape], kept, other, step, flops=PLACING)
        kept, sent = call(
            plane_kernel,
            "plane_sums",
            [(1, ROWS, LANES)] * 2,
            mine,
            across,
            served(kept),
            flops=PLACING,
        )
        came = swapped(sent, "space", 1)
    else:
        row = jnp.broadcast_to(dense[0][0, EDGE : EDGE + 1, :], (8, LANES))
        edges = [shifted(row, "space", 1), shifted(row, "space", blocks - 1)]
        size = blocks // 2
        kept, came = dense[0], swapped(dense[1], "space", size)
        while size > 1:
            size //= 2
            shapes = [(size, ROWS, LANES)] * 2
            kept, sent = call(halving_kernel, "halving", shapes, kept, came)
            came = swapped(sent, "space", size)

    sums = call(
        functools.partial(pair_kernel, weights, instances, orders),
        "pair_sums",
        [state.shape] * (len(orders[0]) - 1),
        state,
        partner,
        flops=PLACING,
    )
    sums = [partnered(value, i) for i, value in enumerate(sums, 1)]

    residual, total = call(
        functools.partial(outer_kernel, weights, instances, orders, blocks),
        "outer",
        [state.shape, (ROWS, LANES)],
        state,
        base,
        kept,
        came,
        partner,
        *edges,
    )
    increment, blade = call(
        update_kernel,
        "update",
        [state.shape, (3, 1, node_block)],
        residual,
        step,
        total,
        *sums,
    )
    return increment, jnp.transpose(blade, (1, 0, 2))


def solution(mesh):
    in_specs = (P("inst", None, None, "space"), P("space"), P("space"), P(None, "space"))
    out_specs = (P("inst", None, None, "space"), P("inst", None, "space"))
    return jax.shard_map(
        functools.partial(per_device, 512),
        mesh=mesh,
        in_specs=in_specs,
        out_specs=out_specs,
        check_vma=False,
    )
```

```python
import functools
import math

import jax
import jax.numpy as jnp
import numpy as np
from jax import lax
from jax.experimental import pallas as pl
from jax.experimental.pallas import tpu as pltpu
from jax.sharding import PartitionSpec as P

gamma_ratio = 1.4
omega_rate = 0.5
cfl_number = 0.8

LANES = 128
ROWS = 16
EDGE = 12
PLACING = 10**10
ORDERS = ((2, 1), (1, 2))
RIDING = 8


def spectral_row(count):
    row = np.zeros((count,), np.float32)
    for shift in range(count):
        row[shift] = (-1.0) ** shift / count
        if shift != 0:
            row[shift] += 0.5 * (-1.0) ** shift / math.tan(math.pi * shift / count)
    return [float(omega_rate * value) for value in row]


def pressure_of(q0, q1, q2, q3):
    inverse = 1.0 / q0
    vr = q1 * inverse
    vc = q2 * inverse
    p = (gamma_ratio - 1.0) * (q3 - 0.5 * q0 * (vr * vr + vc * vc))
    return inverse, vr, vc, p


def own_kernel(high, riding, out):
    me = lax.axis_index("space")
    out[...] = jnp.full(out.shape, (me - me % 2 if riding else me) * high, jnp.int32)


def split(value, size):
    return value >> (size.bit_length() - 1), value & (size - 1)


def forces_kernel(node_block, own, state, cell, node, area, *outs):
    radial, around = state.shape[2:]
    faces = cell.shape[0] * LANES
    chunks = faces // LANES
    _, _, _, p = pressure_of(state[0, 0], state[0, 1], state[0, 2], state[0, 3])
    sublane = lax.broadcasted_iota(jnp.int32, (8, LANES), 0)
    picked = []
    for c in range(chunks):
        tile, lane = split(jnp.broadcast_to(cell[c : c + 1, :], (8, LANES)), LANES)
        total = jnp.zeros((8, LANES), jnp.float32)
        for r in range(radial // 8):
            for h in range(around // LANES):
                part = p[r * 8 : (r + 1) * 8, h * LANES : (h + 1) * LANES]
                value = jnp.take_along_axis(part, lane, axis=1, mode="promise_in_bounds")
                place = (sublane + r * 8) * (around // LANES) + h
                total += jnp.where(tile == place, value, 0.0)
        for turn in (4, 2, 1):
            total += pltpu.roll(total, turn, 0)
        picked.append(total)
    face_pressure = jnp.concatenate(picked, axis=1)
    nodes = jnp.concatenate([node[c : c + 1, :] for c in range(chunks)], axis=1)

    high = node_block // LANES
    place, low = split(nodes, LANES)
    place = place ^ jnp.broadcast_to(own[0:1, 0:1], nodes.shape)
    pick_low = (
        lax.broadcasted_iota(jnp.int32, (LANES, faces), 0) == jnp.broadcast_to(low, (LANES, faces))
    ).astype(jnp.float32).astype(jnp.bfloat16)

    row = lax.broadcasted_iota(jnp.int32, (8, faces), 0)
    x, y, z = (face_pressure * jnp.broadcast_to(area[k : k + 1, :], (8, faces)) for k in range(3))
    groups = []
    for pattern in (jnp.where(row < high, x, y), jnp.where(row < high, z, 0.0)):
        first = pattern.astype(jnp.bfloat16).astype(jnp.float32)
        groups.append((first, pattern - first))
    away = jnp.broadcast_to(place, (8, faces)) - (row & (high - 1))

    def dense(start, count):
        masks = [away == (start + b) * high for b in range(count)]
        left = [jnp.where(m, g[i], 0.0) for i in range(2) for m in masks for g in groups]
        product = lax.dot_general(
            jnp.concatenate(left, axis=0).astype(jnp.bfloat16),
            pick_low,
            (((1,), (1,)), ((), ())),
            preferred_element_type=jnp.float32,
        )
        rows = count * ROWS
        return (product[:rows] + product[rows:]).reshape(count, ROWS, LANES)

    size = outs[0].shape[0]
    core = lax.axis_index("space") % 2
    if len(outs) == 4:
        mine, east, north, diagonal = dense(0, 4 * size).reshape(4, size, ROWS, LANES)
        others = (jnp.where(core == 0, north, east), jnp.where(core == 0, east, north))
        for out, part in zip(outs, (mine, diagonal, *others)):
            out[...] = part
    else:
        for i, out in enumerate(outs):

            @pl.loop(0, size // 8)
            def _(g):
                out[pl.ds(g * 8, 8)] = dense(i * size + g * 8, 8)

    lane = lax.broadcasted_iota(jnp.int32, (8, LANES), 1)
    columns = jnp.zeros((8, LANES), jnp.float32)
    for i, column in enumerate((around - 1, 0)):
        tile, index = divmod(column, LANES)
        index = jnp.full((8, LANES), index, jnp.int32)
        for c in range(4):
            for r in range(radial // 8):
                part = state[0, c, r * 8 : (r + 1) * 8, tile * LANES : (tile + 1) * LANES]
                value = jnp.take_along_axis(part, index, axis=1, mode="promise_in_bounds")
                place = (i * 4 + c) * radial + r * 8
                columns = jnp.where(lane == sublane + place, value, columns)
    edge = jnp.sum(columns, axis=0, keepdims=True)
    row = lax.broadcasted_iota(jnp.int32, (2, LANES), 0)
    pair = jnp.where(row == core, edge, 0.0) if len(outs) == 4 else jnp.where(row == 0, edge, 0.0)
    for out in outs:
        out[0, EDGE : EDGE + 2, :] = pair


def chip_kernel(kept, came, _, out):
    out[...] = kept[...] + came[...]


def plane_kernel(mine, diagonal, served, kept, sent):
    core = lax.axis_index("space") % 2
    first, second = (mine[b] + diagonal[b] + served[b] for b in range(2))
    kept[0] = jnp.where(core == 0, first, second)
    sent[0] = jnp.where(core == 0, second, first)
    rows = [
        jnp.where(core == 0, ref[0, EDGE : EDGE + 1, :], ref[0, EDGE + 1 : EDGE + 2, :])
        for ref in (mine, diagonal)
    ] + [served[0, EDGE : EDGE + 1, :], served[0, EDGE + 1 : EDGE + 2, :]]
    for out in (kept, sent):
        for i, edge in enumerate(rows):
            out[0, EDGE + i : EDGE + i + 1, :] = edge


def halving_kernel(kept, came, *outs):
    size = outs[0].shape[0]
    for i, out in enumerate(outs):
        for b in range(size):
            out[b] = kept[i * size + b] + came[i * size + b]


def weight_from(weights, instances, source, target):
    shift = (target - source + instances) % instances
    value = weights[0]
    for i in range(1, instances):
        value = jnp.where(shift == i, weights[i], value)
    return value


def of_chip(orders):
    chip = lax.axis_index("space") // 2
    return [jnp.where(chip == 0, a, b) for a, b in zip(*orders)]


def pair_kernel(weights, instances, orders, state, partner, *outs):
    me = lax.axis_index("inst")
    first, *seconds = of_chip(orders)
    for second, out in zip(seconds, outs):
        own = weight_from(weights, instances, me, me ^ second)
        other = weight_from(weights, instances, me ^ first, me ^ second)
        out[...] = own * state[...] + other * partner[...]


def around_flux(q, vc, p):
    return (q[2], q[1] * vc, q[2] * vc + p, (q[3] + p) * vc)


def flux_kernel(weight, instances, state, base, step):
    radial, around = state.shape[2:]
    q = [state[0, c] for c in range(4)]
    inverse, vr, vc, p = pressure_of(*q)
    a = jnp.sqrt(gamma_ratio * p * inverse)
    step[...] = cfl_number / (
        jnp.abs(vr) + jnp.abs(vc) + 2.0 * a + omega_rate * instances / 2.0
    )

    def after(x):
        return pltpu.roll(x, around - 1, 1)

    def above(x):
        return pltpu.roll(x, radial - 1, 0)

    column = lax.broadcasted_iota(jnp.int32, (radial, around), 1)
    row = lax.broadcasted_iota(jnp.int32, (radial, around), 0)
    hub, tip = row == 0, row == radial - 1
    speed = jnp.abs(vc) + a
    reach = 0.5 * jnp.maximum(speed, after(speed))
    speed = jnp.abs(vr) + a
    rise = 0.5 * jnp.maximum(speed, above(speed))
    flux = around_flux(q, vc, p)
    radial_flux = (q[1], q[1] * vr + p, q[2] * vr, (q[3] + p) * vr)
    for c in range(4):
        face = 0.5 * (flux[c] + after(flux[c])) - reach * (after(q[c]) - q[c])
        face = jnp.where(column == around - 1, 0.0, face)
        residual = weight * q[c] + (face - pltpu.roll(face, 1, 1))
        wall = p if c == 1 else 0.0
        face = 0.5 * (radial_flux[c] + above(radial_flux[c])) - rise * (above(q[c]) - q[c])
        upper = jnp.where(tip, wall, face)
        lower = jnp.where(hub, wall, pltpu.roll(face, 1, 0))
        base[0, c] = residual + (upper - lower)


def outer_kernel(weights, instances, orders, blocks, state, base, kept, came, partner, *refs):
    *edges, residual, total = refs
    radial, around = state.shape[2:]
    if blocks == RIDING:
        me = lax.axis_index("space")
        core = me % 2
        known = [kept[0, EDGE:, :], came[0, EDGE:, :]]
        known = [
            jnp.where(core == 0, known[0], known[1]),
            jnp.where(core == 0, known[1], known[0]),
        ]
        known = jnp.concatenate(known, axis=0)
        row = lax.broadcasted_iota(jnp.int32, known.shape, 0)

        def edge_of(device):
            chip, of_core = (device ^ (me - core)) // 2, device % 2
            place = jnp.where(chip == 1, 2 + of_core, 6 + of_core)
            place = jnp.where(chip == 0, 4 * of_core, place)
            place = jnp.where(chip == 3, 1 + 4 * of_core, place)
            return jnp.sum(jnp.where(row == place, known, 0.0), axis=0, keepdims=True)

        before = edge_of((me + blocks - 1) % blocks)
        after = edge_of((me + 1) % blocks)
    else:
        before, after = (ref[0:1, :] for ref in edges)
    me = lax.axis_index("inst")
    weight = weight_from(weights, instances, me ^ of_chip(orders)[0], me)
    lane = lax.broadcasted_iota(jnp.int32, (1, LANES), 1)
    edge = jnp.where(lane < LANES // 2, before, after)
    edge = jnp.broadcast_to(edge, (8, LANES))

    sublane = lax.broadcasted_iota(jnp.int32, (8, LANES), 0)
    lane = lax.broadcasted_iota(jnp.int32, (radial, LANES), 1)
    left, right = lane == 0, lane == LANES - 1
    own, far = [], []
    for c in range(4):
        own.append(jnp.where(left, state[0, c, :, :LANES], state[0, c, :, around - LANES :]))
        halo = []
        for r in range(radial // 8):
            index = sublane + jnp.where(lane[:8] == LANES - 1, 4 * radial, 0) + c * radial + r * 8
            halo.append(jnp.take_along_axis(edge, index, axis=1, mode="promise_in_bounds"))
        far.append(jnp.concatenate(halo, axis=0))
    faces, speeds = [], []
    for q in (own, far):
        inverse, _, vc, p = pressure_of(*q)
        speeds.append(jnp.abs(vc) + jnp.sqrt(gamma_ratio * p * inverse))
        faces.append(around_flux(q, vc, p))
    side = jnp.where(right, 0.5, -0.5)
    reach = 0.5 * jnp.maximum(*speeds)
    for c in range(4):
        outer = side * (faces[0][c] + faces[1][c]) - reach * (far[c] - own[c])
        outer = [jnp.where(left, outer, 0.0), jnp.where(right, outer, 0.0)]
        middle = around - 2 * LANES
        if middle:
            outer.insert(1, jnp.zeros((radial, middle), jnp.float32))
        residual[0, c] = base[0, c] + weight * partner[0, c] + jnp.concatenate(outer, axis=1)

    total[...] = kept[0] + came[0]


def update_kernel(residual, step, total, *refs):
    *sums, increment, blade = refs
    high = blade.shape[2] // LANES
    for k in range(3):
        for h in range(high):
            blade[k, :, pl.ds(h * LANES, LANES)] = total[k * high + h : k * high + h + 1, :]
    for c in range(residual.shape[1]):
        change = functools.reduce(jnp.add, [ref[0, c] for ref in (residual, *sums)])
        increment[0, c] = -step[...] * change


def per_device(node_block, state, face_cell, face_node, face_area):
    blocks = lax.axis_size("space")
    instances = lax.axis_size("inst")
    radial, around = state.shape[2:]
    chunks = face_cell.shape[0] // LANES
    vmem = pl.BlockSpec(memory_space=pltpu.VMEM)
    params = pltpu.CompilerParams(vmem_limit_bytes=(4 if blocks <= 16 else 16) * 2**20)

    def swapped(value, axis, bit):
        return lax.ppermute(value, axis, [(i, i ^ bit) for i in range(lax.axis_size(axis))])

    def shifted(value, axis, s):
        count = lax.axis_size(axis)
        return lax.ppermute(value, axis, [(i, (i + s) % count) for i in range(count)])

    def served(value):
        pairs = [(i, i ^ (4 if i % 2 else 2)) for i in range(blocks)]
        return lax.ppermute(value, "space", pairs)

    def call(kernel, name, shapes, *operands, flops=0, dtype=jnp.float32):
        return pl.pallas_call(
            kernel,
            out_shape=[jax.ShapeDtypeStruct(shape, dtype) for shape in shapes],
            in_specs=[vmem] * len(operands),
            out_specs=[vmem] * len(shapes),
            compiler_params=params,
            cost_estimate=pl.CostEstimate(flops=flops, bytes_accessed=0, transcendentals=0),
            name=name,
        )(*operands)

    weights = spectral_row(instances)
    def partnered(value, place):
        pairs = [
            (i * instances + n, i * instances + (n ^ orders[min(i // 2, 1)][place]))
            for i in range(blocks)
            for n in range(instances)
        ]
        return lax.ppermute(value, ("space", "inst"), pairs)

    orders = ORDERS if instances == 4 else ((1, *range(2, instances, 2)),) * 2
    partner = partnered(state, 0)

    riding = blocks == RIDING
    parts = 4 if riding else 2
    (own,) = call(
        functools.partial(own_kernel, node_block // LANES, riding),
        "own",
        [(8, LANES)],
        dtype=jnp.int32,
        flops=PLACING,
    )
    dense = call(
        functools.partial(forces_kernel, node_block),
        "face_forces",
        [(blocks // parts, ROWS, LANES)] * parts,
        own,
        state,
        face_cell.reshape(chunks, LANES),
        face_node.reshape(chunks, LANES),
        face_area,
        flops=PLACING,
    )

    base, step = call(
        functools.partial(flux_kernel, weights[0], instances),
        "flux",
        [state.shape, (radial, around)],
        state,
        flops=PLACING,
    )
    edges = []
    if riding:
        mine, across, other, kept = dense
        other = swapped(other, "space", 1)
        across = swapped(across, "space", 6)
        (kept,) = call(chip_kernel, "chip_sums", [kept.shape], kept, other, step, flops=PLACING)
        kept, sent = call(
            plane_kernel,
            "plane_sums",
            [(1, ROWS, LANES)] * 2,
            mine,
            across,
            served(kept),
            flops=PLACING,
        )
        came = swapped(sent, "space", 1)
    else:
        row = jnp.broadcast_to(dense[0][0, EDGE : EDGE + 1, :], (8, LANES))
        edges = [shifted(row, "space", 1), shifted(row, "space", blocks - 1)]
        size = blocks // 2
        kept, came = dense[0], swapped(dense[1], "space", size)
        while size > 1:
            size //= 2
            shapes = [(size, ROWS, LANES)] * 2
            kept, sent = call(halving_kernel, "halving", shapes, kept, came)
            came = swapped(sent, "space", size)

    sums = call(
        functools.partial(pair_kernel, weights, instances, orders),
        "pair_sums",
        [state.shape] * (len(orders[0]) - 1),
        state,
        partner,
        flops=PLACING,
    )
    sums = [partnered(value, i) for i, value in enumerate(sums, 1)]

    residual, total = call(
        functools.partial(outer_kernel, weights, instances, orders, blocks),
        "outer",
        [state.shape, (ROWS, LANES)],
        state,
        base,
        kept,
        came,
        partner,
        *edges,
    )
    increment, blade = call(
        update_kernel,
        "update",
        [state.shape, (3, 1, node_block)],
        residual,
        step,
        total,
        *sums,
    )
    return increment, jnp.transpose(blade, (1, 0, 2))


def solution(mesh):
    in_specs = (P("inst", None, None, "space"), P("space"), P("space"), P(None, "space"))
    out_specs = (P("inst", None, None, "space"), P("inst", None, "space"))
    return jax.shard_map(
        functools.partial(per_device, 512),
        mesh=mesh,
        in_specs=in_specs,
        out_specs=out_specs,
        check_vma=False,
    )
```
